32 devices in a mesh: elem: 8 (over z, y), lev: 4 (over x, core).
Axes of the slice: x: 2, y: 2, z: 4, core: 2. Of those that a mesh axis runs over, the one named last changes fastest.
Arguments:
- tracers: bfloat16 [1024, 16, 1024], P('elem', 'lev'), may hold values from -6 to 6
- velocity: float32 [3, 16, 16, 1024], P(None, None, 'lev', 'elem'), may hold values from -6 to 6
- node_mass: float32 [16, 1024], P(None, 'elem'), may hold values from 0.5 to 2
- source: int32 [1024], P('elem'), may hold values from 0 to 1023, as said below
Outputs:
- advected: bfloat16 [1024, 16, 1024], P('elem', 'lev')
The draws below stay inside these ranges and needn't reach their ends.
Inputs may be any that keep to these rules, and one draw needn't show every extreme that they name: The source of element e lies at most 64 elements before or after e along the curve, cyclically over 1024 elements. Within each aligned run of 128 elements, only the first 32 may take a source before the run and only the last 32 one after it; in every draw some run has all of its first 32 elements taking sources 64 elements before them, and some run all of its last 32 elements taking sources 64 elements after them.
All inputs are finite; a program needn't handle non-finite values.
Results may differ from the reference program's by a relative error of at most 0.006.
Values may be sent and summed in bfloat16 or wider, within the bound.
No kernel may reach another device: no remote copies, remote signals or barrier semaphores. Data moves between devices by JAX's collectives and lax.ppermute only.
A program may use at most 64 MiB of HBM per device.

```python
import math
import jax
import jax.numpy as jnp
import numpy as np
from jax import lax

NODES = 16
Q = 64
E_DEV = 128
SPAN = 64
CAP = 32
ELEMS = 1024
LEVELS = 16


def draw_source(key, part):
    first_key, second_key, third_key = jax.random.split(jax.random.fold_in(key, 7301), 3)
    element = jnp.arange(ELEMS, dtype=jnp.int32)
    position = element % E_DEV
    backward = E_DEV - 1 - position
    lowest = jnp.where(position < CAP, -SPAN, jnp.maximum(-SPAN, -position))
    highest = jnp.where(backward < CAP, SPAN, jnp.minimum(SPAN, backward))
    raw_draw = jax.random.randint(first_key, (ELEMS,), 0, 1 << 20, dtype=jnp.int32)
    offset = lowest + raw_draw % (highest - lowest + 1)
    run_index = element // E_DEV
    chosen_before = jax.random.randint(second_key, (), 0, ELEMS // E_DEV, dtype=jnp.int32)
    chosen_after = jax.random.randint(third_key, (), 0, ELEMS // E_DEV, dtype=jnp.int32)
    offset = jnp.where((run_index == chosen_before) & (position < CAP), -SPAN, offset)
    offset = jnp.where((run_index == chosen_after) & (backward < CAP), SPAN, offset)
    return ((element + offset) % ELEMS).astype(jnp.int32)


def block_scale(stream_key, extent, cuts, low, top_value):
    level = 1.0
    for dim, parts in cuts:
        steps = jax.random.uniform(jax.random.fold_in(jax.random.fold_in(stream_key, 6), dim), (parts,), jnp.float32, low / len(cuts), top_value / len(cuts))
        level = level * jnp.repeat(jnp.exp(steps), extent[dim] // parts).reshape((-1,) + (1,) * (len(extent) - 1 - dim))
    return level


def gaussian(key, dims, width, reach, shards=(), held_as=jnp.bfloat16):
    gain = block_scale(key, dims, shards, -0.22, 0.18) if shards else 1.0
    values = jax.random.normal(key, dims, jnp.float32) * width * gain
    return jnp.minimum(jnp.maximum(values, -reach), reach).astype(held_as)


def setup_inputs(seed: int = 0) -> dict:
    keys = jax.random.split(jax.random.key(seed), 5)
    tracers = gaussian(keys[0], (ELEMS, LEVELS, NODES * Q), 1.0, 6.0, ((0, 8), (1, 4)))
    velocity = gaussian(keys[1], (3, NODES, LEVELS, ELEMS), 1.0, 6.0, ((2, 4), (3, 8)), jnp.float32)
    node_mass = jnp.clip(jnp.exp(math.log(2.0) - 1.3862944 * jax.random.uniform(keys[2], (NODES, ELEMS), jnp.float32) ** block_scale(keys[2], (NODES, ELEMS), ((1, 8),), -0.2, 0.2)), 0.5, 2.0)
    source = draw_source(jax.random.fold_in(keys[4], 71), 0)
    return {"tracers": tracers, "velocity": velocity, "node_mass": node_mass, "source": source}


gll_points = (-1.0, -0.4472135954999579, 0.4472135954999579, 1.0)
east_nodes = np.array([3, 7, 11, 15])
west_nodes = np.array([0, 4, 8, 12])
courant = 0.15


def lagrange(position):
    columns = []
    for column in range(4):
        factor = jnp.ones_like(position)
        for other in range(4):
            if other != column:
                factor = factor * (position - gll_points[other]) / (gll_points[column] - gll_points[other])
        columns.append(factor)
    return jnp.stack(columns, axis=-1)


def weights(horizontal):
    along_nodes = jnp.array([gll_points[node % 4] for node in range(16)], jnp.float32)
    across_nodes = jnp.array([gll_points[node // 4] for node in range(16)], jnp.float32)
    along_basis = lagrange(along_nodes - courant * horizontal[..., 0])
    across_basis = lagrange(across_nodes - courant * horizontal[..., 1])
    table = across_basis[..., :, :, None] * along_basis[..., :, None, :]
    return table.reshape(table.shape[:-2] + (16,)).astype(jnp.bfloat16)


def share_edges(field, node_mass):
    east = field[:, east_nodes, :]
    west = field[:, west_nodes, :]
    mass_east = node_mass[:, east_nodes][:, :, None]
    mass_west = node_mass[:, west_nodes][:, :, None]
    west_after = jnp.roll(west, -1, axis=0)
    mass_after = jnp.roll(mass_west, -1, axis=0)
    shared = (mass_east * east + mass_after * west_after) / (mass_east + mass_after)
    field = field.at[:, east_nodes, :].set(shared)
    return field.at[:, west_nodes, :].set(jnp.roll(shared, 1, axis=0))


def reference(tracers, velocity, node_mass, source):
    elements, levels_all, columns_all = tracers.shape
    tracer_count = columns_all // 16
    winds_all = jnp.transpose(velocity, (3, 2, 0, 1))
    masses = jnp.transpose(node_mass)

    def one_level(level):
        here = lax.dynamic_index_in_dim(tracers, level, 1, keepdims=False).astype(jnp.float32)
        upper = lax.dynamic_index_in_dim(tracers, jnp.maximum(level - 1, 0), 1, keepdims=False).astype(jnp.float32)
        upper = jnp.where(level > 0, upper, jnp.zeros((), jnp.float32))
        winds = lax.dynamic_index_in_dim(winds_all, level, 1, keepdims=False)
        descent = jax.nn.sigmoid(winds[:, 2, :])[:, :, None]
        lifted = ((1.0 - descent) * here.reshape(elements, 16, tracer_count)
                  + descent * upper.reshape(elements, 16, tracer_count)).astype(jnp.bfloat16)
        horizontal = share_edges(jnp.swapaxes(winds[:, :2, :], 1, 2), masses)
        table = weights(horizontal)
        blocks = jnp.take(lifted, source, axis=0)
        moved = jnp.einsum("enm,emt->ent", table.astype(jnp.float32), blocks.astype(jnp.float32),
                           precision=lax.Precision.HIGHEST).astype(jnp.bfloat16)
        final = share_edges(moved.astype(jnp.float32), masses).astype(jnp.bfloat16)
        return final.reshape(elements, columns_all)

    stacked = lax.map(one_level, jnp.arange(levels_all, dtype=jnp.int32))
    return jnp.swapaxes(stacked, 0, 1)
```

```python
import functools

import jax
import jax.numpy as jnp
from jax import lax
from jax.experimental import pallas as pl
from jax.experimental.pallas import tpu as pltpu
from jax.sharding import PartitionSpec as P

gll_points = (-1.0, -0.4472135954999579, 0.4472135954999579, 1.0)
courant = 0.15
f32 = jnp.float32
bf16 = jnp.bfloat16
VMEM_LIMIT = 40 << 20
CHUNK = 16

MASS, NEAR, NEAR_MASS, SOURCE, PACKET = 32, 48, 56, 60, 64


def params():
    return pltpu.CompilerParams(vmem_limit_bytes=VMEM_LIMIT)


def ring(array, axis, by):
    peers = lax.axis_size(axis)
    return lax.ppermute(array, axis, [(i, (i + by) % peers) for i in range(peers)])


def interleave(groups, members):
    size = groups * members
    row = lax.broadcasted_iota(jnp.int32, (size, size), 0)
    column = lax.broadcasted_iota(jnp.int32, (size, size), 1)
    same = (row // groups == column % members) & (row % groups == column // members)
    return jnp.where(same, 1.0, 0.0).astype(bf16)


def basis(position):
    out = []
    for a in range(4):
        scale = 1.0
        factor = None
        for other in range(4):
            if other != a:
                scale /= gll_points[a] - gll_points[other]
                term = position - gll_points[other]
                factor = term if factor is None else factor * term
        out.append(factor * scale)
    return out


def node_rows(rows, lanes, of_i):
    row = lax.broadcasted_iota(jnp.int32, (rows, lanes), 0)
    index = row // 4 if of_i else row % 4
    out = jnp.full((rows, lanes), gll_points[0], f32)
    for a in range(1, 4):
        out = jnp.where(index == a, gll_points[a], out)
    return out


def table(winds, coefficient):
    rows, lanes = winds[0].shape
    along = basis(node_rows(rows, lanes, True) - courant * winds[0])
    across_position = node_rows(rows, lanes, False) - courant * winds[1]
    across = [factor * coefficient for factor in basis(across_position)]
    return along, across


def pack_kernel(velocity_ref, mass_ref, source_ref, head_ref, tail_ref):
    _, _, levels, elements = velocity_ref.shape
    cap = elements // levels
    runs = lax.axis_size("elem")
    start = lax.axis_index("elem") * elements
    total = runs * elements
    for out_ref, low, nodes, step in (
        (head_ref, 0, 0, 1),
        (tail_ref, elements - cap, 3, -1),
    ):
        def lanes(pieces, shift=0):
            return jnp.concatenate([x[:, low + shift : low + shift + cap] for x in pieces], axis=1)

        for c in range(2):
            pieces = [velocity_ref[c, :, k, :] for k in range(levels)]
            out_ref[16 * c : 16 * c + 16, :] = lanes(pieces)
            near = lanes(pieces, step)
            for j in range(4):
                out_ref[NEAR + 4 * c + j : NEAR + 4 * c + j + 1, :] = near[4 * j + nodes : 4 * j + nodes + 1]
        mass = mass_ref[...]
        out_ref[MASS : MASS + 16, :] = lanes([mass] * levels)
        near = lanes([mass] * levels, step)
        for j in range(4):
            out_ref[NEAR_MASS + j : NEAR_MASS + j + 1, :] = near[4 * j + nodes : 4 * j + nodes + 1]
        relative = source_ref[...] - start + (elements if step == 1 else -elements)
        relative = jnp.where(relative < 0, relative + total, relative)
        relative = jnp.where(relative < 0, relative + total, relative)
        relative = jnp.where(relative >= total, relative - total, relative)
        out_ref[SOURCE : SOURCE + 1, :] = lanes([relative.astype(f32)] * levels)
        out_ref[SOURCE + 1 :, :] = jnp.zeros((PACKET - SOURCE - 1, elements), f32)


def transpose_kernel(tracers_ref, out_ref, lowest_ref):
    elements, levels, columns = tracers_ref.shape
    order = interleave(levels, elements)
    x = tracers_ref[...].reshape(elements * levels, columns)
    step = 256
    for c in range(0, columns, step):
        y = lax.dot_general(
            x[:, c : c + step], order, (((0,), (0,)), ((), ())), preferred_element_type=f32
        ).astype(bf16)
        out_ref[c : c + step, :] = y
        lowest_ref[c : c + step, :] = y[:, (levels - 1) * elements :]


def lift_kernel(here_ref, above_ref, velocity_ref, out_ref):
    _, nodes, levels, elements = velocity_ref.shape
    tracers = here_ref.shape[0] // nodes
    for k in range(levels):
        descent = 1.0 / (1.0 + jnp.exp(-velocity_ref[0, :, k, :]))
        lanes = slice(k * elements, (k + 1) * elements)
        for m in range(nodes):
            rows = slice(m * tracers, (m + 1) * tracers)
            here = here_ref[rows, lanes].astype(f32)
            if k == 0:
                upper = above_ref[rows, :].astype(f32)
            else:
                upper = here_ref[rows, (k - 1) * elements : k * elements].astype(f32)
            d = descent[m : m + 1]
            out_ref[rows, lanes] = ((1.0 - d) * here + d * upper).astype(bf16)


def by_i(ref, first, nodes=16):
    return [ref[pl.ds(first + i, 4, stride=4), :] for i in range(4)]


def shared(mass_left, left, mass_right, right):
    return (mass_left * left + mass_right * right) / (mass_left + mass_right)


def interpolate(weights_ref, blocks_ref, node, rows, lanes):
    total = None
    for m in range(16):
        term = weights_ref[m, node : node + 1, :] * blocks_ref[m, rows, lanes]
        total = term if total is None else total + term
    return total


def remote_kernel(ahead, packet_ref, own_ref, lifted_ref, out_ref, blocks_ref, weights_ref, extra_ref):
    levels = lifted_ref.shape[1] // packet_ref.shape[1]
    lanes_all = packet_ref.shape[1]
    elements = lanes_all
    cap = elements // levels
    tracers = lifted_ref.shape[0] // 16
    total = lax.axis_size("elem") * elements
    lane = lax.broadcasted_iota(jnp.int32, (1, lanes_all), 1)
    level, place = lane // cap, lane % cap
    edge = place == (0 if ahead else cap - 1)

    def beside(values, own):
        if ahead:
            return jnp.where(edge, pltpu.roll(own, lanes_all - (cap - 1), 1), pltpu.roll(values, 1, 1))
        return jnp.where(edge, pltpu.roll(own, cap - 1, 1), pltpu.roll(values, lanes_all - 1, 1))

    mass = by_i(packet_ref, MASS)
    own_mass = by_i(own_ref, MASS)
    near_mass = packet_ref[NEAR_MASS : NEAR_MASS + 4, :]
    if ahead:
        mass_before, mass_after = beside(mass[3], own_mass[3]), near_mass
    else:
        mass_before, mass_after = near_mass, beside(mass[0], own_mass[0])
    share_west = mass[0] / (mass_before + mass[0])
    share_east = mass[3] / (mass[3] + mass_after)
    winds = []
    edge_winds = []
    for c in range(2):
        wind = by_i(packet_ref, 16 * c)
        own = by_i(own_ref, 16 * c)
        near = packet_ref[NEAR + 4 * c : NEAR + 4 * c + 4, :]
        if ahead:
            before, after = beside(wind[3], own[3]), near
        else:
            before, after = near, beside(wind[0], own[0])
        west = shared(mass_before, before, mass[0], wind[0])
        east = shared(mass[3], wind[3], mass_after, after)
        winds.append(jnp.concatenate([west, wind[1], wind[2], east], axis=0))
        edge_winds.append(west if ahead else east)
    ones = jnp.ones((8, lanes_all), f32)
    along, across = table(winds, jnp.concatenate([share_west, ones, share_east], axis=0))
    for b in range(4):
        for a in range(4):
            weights_ref[4 * b + a] = along[a] * across[b]
    edge_share = 1.0 - (share_west if ahead else share_east)
    extra_along = basis(gll_points[3 if ahead else 0] - courant * edge_winds[0])
    across_position = node_rows(4, lanes_all, False) - courant * edge_winds[1]
    extra_across = [factor * edge_share for factor in basis(across_position)]
    for b in range(4):
        for a in range(4):
            extra_ref[4 * b + a, 0:4] = extra_along[a] * extra_across[b]

    source = packet_ref[SOURCE : SOURCE + 1, :].astype(jnp.int32)
    own_source = own_ref[SOURCE : SOURCE + 1, :].astype(jnp.int32) + (elements if ahead else -elements)
    own_source = jnp.where(own_source >= total, own_source - total, own_source)
    own_source = jnp.where(own_source < 0, own_source + total, own_source)
    own_source = pltpu.roll(own_source, lanes_all - (cap - 1) if ahead else cap - 1, 1)
    row = lax.broadcasted_iota(jnp.int32, (levels * elements, lanes_all), 0)
    same = row // elements == level
    first = jnp.where(same & (row % elements == source), 1.0, 0.0).astype(bf16)
    second = jnp.where(same & edge & (row % elements == own_source), 1.0, 0.0).astype(bf16)
    chosen = jnp.concatenate([first, second], axis=1)
    step = 4
    for m in range(0, 16, step):
        y = jnp.dot(lifted_ref[m * tracers : (m + step) * tracers, :], chosen, preferred_element_type=f32)
        blocks_ref[m : m + step] = y.reshape(step, tracers, 2 * lanes_all)

    def one(index, carry):
        t = pl.multiple_of(index * CHUNK, CHUNK)
        rows = pl.ds(t, CHUNK)
        lanes = slice(0, lanes_all)
        for j in range(4):
            moved = [interpolate(weights_ref, blocks_ref, 4 * i + j, rows, lanes) for i in range(4)]
            own = interpolate(extra_ref, blocks_ref, j, rows, slice(lanes_all, 2 * lanes_all))
            if ahead:
                west = moved[0] + jnp.where(edge, own, pltpu.roll(moved[3], 1, 1))
                east = jnp.where(place == cap - 1, moved[3], pltpu.roll(west, lanes_all - 1, 1))
            else:
                east = moved[3] + jnp.where(edge, own, pltpu.roll(moved[0], lanes_all - 1, 1))
                west = jnp.where(place == 0, moved[0], pltpu.roll(east, 1, 1))
            for i, value in enumerate((west, moved[1], moved[2], east)):
                out_ref[pl.ds(t + (4 * j + i) * tracers, CHUNK), :] = value.astype(bf16)
        return carry

    lax.fori_loop(0, tracers // CHUNK, one, 0)


def local_kernel(velocity_ref, mass_ref, source_ref, lifted_ref, out_ref, blocks_ref, weights_ref, wind_ref, moved_ref):
    _, _, levels, elements = velocity_ref.shape
    columns = out_ref.shape[2]
    tracers = columns // 16
    start = lax.axis_index("elem") * elements
    lane = lax.broadcasted_iota(jnp.int32, (1, elements), 1)
    mass = by_i(mass_ref, 0)
    mass_before = pltpu.roll(mass[3], 1, 1)
    mass_after = pltpu.roll(mass[0], elements - 1, 1)
    share_west = mass[0] / (mass_before + mass[0])
    share_east = mass[3] / (mass[3] + mass_after)
    coefficient = jnp.concatenate([share_west, jnp.ones((8, elements), f32), share_east], axis=0)
    row = lax.broadcasted_iota(jnp.int32, (elements, elements), 0)
    chosen = jnp.where(row == source_ref[...] - start, 1.0, 0.0).astype(bf16)
    for k in range(levels):
        winds = []
        for c in range(2):
            wind_ref[c] = velocity_ref[c, :, k, :]
            wind = [wind_ref[c, pl.ds(i, 4, stride=4), :] for i in range(4)]
            west = shared(mass_before, pltpu.roll(wind[3], 1, 1), mass[0], wind[0])
            east = shared(mass[3], wind[3], mass_after, pltpu.roll(wind[0], elements - 1, 1))
            winds.append(jnp.concatenate([west, wind[1], wind[2], east], axis=0))
        along, across = table(winds, coefficient)
        for b in range(4):
            for a in range(4):
                weights_ref[4 * b + a] = along[a] * across[b]
        lanes = slice(k * elements, (k + 1) * elements)
        y = jnp.dot(lifted_ref[:, lanes], chosen, preferred_element_type=f32)
        blocks_ref[...] = y.reshape(16, tracers, elements)

        def one(index, carry):
            t = pl.multiple_of(index * CHUNK, CHUNK)
            rows = pl.ds(t, CHUNK)
            for j in range(4):
                moved = [
                    interpolate(weights_ref, blocks_ref, 4 * i + j, rows, slice(0, elements)) for i in range(4)
                ]
                west = jnp.where(lane == 0, 0.0, moved[0] + pltpu.roll(moved[3], 1, 1))
                east = pltpu.roll(west, elements - 1, 1)
                for i, value in enumerate((west, moved[1], moved[2], east)):
                    moved_ref[pl.ds(t + (4 * j + i) * tracers, CHUNK), lanes] = value.astype(bf16)
            return carry

        lax.fori_loop(0, tracers // CHUNK, one, 0)
    order = interleave(levels, elements)
    step = 256
    for c in range(0, columns, step):
        y = lax.dot_general(
            order, moved_ref[c : c + step, :], (((1,), (1,)), ((), ())), preferred_element_type=f32
        )
        out_ref[:, :, c : c + step] = y.reshape(elements, levels, step).astype(bf16)


def combine_kernel(part_ref, head_ref, tail_ref, ahead_ref, back_ref, out_ref, first_ref, last_ref, sems):
    elements, levels, columns = out_ref.shape
    lanes_all = head_ref.shape[1]
    cap = elements // levels
    tracers = columns // 16
    span = 4 * tracers
    spots = ((first_ref, pl.ds(0, cap + 1)), (last_ref, pl.ds(elements - cap - 1, cap + 1)))
    loads = [pltpu.make_async_copy(out_ref.at[rows], ref, sems.at[n]) for n, (ref, rows) in enumerate(spots)]
    for load in loads:
        load.start()
    place = lax.broadcasted_iota(jnp.int32, (1, lanes_all), 1) % cap
    column = lax.broadcasted_iota(jnp.int32, (1, columns), 1) % span
    order = interleave(levels, cap)
    stores = []
    for n, (ref, rows) in enumerate(spots):
        received_ref = (head_ref, tail_ref)[n]
        pieces = []
        for node in range(16):
            value = received_ref[node * tracers : (node + 1) * tracers, :]
            if n == 0 and node % 4 == 0:
                own = back_ref[(node + 3) * tracers : (node + 4) * tracers, :].astype(f32)
                own = pltpu.roll(own, lanes_all - (cap - 1), 1)
                value = (value.astype(f32) + jnp.where(place == 0, own, 0.0)).astype(bf16)
            if n == 1 and node % 4 == 3:
                own = ahead_ref[(node - 3) * tracers : (node - 2) * tracers, :].astype(f32)
                own = pltpu.roll(own, cap - 1, 1)
                value = (value.astype(f32) + jnp.where(place == cap - 1, own, 0.0)).astype(bf16)
            pieces.append(value)
        received = jnp.concatenate(pieces, axis=0)
        y = lax.dot_general(order, received, (((1,), (1,)), ((), ())), preferred_element_type=f32)
        y = y.reshape(cap, levels, columns)
        loads[n].wait()
        if n == 0:
            ref[0:cap] = (ref[0:cap].astype(f32) + y).astype(bf16)
            east = pltpu.roll(y[cap - 1], columns - 3 * tracers, 1)
            ref[cap] = (ref[cap].astype(f32) + jnp.where(column < tracers, east, 0.0)).astype(bf16)
        else:
            ref[1 : cap + 1] = (ref[1 : cap + 1].astype(f32) + y).astype(bf16)
            west = pltpu.roll(y[0], 3 * tracers, 1)
            ref[0] = (ref[0].astype(f32) + jnp.where(column >= 3 * tracers, west, 0.0)).astype(bf16)
        store = pltpu.make_async_copy(ref, out_ref.at[rows], sems.at[2 + n])
        store.start()
        stores.append(store)
    for store in stores:
        store.wait()


def on_device(tracers, velocity, node_mass, source):
    elements, levels, columns = tracers.shape
    count = columns // 16
    lanes = levels * elements
    shape = jax.ShapeDtypeStruct
    source = source.reshape(1, elements)
    packet = shape((PACKET, elements), f32)
    head, tail = pl.pallas_call(
        pack_kernel, out_shape=(packet, packet), compiler_params=params(), name="pack"
    )(velocity, node_mass, source)
    next_head = ring(head, "elem", -1)
    prev_tail = ring(tail, "elem", 1)
    here, lowest = pl.pallas_call(
        transpose_kernel,
        out_shape=(shape((columns, lanes), bf16), shape((columns, elements), bf16)),
        compiler_params=params(),
        name="transpose",
    )(tracers)
    blocks = lax.axis_size("lev")
    above = lax.ppermute(lowest, "lev", [(i, i + 1) for i in range(blocks - 1)])
    lifted = pl.pallas_call(
        lift_kernel, out_shape=shape((columns, lanes), bf16), compiler_params=params(), name="lift"
    )(here, above, velocity[2:])

    def contributions(ahead, packet, own):
        return pl.pallas_call(
            functools.partial(remote_kernel, ahead),
            out_shape=shape((columns, elements), bf16),
            scratch_shapes=[
                pltpu.VMEM((16, count, 2 * elements), f32),
                pltpu.VMEM((16, 16, elements), f32),
                pltpu.VMEM((16, 8, elements), f32),
            ],
            compiler_params=params(),
            name="remote_ahead" if ahead else "remote_back",
        )(packet, own, lifted)

    ahead = contributions(True, next_head, tail)
    back = contributions(False, prev_tail, head)
    from_prev = ring(ahead, "elem", 1)
    from_next = ring(back, "elem", -1)
    part = pl.pallas_call(
        local_kernel,
        out_shape=shape((elements, levels, columns), bf16),
        scratch_shapes=[
            pltpu.VMEM((16, count, elements), f32),
            pltpu.VMEM((16, 16, elements), f32),
            pltpu.VMEM((2, 16, elements), f32),
            pltpu.VMEM((columns, lanes), bf16),
        ],
        compiler_params=params(),
        name="local",
    )(velocity, node_mass, source, lifted)
    cap = elements // levels
    vmem = pl.BlockSpec(memory_space=pltpu.VMEM)
    anywhere = pl.BlockSpec(memory_space=pl.ANY)
    return pl.pallas_call(
        combine_kernel,
        out_shape=shape((elements, levels, columns), bf16),
        in_specs=[anywhere, vmem, vmem, vmem, vmem],
        out_specs=anywhere,
        scratch_shapes=[
            pltpu.VMEM((cap + 1, levels, columns), bf16),
            pltpu.VMEM((cap + 1, levels, columns), bf16),
            pltpu.SemaphoreType.DMA((4,)),
        ],
        input_output_aliases={0: 0},
        compiler_params=params(),
        name="combine",
    )(part, from_prev, from_next, ahead, back)


def solution(mesh):
    placed = (P("elem", "lev", None), P(None, None, "lev", "elem"), P(None, "elem"), P("elem"))
    return jax.shard_map(
        on_device, mesh=mesh, in_specs=placed, out_specs=P("elem", "lev", None), check_vma=False
    )
```

```python
import functools

import jax
import jax.numpy as jnp
from jax import lax
from jax.experimental import pallas as pl
from jax.experimental.pallas import tpu as pltpu
from jax.sharding import PartitionSpec as P

gll_points = (-1.0, -0.4472135954999579, 0.4472135954999579, 1.0)
courant = 0.15
f32 = jnp.float32
bf16 = jnp.bfloat16
VMEM_LIMIT = 40 << 20
CHUNK = 16

MASS, NEAR, NEAR_MASS, SOURCE, PACKET = 32, 48, 56, 60, 64


def params():
    return pltpu.CompilerParams(vmem_limit_bytes=VMEM_LIMIT)


def interleave(groups, members):
    size = groups * members
    row = lax.broadcasted_iota(jnp.int32, (size, size), 0)
    column = lax.broadcasted_iota(jnp.int32, (size, size), 1)
    same = (row // groups == column % members) & (row % groups == column // members)
    return jnp.where(same, 1.0, 0.0).astype(bf16)


def basis(position):
    out = []
    for a in range(4):
        scale = 1.0
        factor = None
        for other in range(4):
            if other != a:
                scale /= gll_points[a] - gll_points[other]
                term = position - gll_points[other]
                factor = term if factor is None else factor * term
        out.append(factor * scale)
    return out


def node_rows(rows, lanes, of_i):
    row = lax.broadcasted_iota(jnp.int32, (rows, lanes), 0)
    index = row // 4 if of_i else row % 4
    out = jnp.full((rows, lanes), gll_points[0], f32)
    for a in range(1, 4):
        out = jnp.where(index == a, gll_points[a], out)
    return out


def table(winds, coefficient):
    rows, lanes = winds[0].shape
    along = basis(node_rows(rows, lanes, True) - courant * winds[0])
    across_position = node_rows(rows, lanes, False) - courant * winds[1]
    across = [factor * coefficient for factor in basis(across_position)]
    return along, across


def is_even():
    return lax.axis_index("elem") % 2 == 0


def pack_kernel(velocity_ref, mass_ref, source_ref, pair_ref, cross_ref):
    even = is_even()
    pl.when(even)(lambda: pack(velocity_ref, mass_ref, source_ref, cross_ref, pair_ref))
    pl.when(jnp.logical_not(even))(lambda: pack(velocity_ref, mass_ref, source_ref, pair_ref, cross_ref))


def pack(velocity_ref, mass_ref, source_ref, head_ref, tail_ref):
    _, _, levels, elements = velocity_ref.shape
    cap = elements // levels
    runs = lax.axis_size("elem")
    start = lax.axis_index("elem") * elements
    total = runs * elements
    for out_ref, low, nodes, step in (
        (head_ref, 0, 0, 1),
        (tail_ref, elements - cap, 3, -1),
    ):
        def lanes(pieces, shift=0):
            return jnp.concatenate([x[:, low + shift : low + shift + cap] for x in pieces], axis=1)

        for c in range(2):
            pieces = [velocity_ref[c, :, k, :] for k in range(levels)]
            out_ref[16 * c : 16 * c + 16, :] = lanes(pieces)
            near = lanes(pieces, step)
            for j in range(4):
                out_ref[NEAR + 4 * c + j : NEAR + 4 * c + j + 1, :] = near[4 * j + nodes : 4 * j + nodes + 1]
        mass = mass_ref[...]
        out_ref[MASS : MASS + 16, :] = lanes([mass] * levels)
        near = lanes([mass] * levels, step)
        for j in range(4):
            out_ref[NEAR_MASS + j : NEAR_MASS + j + 1, :] = near[4 * j + nodes : 4 * j + nodes + 1]
        relative = source_ref[...] - start + (elements if step == 1 else -elements)
        relative = jnp.where(relative < 0, relative + total, relative)
        relative = jnp.where(relative < 0, relative + total, relative)
        relative = jnp.where(relative >= total, relative - total, relative)
        out_ref[SOURCE : SOURCE + 1, :] = lanes([relative.astype(f32)] * levels)
        out_ref[SOURCE + 1 :, :] = jnp.zeros((PACKET - SOURCE - 1, elements), f32)


def transpose_kernel(tracers_ref, out_ref, lowest_ref):
    elements, levels, columns = tracers_ref.shape
    order = interleave(levels, elements)
    x = tracers_ref[...].reshape(elements * levels, columns)
    step = 256
    for c in range(0, columns, step):
        y = lax.dot_general(
            x[:, c : c + step], order, (((0,), (0,)), ((), ())), preferred_element_type=f32
        ).astype(bf16)
        out_ref[c : c + step, :] = y
        lowest_ref[c : c + step, :] = y[:, (levels - 1) * elements :]


def lift_kernel(here_ref, above_ref, velocity_ref, out_ref):
    _, nodes, levels, elements = velocity_ref.shape
    tracers = here_ref.shape[0] // nodes
    for k in range(levels):
        descent = 1.0 / (1.0 + jnp.exp(-velocity_ref[0, :, k, :]))
        lanes = slice(k * elements, (k + 1) * elements)
        for m in range(nodes):
            rows = slice(m * tracers, (m + 1) * tracers)
            here = here_ref[rows, lanes].astype(f32)
            if k == 0:
                upper = above_ref[rows, :].astype(f32)
            else:
                upper = here_ref[rows, (k - 1) * elements : k * elements].astype(f32)
            d = descent[m : m + 1]
            out_ref[rows, lanes] = ((1.0 - d) * here + d * upper).astype(bf16)


def by_i(ref, first, nodes=16):
    return [ref[pl.ds(first + i, 4, stride=4), :] for i in range(4)]


def shared(mass_left, left, mass_right, right):
    return (mass_left * left + mass_right * right) / (mass_left + mass_right)


def interpolate(weights_ref, blocks_ref, node, rows, lanes):
    total = None
    for m in range(16):
        term = weights_ref[m, node : node + 1, :] * blocks_ref[m, rows, lanes]
        total = term if total is None else total + term
    return total


def remote_kernel(pair, *refs):
    even = is_even()
    ahead = even if pair else jnp.logical_not(even)
    pl.when(ahead)(lambda: remote(True, *refs))
    pl.when(jnp.logical_not(ahead))(lambda: remote(False, *refs))


def remote(ahead, packet_ref, own_ref, lifted_ref, out_ref, blocks_ref, weights_ref, extra_ref, edge_ref):
    levels = lifted_ref.shape[1] // packet_ref.shape[1]
    lanes_all = packet_ref.shape[1]
    elements = lanes_all
    cap = elements // levels
    tracers = lifted_ref.shape[0] // 16
    total = lax.axis_size("elem") * elements
    lane = lax.broadcasted_iota(jnp.int32, (1, lanes_all), 1)
    level, place = lane // cap, lane % cap
    edge = place == (0 if ahead else cap - 1)

    def beside(values, own):
        if ahead:
            return jnp.where(edge, pltpu.roll(own, lanes_all - (cap - 1), 1), pltpu.roll(values, 1, 1))
        return jnp.where(edge, pltpu.roll(own, cap - 1, 1), pltpu.roll(values, lanes_all - 1, 1))

    mass = by_i(packet_ref, MASS)
    own_mass = by_i(own_ref, MASS)
    near_mass = packet_ref[NEAR_MASS : NEAR_MASS + 4, :]
    if ahead:
        mass_before, mass_after = beside(mass[3], own_mass[3]), near_mass
    else:
        mass_before, mass_after = near_mass, beside(mass[0], own_mass[0])
    share_west = mass[0] / (mass_before + mass[0])
    share_east = mass[3] / (mass[3] + mass_after)
    winds = []
    edge_winds = []
    for c in range(2):
        wind = by_i(packet_ref, 16 * c)
        own = by_i(own_ref, 16 * c)
        near = packet_ref[NEAR + 4 * c : NEAR + 4 * c + 4, :]
        if ahead:
            before, after = beside(wind[3], own[3]), near
        else:
            before, after = near, beside(wind[0], own[0])
        west = shared(mass_before, before, mass[0], wind[0])
        east = shared(mass[3], wind[3], mass_after, after)
        winds.append(jnp.concatenate([west, wind[1], wind[2], east], axis=0))
        edge_winds.append(west if ahead else east)
    ones = jnp.ones((8, lanes_all), f32)
    along, across = table(winds, jnp.concatenate([share_west, ones, share_east], axis=0))
    for b in range(4):
        for a in range(4):
            weights_ref[4 * b + a] = along[a] * across[b]
    edge_share = 1.0 - (share_west if ahead else share_east)
    extra_along = basis(gll_points[3 if ahead else 0] - courant * edge_winds[0])
    across_position = node_rows(4, lanes_all, False) - courant * edge_winds[1]
    extra_across = [factor * edge_share for factor in basis(across_position)]
    for b in range(4):
        for a in range(4):
            extra_ref[4 * b + a, 0:4] = extra_along[a] * extra_across[b]

    source = packet_ref[SOURCE : SOURCE + 1, :].astype(jnp.int32)
    own_source = own_ref[SOURCE : SOURCE + 1, :].astype(jnp.int32) + (elements if ahead else -elements)
    own_source = jnp.where(own_source >= total, own_source - total, own_source)
    own_source = jnp.where(own_source < 0, own_source + total, own_source)
    own_source = pltpu.roll(own_source, lanes_all - (cap - 1) if ahead else cap - 1, 1)
    row = lax.broadcasted_iota(jnp.int32, (levels * elements, lanes_all), 0)
    same = row // elements == level
    first = jnp.where(same & (row % elements == source), 1.0, 0.0).astype(bf16)
    second = jnp.where(same & edge & (row % elements == own_source), 1.0, 0.0).astype(bf16)
    chosen = jnp.concatenate([first, second], axis=1)
    step = 4
    for m in range(0, 16, step):
        y = jnp.dot(lifted_ref[m * tracers : (m + step) * tracers, :], chosen, preferred_element_type=f32)
        blocks_ref[m : m + step] = y.reshape(step, tracers, 2 * lanes_all)

    def one(index, carry):
        t = pl.multiple_of(index * CHUNK, CHUNK)
        rows = pl.ds(t, CHUNK)
        lanes = slice(0, lanes_all)
        for j in range(4):
            moved = [interpolate(weights_ref, blocks_ref, 4 * i + j, rows, lanes) for i in range(4)]
            own = interpolate(extra_ref, blocks_ref, j, rows, slice(lanes_all, 2 * lanes_all))
            if ahead:
                west = moved[0] + jnp.where(edge, own, pltpu.roll(moved[3], 1, 1))
                values, far = (west, moved[1], moved[2]), moved[3]
            else:
                east = moved[3] + jnp.where(edge, own, pltpu.roll(moved[0], lanes_all - 1, 1))
                values, far = (moved[1], moved[2], east), moved[0]
            for i, value in enumerate(values):
                out_ref[pl.ds(t + (3 * j + i) * tracers, CHUNK), :] = value.astype(bf16)
            edge_ref[pl.ds(t + j * tracers, CHUNK), :] = far.astype(bf16)
        return carry

    lax.fori_loop(0, tracers // CHUNK, one, 0)
    row = lax.broadcasted_iota(jnp.int32, (8, lanes_all), 0)
    far_place = cap - 1 if ahead else 0
    pick = jnp.where(lane == row * cap + far_place, 1.0, 0.0).astype(bf16)
    far = lax.dot_general(pick, edge_ref[...], (((1,), (1,)), ((), ())), preferred_element_type=f32)
    far = [far[:, n : n + lanes_all] for n in range(0, 4 * tracers, lanes_all)]
    out_ref[12 * tracers :, :] = jnp.concatenate(far, axis=0).astype(bf16)


def local_kernel(
    velocity_ref, mass_ref, source_ref, lifted_ref,
    out_ref, ends_ref, sides_ref,
    blocks_ref, weights_ref, wind_ref, moved_ref, inner_ref, sem,
):
    _, _, levels, elements = velocity_ref.shape
    cap = elements // levels
    columns = out_ref.shape[2]
    tracers = columns // 16
    start = lax.axis_index("elem") * elements
    lane = lax.broadcasted_iota(jnp.int32, (1, elements), 1)
    mass = by_i(mass_ref, 0)
    mass_before = pltpu.roll(mass[3], 1, 1)
    mass_after = pltpu.roll(mass[0], elements - 1, 1)
    share_west = mass[0] / (mass_before + mass[0])
    share_east = mass[3] / (mass[3] + mass_after)
    coefficient = jnp.concatenate([share_west, jnp.ones((8, elements), f32), share_east], axis=0)
    row = lax.broadcasted_iota(jnp.int32, (elements, elements), 0)
    chosen = jnp.where(row == source_ref[...] - start, 1.0, 0.0).astype(bf16)
    for k in range(levels):
        winds = []
        for c in range(2):
            wind_ref[c] = velocity_ref[c, :, k, :]
            wind = [wind_ref[c, pl.ds(i, 4, stride=4), :] for i in range(4)]
            west = shared(mass_before, pltpu.roll(wind[3], 1, 1), mass[0], wind[0])
            east = shared(mass[3], wind[3], mass_after, pltpu.roll(wind[0], elements - 1, 1))
            winds.append(jnp.concatenate([west, wind[1], wind[2], east], axis=0))
        along, across = table(winds, coefficient)
        for b in range(4):
            for a in range(4):
                weights_ref[4 * b + a] = along[a] * across[b]
        lanes = slice(k * elements, (k + 1) * elements)
        y = jnp.dot(lifted_ref[:, lanes], chosen, preferred_element_type=f32)
        blocks_ref[...] = y.reshape(16, tracers, elements)

        def one(index, carry):
            t = pl.multiple_of(index * CHUNK, CHUNK)
            rows = pl.ds(t, CHUNK)
            for j in range(4):
                moved = [
                    interpolate(weights_ref, blocks_ref, 4 * i + j, rows, slice(0, elements)) for i in range(4)
                ]
                west = jnp.where(lane == 0, 0.0, moved[0] + pltpu.roll(moved[3], 1, 1))
                east = pltpu.roll(west, elements - 1, 1)
                for i, value in enumerate((west, moved[1], moved[2], east)):
                    moved_ref[pl.ds(t + (4 * j + i) * tracers, CHUNK), lanes] = value.astype(bf16)
            return carry

        lax.fori_loop(0, tracers // CHUNK, one, 0)
    inner = elements - 2 * cap
    row = lax.broadcasted_iota(jnp.int32, (inner * levels, elements * levels), 0)
    column = lax.broadcasted_iota(jnp.int32, (inner * levels, elements * levels), 1)
    same = (row // levels + cap == column % elements) & (row % levels == column // elements)
    order = jnp.where(same, 1.0, 0.0).astype(bf16)
    step = 256
    for c in range(0, columns, step):
        y = lax.dot_general(
            order, moved_ref[c : c + step, :], (((1,), (1,)), ((), ())), preferred_element_type=f32
        )
        inner_ref[:, :, c : c + step] = y.reshape(inner, levels, step).astype(bf16)
    store = pltpu.make_async_copy(
        inner_ref.at[pl.ds(1, inner - 2)], out_ref.at[pl.ds(cap + 1, inner - 2)], sem
    )
    store.start()
    sides_ref[0] = inner_ref[0]
    sides_ref[1] = inner_ref[inner - 1]
    for n, low in enumerate((0, elements - cap)):
        ends_ref[n] = jnp.concatenate(
            [moved_ref[:, k * elements + low : k * elements + low + cap] for k in range(levels)], axis=1
        )
    store.wait()


def combine_kernel(pair, part_ref, ends_ref, sides_ref, received_ref, sent_ref, out_ref, rows_ref, sem):
    del part_ref
    refs = (ends_ref, sides_ref, received_ref, sent_ref, out_ref, rows_ref, sem)
    even = is_even()
    head = jnp.logical_not(even) if pair else even
    pl.when(head)(lambda: combine(True, *refs))
    pl.when(jnp.logical_not(head))(lambda: combine(False, *refs))


def combine(head, ends_ref, sides_ref, received_ref, sent_ref, out_ref, rows_ref, sem):
    elements, levels, columns = out_ref.shape
    lanes_all = received_ref.shape[1]
    cap = elements // levels
    tracers = columns // 16
    end = 0 if head else 1
    place = lax.broadcasted_iota(jnp.int32, (1, lanes_all), 1) % cap
    order = interleave(levels, cap)

    def rows(ref, block):
        return ref[block * tracers : (block + 1) * tracers, :].astype(f32)

    pieces = []
    for j in range(4):
        got = [rows(received_ref, 3 * j + i) for i in range(3)]
        if head:
            own = pltpu.roll(rows(sent_ref, 3 * j + 2), lanes_all - (cap - 1), 1)
            west = got[0] + jnp.where(place == 0, own, 0.0)
            east = jnp.where(place == cap - 1, 0.0, pltpu.roll(got[0], lanes_all - 1, 1))
            got = [west, got[1], got[2], east]
        else:
            own = pltpu.roll(rows(sent_ref, 3 * j), cap - 1, 1)
            east = got[2] + jnp.where(place == cap - 1, own, 0.0)
            west = jnp.where(place == 0, 0.0, pltpu.roll(got[2], 1, 1))
            got = [west, got[0], got[1], east]
        for i, value in enumerate(got):
            node = 4 * j + i
            here = ends_ref[end, node * tracers : (node + 1) * tracers, :].astype(f32)
            pieces.append((here + value).astype(bf16))
    y = lax.dot_general(
        order, jnp.concatenate(pieces, axis=0), (((1,), (1,)), ((), ())), preferred_element_type=f32
    ).reshape(cap, levels, columns)
    far = received_ref[12 * tracers :, :]
    far = jnp.concatenate([far[n : n + 8] for n in range(0, far.shape[0], 8)], axis=1)
    row = lax.broadcasted_iota(jnp.int32, (4 * tracers, columns), 0)
    column = lax.broadcasted_iota(jnp.int32, (4 * tracers, columns), 1)
    spread = jnp.where(column == (row // tracers) * 4 * tracers + row % tracers, 1.0, 0.0).astype(bf16)
    west = jnp.dot(far, spread, preferred_element_type=f32)
    east = pltpu.roll(west, 3 * tracers, 1)[:levels]
    west = west[:levels]
    if head:
        rows_ref[0 : cap - 1] = y[: cap - 1].astype(bf16)
        rows_ref[cap - 1] = (y[cap - 1] + east).astype(bf16)
        rows_ref[cap] = (sides_ref[0].astype(f32) + west).astype(bf16)
        spot = pl.ds(0, cap + 1)
    else:
        rows_ref[2:] = y[1:].astype(bf16)
        rows_ref[1] = (y[0] + west).astype(bf16)
        rows_ref[0] = (sides_ref[1].astype(f32) + east).astype(bf16)
        spot = pl.ds(elements - cap - 1, cap + 1)
    store = pltpu.make_async_copy(rows_ref, out_ref.at[spot], sem)
    store.start()
    store.wait()


def on_device(tracers, velocity, node_mass, source):
    elements, levels, columns = tracers.shape
    cap = elements // 4
    assert cap * levels == elements
    count = columns // 16
    lanes = levels * elements
    runs = lax.axis_size("elem")
    pairing = [(i, i ^ 1) for i in range(runs)]
    crossing = [(i, (i - 1 if i % 2 == 0 else i + 1) % runs) for i in range(runs)]
    shape = jax.ShapeDtypeStruct
    vmem = pl.BlockSpec(memory_space=pltpu.VMEM)
    anywhere = pl.BlockSpec(memory_space=pl.ANY)
    source = source.reshape(1, elements)
    packet = shape((PACKET, elements), f32)
    pair_sent, cross_sent = pl.pallas_call(
        pack_kernel, out_shape=(packet, packet), compiler_params=params(), name="pack"
    )(velocity, node_mass, source)
    cross_packet = lax.ppermute(cross_sent, "elem", crossing)
    pair_packet = lax.ppermute(pair_sent, "elem", pairing)
    here, lowest = pl.pallas_call(
        transpose_kernel,
        out_shape=(shape((columns, lanes), bf16), shape((columns, elements), bf16)),
        compiler_params=params(),
        name="transpose",
    )(tracers)
    blocks = lax.axis_size("lev")
    above = lax.ppermute(lowest, "lev", [(i, i + 1) for i in range(blocks - 1)])
    lifted = pl.pallas_call(
        lift_kernel, out_shape=shape((columns, lanes), bf16), compiler_params=params(), name="lift"
    )(here, above, velocity[2:])

    far_rows = 8 * (4 * count // elements)

    def contributions(pair, packet, own):
        return pl.pallas_call(
            functools.partial(remote_kernel, pair),
            out_shape=shape((12 * count + far_rows, elements), bf16),
            scratch_shapes=[
                pltpu.VMEM((16, count, 2 * elements), f32),
                pltpu.VMEM((16, 16, elements), f32),
                pltpu.VMEM((16, 8, elements), f32),
                pltpu.VMEM((4 * count, elements), bf16),
            ],
            compiler_params=params(),
            name="remote_pair" if pair else "remote_cross",
        )(packet, own, lifted)

    cross_out = contributions(False, cross_packet, cross_sent)
    cross_in = lax.ppermute(cross_out, "elem", crossing)
    pair_out = contributions(True, pair_packet, pair_sent)
    pair_in = lax.ppermute(pair_out, "elem", pairing)
    result = shape((elements, levels, columns), bf16)
    part, ends, sides = pl.pallas_call(
        local_kernel,
        out_shape=(result, shape((2, columns, elements), bf16), shape((2, levels, columns), bf16)),
        out_specs=(anywhere, vmem, vmem),
        scratch_shapes=[
            pltpu.VMEM((16, count, elements), f32),
            pltpu.VMEM((16, 16, elements), f32),
            pltpu.VMEM((2, 16, elements), f32),
            pltpu.VMEM((columns, lanes), bf16),
            pltpu.VMEM((elements - 2 * cap, levels, columns), bf16),
            pltpu.SemaphoreType.DMA,
        ],
        compiler_params=params(),
        name="local",
    )(velocity, node_mass, source, lifted)
    for pair, received, sent in ((True, pair_in, pair_out), (False, cross_in, cross_out)):
        part = pl.pallas_call(
            functools.partial(combine_kernel, pair),
            out_shape=result,
            in_specs=[anywhere, vmem, vmem, vmem, vmem],
            out_specs=anywhere,
            scratch_shapes=[pltpu.VMEM((cap + 1, levels, columns), bf16), pltpu.SemaphoreType.DMA],
            input_output_aliases={0: 0},
            compiler_params=params(),
            name="combine_pair" if pair else "combine_cross",
        )(part, ends, sides, received, sent)
    return part


def solution(mesh):
    placed = (P("elem", "lev", None), P(None, None, "lev", "elem"), P(None, "elem"), P("elem"))
    return jax.shard_map(
        on_device, mesh=mesh, in_specs=placed, out_specs=P("elem", "lev", None), check_vma=False
    )
```

```python
import functools

import jax
import jax.numpy as jnp
from jax import lax
from jax.experimental import pallas as pl
from jax.experimental.pallas import tpu as pltpu
from jax.sharding import PartitionSpec as P

gll_points = (-1.0, -0.4472135954999579, 0.4472135954999579, 1.0)
courant = 0.15
f32 = jnp.float32
bf16 = jnp.bfloat16
VMEM_LIMIT = 40 << 20
CHUNK = 16

MASS, NEAR, NEAR_MASS, SOURCE, PACKET = 32, 48, 56, 60, 64


def params():
    return pltpu.CompilerParams(vmem_limit_bytes=VMEM_LIMIT)


def cost(work):
    return pl.CostEstimate(flops=100 * work, bytes_accessed=work, transcendentals=0)


def interleave(groups, members):
    size = groups * members
    row = lax.broadcasted_iota(jnp.int32, (size, size), 0)
    column = lax.broadcasted_iota(jnp.int32, (size, size), 1)
    same = (row // groups == column % members) & (row % groups == column // members)
    return jnp.where(same, 1.0, 0.0).astype(bf16)


def basis(position):
    out = []
    for a in range(4):
        scale = 1.0
        factor = None
        for other in range(4):
            if other != a:
                scale /= gll_points[a] - gll_points[other]
                term = position - gll_points[other]
                factor = term if factor is None else factor * term
        out.append(factor * scale)
    return out


def node_rows(rows, lanes, of_i):
    row = lax.broadcasted_iota(jnp.int32, (rows, lanes), 0)
    index = row // 4 if of_i else row % 4
    out = jnp.full((rows, lanes), gll_points[0], f32)
    for a in range(1, 4):
        out = jnp.where(index == a, gll_points[a], out)
    return out


def table(winds, coefficient):
    rows, lanes = winds[0].shape
    along = basis(node_rows(rows, lanes, True) - courant * winds[0])
    across_position = node_rows(rows, lanes, False) - courant * winds[1]
    across = [factor * coefficient for factor in basis(across_position)]
    return along, across


def is_even():
    return lax.axis_index("elem") % 2 == 0


def prepare_kernel(
    tracers_hbm, velocity_hbm, mass_hbm, source_hbm,
    here_ref, lowest_ref, cross_ref, pair_ref, velocity_ref, mass_ref, source_ref,
    tracers_ref, sems,
):
    elements, levels, columns = tracers_hbm.shape
    step = 256
    copies = [
        pltpu.make_async_copy(here, there, sems.at[n])
        for n, (here, there) in enumerate(
            ((velocity_hbm, velocity_ref), (mass_hbm, mass_ref), (source_hbm, source_ref))
        )
    ]
    copies.append(pltpu.make_async_copy(tracers_hbm, tracers_ref, sems.at[3]))
    for copy in copies:
        copy.start()
    for copy in copies[:3]:
        copy.wait()
    even = is_even()
    refs = (velocity_ref, mass_ref, source_ref)

    def both(head_ref, tail_ref):
        pack(True, *refs, head_ref)
        pack(False, *refs, tail_ref)

    pl.when(even)(lambda: both(cross_ref, pair_ref))
    pl.when(jnp.logical_not(even))(lambda: both(pair_ref, cross_ref))
    order = interleave(levels, elements)
    copies[3].wait()
    x = tracers_ref[...].reshape(elements * levels, columns)
    for n in range(0, columns, step):
        y = lax.dot_general(
            x[:, n : n + step], order, (((0,), (0,)), ((), ())), preferred_element_type=f32
        ).astype(bf16)
        here_ref[n : n + step, :] = y
        lowest_ref[n : n + step, :] = y[:, (levels - 1) * elements :]


def pack(head, velocity_ref, mass_ref, source_ref, out_ref):
    _, _, levels, elements = velocity_ref.shape
    cap = elements // levels
    runs = lax.axis_size("elem")
    start = lax.axis_index("elem") * elements
    total = runs * elements
    low, nodes, step = (0, 0, 1) if head else (elements - cap, 3, -1)

    def lanes(pieces, shift=0):
        return jnp.concatenate([x[:, low + shift : low + shift + cap] for x in pieces], axis=1)

    for c in range(2):
        pieces = [velocity_ref[c, :, k, :] for k in range(levels)]
        out_ref[16 * c : 16 * c + 16, :] = lanes(pieces)
        near = lanes(pieces, step)
        for j in range(4):
            out_ref[NEAR + 4 * c + j : NEAR + 4 * c + j + 1, :] = near[4 * j + nodes : 4 * j + nodes + 1]
    mass = mass_ref[...]
    out_ref[MASS : MASS + 16, :] = lanes([mass] * levels)
    near = lanes([mass] * levels, step)
    for j in range(4):
        out_ref[NEAR_MASS + j : NEAR_MASS + j + 1, :] = near[4 * j + nodes : 4 * j + nodes + 1]
    relative = source_ref[...] - start + step * elements
    relative = jnp.where(relative < 0, relative + total, relative)
    relative = jnp.where(relative < 0, relative + total, relative)
    relative = jnp.where(relative >= total, relative - total, relative)
    out_ref[SOURCE : SOURCE + 1, :] = lanes([relative.astype(f32)] * levels)
    out_ref[SOURCE + 1 :, :] = jnp.zeros((PACKET - SOURCE - 1, elements), f32)


def lift_kernel(here_ref, above_ref, velocity_ref, out_ref):
    _, nodes, levels, elements = velocity_ref.shape
    tracers = here_ref.shape[0] // nodes
    below_top = lax.axis_index("lev") > 0
    for k in range(levels):
        descent = 1.0 / (1.0 + jnp.exp(-velocity_ref[2, :, k, :]))
        lanes = slice(k * elements, (k + 1) * elements)
        for m in range(nodes):
            rows = slice(m * tracers, (m + 1) * tracers)
            here = here_ref[rows, lanes].astype(f32)
            if k == 0:
                upper = jnp.where(below_top, above_ref[rows, :].astype(f32), 0.0)
            else:
                upper = here_ref[rows, (k - 1) * elements : k * elements].astype(f32)
            d = descent[m : m + 1]
            out_ref[m, :, lanes] = ((1.0 - d) * here + d * upper).astype(bf16)


def by_i(ref, first, nodes=16):
    return [ref[pl.ds(first + i, 4, stride=4), :] for i in range(4)]


def shared(mass_left, left, mass_right, right):
    return (mass_left * left + mass_right * right) / (mass_left + mass_right)


def interpolate(weights_ref, blocks_ref, node, rows, lanes, *slot):
    total = None
    for m in range(16):
        term = weights_ref[m, node : node + 1, :] * blocks_ref[(*slot, m, rows, lanes)]
        total = term if total is None else total + term
    return total


def fetch(lifted_ref, t, lanes, chosen):
    x = lifted_ref[:, pl.ds(t, CHUNK), lanes].reshape(16 * CHUNK, chosen.shape[0])
    y = jnp.dot(x, chosen, preferred_element_type=f32)
    return y.reshape(16, CHUNK, chosen.shape[1])


def by_side(pair, body, *args):
    even = is_even()
    ahead = even if pair else jnp.logical_not(even)
    pl.when(ahead)(lambda: body(True, *args))
    pl.when(jnp.logical_not(ahead))(lambda: body(False, *args))


def weigh_kernel(pair, levels, after_ref, packet_ref, own_ref, weights_ref, extra_ref, chosen_ref):
    del after_ref
    by_side(pair, weigh, levels, packet_ref, own_ref, weights_ref, extra_ref, chosen_ref)


def remote_kernel(pair, after_ref, *refs):
    del after_ref
    by_side(pair, remote, *refs)


def weigh(ahead, levels, packet_ref, own_ref, weights_ref, extra_ref, chosen_ref):
    lanes_all = packet_ref.shape[1]
    elements = lanes_all
    cap = elements // levels
    total = lax.axis_size("elem") * elements
    lane = lax.broadcasted_iota(jnp.int32, (1, lanes_all), 1)
    level, place = lane // cap, lane % cap
    edge = place == (0 if ahead else cap - 1)

    def beside(values, own):
        if ahead:
            return jnp.where(edge, pltpu.roll(own, lanes_all - (cap - 1), 1), pltpu.roll(values, 1, 1))
        return jnp.where(edge, pltpu.roll(own, cap - 1, 1), pltpu.roll(values, lanes_all - 1, 1))

    mass = by_i(packet_ref, MASS)
    own_mass = by_i(own_ref, MASS)
    near_mass = packet_ref[NEAR_MASS : NEAR_MASS + 4, :]
    if ahead:
        mass_before, mass_after = beside(mass[3], own_mass[3]), near_mass
    else:
        mass_before, mass_after = near_mass, beside(mass[0], own_mass[0])
    share_west = mass[0] / (mass_before + mass[0])
    share_east = mass[3] / (mass[3] + mass_after)
    winds = []
    edge_winds = []
    for c in range(2):
        wind = by_i(packet_ref, 16 * c)
        own = by_i(own_ref, 16 * c)
        near = packet_ref[NEAR + 4 * c : NEAR + 4 * c + 4, :]
        if ahead:
            before, after = beside(wind[3], own[3]), near
        else:
            before, after = near, beside(wind[0], own[0])
        west = shared(mass_before, before, mass[0], wind[0])
        east = shared(mass[3], wind[3], mass_after, after)
        winds.append(jnp.concatenate([west, wind[1], wind[2], east], axis=0))
        edge_winds.append(west if ahead else east)
    ones = jnp.ones((8, lanes_all), f32)
    along, across = table(winds, jnp.concatenate([share_west, ones, share_east], axis=0))
    for b in range(4):
        for a in range(4):
            weights_ref[4 * b + a] = along[a] * across[b]
    edge_share = 1.0 - (share_west if ahead else share_east)
    extra_along = basis(gll_points[3 if ahead else 0] - courant * edge_winds[0])
    across_position = node_rows(4, lanes_all, False) - courant * edge_winds[1]
    extra_across = [factor * edge_share for factor in basis(across_position)]
    for b in range(4):
        for a in range(4):
            extra_ref[4 * b + a, 0:4] = extra_along[a] * extra_across[b]

    source = packet_ref[SOURCE : SOURCE + 1, :].astype(jnp.int32)
    own_source = own_ref[SOURCE : SOURCE + 1, :].astype(jnp.int32) + (elements if ahead else -elements)
    own_source = jnp.where(own_source >= total, own_source - total, own_source)
    own_source = jnp.where(own_source < 0, own_source + total, own_source)
    own_source = pltpu.roll(own_source, lanes_all - (cap - 1) if ahead else cap - 1, 1)
    row = lax.broadcasted_iota(jnp.int32, (levels * elements, lanes_all), 0)
    same = row // elements == level
    first = jnp.where(same & (row % elements == source), 1.0, 0.0).astype(bf16)
    second = jnp.where(same & edge & (row % elements == own_source), 1.0, 0.0).astype(bf16)
    chosen_ref[...] = jnp.concatenate([first, second], axis=1)


def remote(ahead, lifted_ref, weights_ref, extra_ref, chosen_ref, out_ref, blocks_ref, edge_ref):
    lanes_all = out_ref.shape[1]
    levels = lifted_ref.shape[2] // lanes_all
    cap = lanes_all // levels
    tracers = lifted_ref.shape[1]
    lane = lax.broadcasted_iota(jnp.int32, (1, lanes_all), 1)
    place = lane % cap
    edge = place == (0 if ahead else cap - 1)
    chosen = chosen_ref[...]
    for m in range(0, 16, 4):
        x = lifted_ref[m : m + 4].reshape(4 * tracers, levels * lanes_all)
        y = jnp.dot(x, chosen, preferred_element_type=f32)
        blocks_ref[m : m + 4] = y.reshape(4, tracers, 2 * lanes_all)

    def one(index, carry):
        t = pl.multiple_of(index * CHUNK, CHUNK)
        rows = pl.ds(t, CHUNK)
        lanes = slice(0, lanes_all)
        for j in range(4):
            moved = [interpolate(weights_ref, blocks_ref, 4 * i + j, rows, lanes) for i in range(4)]
            own = interpolate(extra_ref, blocks_ref, j, rows, slice(lanes_all, 2 * lanes_all))
            if ahead:
                west = moved[0] + jnp.where(edge, own, pltpu.roll(moved[3], 1, 1))
                values, far = (west, moved[1], moved[2]), moved[3]
            else:
                east = moved[3] + jnp.where(edge, own, pltpu.roll(moved[0], lanes_all - 1, 1))
                values, far = (moved[1], moved[2], east), moved[0]
            for i, value in enumerate(values):
                out_ref[pl.ds(t + (3 * j + i) * tracers, CHUNK), :] = value.astype(bf16)
            edge_ref[pl.ds(t + j * tracers, CHUNK), :] = far.astype(bf16)
        return carry

    lax.fori_loop(0, tracers // CHUNK, one, 0)
    row = lax.broadcasted_iota(jnp.int32, (8, lanes_all), 0)
    far_place = cap - 1 if ahead else 0
    pick = jnp.where(lane == row * cap + far_place, 1.0, 0.0).astype(bf16)
    far = lax.dot_general(pick, edge_ref[...], (((1,), (1,)), ((), ())), preferred_element_type=f32)
    far = [far[:, n : n + lanes_all] for n in range(0, 4 * tracers, lanes_all)]
    out_ref[12 * tracers :, :] = jnp.concatenate(far, axis=0).astype(bf16)


def local_kernel(
    velocity_ref, mass_ref, source_ref, lifted_ref, after_ref,
    out_ref, ends_ref, sides_ref,
    blocks_ref, weights_ref, wind_ref, moved_ref, inner_ref, sems,
):
    del after_ref
    _, _, levels, elements = velocity_ref.shape
    cap = elements // levels
    columns = out_ref.shape[2]
    tracers = columns // 16
    start = lax.axis_index("elem") * elements
    lane = lax.broadcasted_iota(jnp.int32, (1, elements), 1)
    mass = by_i(mass_ref, 0)
    mass_before = pltpu.roll(mass[3], 1, 1)
    mass_after = pltpu.roll(mass[0], elements - 1, 1)
    share_west = mass[0] / (mass_before + mass[0])
    share_east = mass[3] / (mass[3] + mass_after)
    coefficient = jnp.concatenate([share_west, jnp.ones((8, elements), f32), share_east], axis=0)
    row = lax.broadcasted_iota(jnp.int32, (elements, elements), 0)
    chosen = jnp.where(row == source_ref[...] - start, 1.0, 0.0).astype(bf16)
    blocks_ref[0] = fetch(lifted_ref, 0, slice(0, elements), chosen)
    for k in range(levels):
        winds = []
        for c in range(2):
            wind_ref[c] = velocity_ref[c, :, k, :]
            wind = [wind_ref[c, pl.ds(i, 4, stride=4), :] for i in range(4)]
            west = shared(mass_before, pltpu.roll(wind[3], 1, 1), mass[0], wind[0])
            east = shared(mass[3], wind[3], mass_after, pltpu.roll(wind[0], elements - 1, 1))
            winds.append(jnp.concatenate([west, wind[1], wind[2], east], axis=0))
        along, across = table(winds, coefficient)
        for b in range(4):
            for a in range(4):
                weights_ref[4 * b + a] = along[a] * across[b]
        lanes = slice(k * elements, (k + 1) * elements)

        def one(t, slot, later, later_lanes):
            blocks_ref[1 - slot] = fetch(lifted_ref, later, later_lanes, chosen)
            for j in range(4):
                moved = [
                    interpolate(weights_ref, blocks_ref, 4 * i + j, slice(None), slice(0, elements), slot)
                    for i in range(4)
                ]
                west = jnp.where(lane == 0, 0.0, moved[0] + pltpu.roll(moved[3], 1, 1))
                east = pltpu.roll(west, elements - 1, 1)
                for i, value in enumerate((west, moved[1], moved[2], east)):
                    moved_ref[pl.ds(t + (4 * j + i) * tracers, CHUNK), lanes] = value.astype(bf16)

        def two(index, carry):
            t = pl.multiple_of(index * (2 * CHUNK), 2 * CHUNK)
            later = t + 2 * CHUNK
            over = later >= tracers
            level = jnp.where(over, min(k + 1, levels - 1), k)
            later_lanes = pl.ds(pl.multiple_of(level * elements, elements), elements)
            one(t, 0, t + CHUNK, lanes)
            one(t + CHUNK, 1, pl.multiple_of(jnp.where(over, 0, later), CHUNK), later_lanes)
            return carry

        lax.fori_loop(0, tracers // (2 * CHUNK), two, 0)
    inner = elements - 2 * cap
    row = lax.broadcasted_iota(jnp.int32, (inner * levels, elements * levels), 0)
    column = lax.broadcasted_iota(jnp.int32, (inner * levels, elements * levels), 1)
    same = (row // levels + cap == column % elements) & (row % levels == column // elements)
    order = jnp.where(same, 1.0, 0.0).astype(bf16)
    step = columns // 4
    stores = []
    for n in range(4):
        part = pl.ds(n * step, step)
        y = lax.dot_general(
            order, moved_ref[part, :], (((1,), (1,)), ((), ())), preferred_element_type=f32
        )
        inner_ref[:, :, part] = y.reshape(inner, levels, step).astype(bf16)
        stores.append(pltpu.make_async_copy(
            inner_ref.at[pl.ds(1, inner - 2), :, part], out_ref.at[pl.ds(cap + 1, inner - 2), :, part], sems.at[n]
        ))
        stores[n].start()
    sides_ref[0] = inner_ref[0]
    sides_ref[1] = inner_ref[inner - 1]
    for n, low in enumerate((0, elements - cap)):
        ends_ref[n] = jnp.concatenate(
            [moved_ref[:, k * elements + low : k * elements + low + cap] for k in range(levels)], axis=1
        )
    for store in stores:
        store.wait()


def combine_kernel(pair, part_ref, ends_ref, sides_ref, received_ref, sent_ref, out_ref, rows_ref, sems):
    del part_ref
    refs = (ends_ref, sides_ref, received_ref, sent_ref, out_ref, rows_ref, sems)
    even = is_even()
    head = jnp.logical_not(even) if pair else even
    pl.when(head)(lambda: combine(True, *refs))
    pl.when(jnp.logical_not(head))(lambda: combine(False, *refs))


def combine(head, ends_ref, sides_ref, received_ref, sent_ref, out_ref, rows_ref, sems):
    elements, levels, columns = out_ref.shape
    lanes_all = received_ref.shape[1]
    cap = elements // levels
    tracers = columns // 16
    end = 0 if head else 1
    place = lax.broadcasted_iota(jnp.int32, (1, lanes_all), 1) % cap
    order = interleave(levels, cap)
    span = 4 * tracers
    spot = pl.ds(0, cap + 1) if head else pl.ds(elements - cap - 1, cap + 1)

    def rows(ref, block):
        return ref[block * tracers : (block + 1) * tracers, :].astype(f32)

    stores = []
    for j in range(4):
        got = [rows(received_ref, 3 * j + i) for i in range(3)]
        if head:
            own = pltpu.roll(rows(sent_ref, 3 * j + 2), lanes_all - (cap - 1), 1)
            west = got[0] + jnp.where(place == 0, own, 0.0)
            east = jnp.where(place == cap - 1, 0.0, pltpu.roll(got[0], lanes_all - 1, 1))
            got = [west, got[1], got[2], east]
        else:
            own = pltpu.roll(rows(sent_ref, 3 * j), cap - 1, 1)
            east = got[2] + jnp.where(place == cap - 1, own, 0.0)
            west = jnp.where(place == 0, 0.0, pltpu.roll(got[2], 1, 1))
            got = [west, got[0], got[1], east]
        pieces = []
        for i, value in enumerate(got):
            node = 4 * j + i
            here = ends_ref[end, node * tracers : (node + 1) * tracers, :].astype(f32)
            pieces.append((here + value).astype(bf16))
        y = lax.dot_general(
            order, jnp.concatenate(pieces, axis=0), (((1,), (1,)), ((), ())), preferred_element_type=f32
        ).reshape(cap, levels, span)
        first = 12 * tracers + 8 * (j * tracers // lanes_all)
        low = j * tracers % lanes_all
        far = received_ref[first : first + 8, low : low + tracers].astype(f32)[:levels]
        zeros = jnp.zeros((levels, span - tracers), f32)
        west = jnp.concatenate([far, zeros], axis=1)
        east = jnp.concatenate([zeros, far], axis=1)
        part = slice(j * span, (j + 1) * span)
        if head:
            rows_ref[0 : cap - 1, :, part] = y[: cap - 1].astype(bf16)
            rows_ref[cap - 1, :, part] = (y[cap - 1] + east).astype(bf16)
            rows_ref[cap, :, part] = (sides_ref[0, :, part].astype(f32) + west).astype(bf16)
        else:
            rows_ref[2:, :, part] = y[1:].astype(bf16)
            rows_ref[1, :, part] = (y[0] + west).astype(bf16)
            rows_ref[0, :, part] = (sides_ref[1, :, part].astype(f32) + east).astype(bf16)
        part = pl.ds(j * span, span)
        stores.append(pltpu.make_async_copy(rows_ref.at[:, :, part], out_ref.at[spot, :, part], sems.at[j]))
        stores[j].start()
    for store in stores:
        store.wait()


def on_device(tracers, velocity, node_mass, source):
    elements, levels, columns = tracers.shape
    cap = elements // 4
    assert cap * levels == elements
    count = columns // 16
    lanes = levels * elements
    runs = lax.axis_size("elem")
    pairing = [(i, i ^ 1) for i in range(runs)]
    crossing = [(i, (i - 1 if i % 2 == 0 else i + 1) % runs) for i in range(runs)]
    shape = jax.ShapeDtypeStruct
    vmem = pl.BlockSpec(memory_space=pltpu.VMEM)
    anywhere = pl.BlockSpec(memory_space=pl.ANY)
    source = source.reshape(1, elements)

    packet = shape((PACKET, elements), f32)
    inputs = (tracers, velocity, node_mass, source)
    here, lowest, cross_sent, pair_sent, velocity, node_mass, source = pl.pallas_call(
        prepare_kernel,
        out_shape=(shape((columns, lanes), bf16), shape((columns, elements), bf16), packet, packet)
        + tuple(shape(x.shape, x.dtype) for x in inputs[1:]),
        in_specs=[anywhere] * 4,
        scratch_shapes=[pltpu.VMEM(tracers.shape, bf16), pltpu.SemaphoreType.DMA((4,))],
        compiler_params=params(),
        name="prepare",
    )(*[pltpu.with_memory_space_constraint(x, pltpu.HBM) for x in inputs])
    blocks = lax.axis_size("lev")
    above = lax.ppermute(lowest, "lev", [(i, (i + 1) % blocks) for i in range(blocks)])
    pair_packet = lax.ppermute(pair_sent, "elem", pairing)
    cross_packet = lax.ppermute(cross_sent, "elem", crossing)
    def weighed(pair, packet, own, after):
        return pl.pallas_call(
            functools.partial(weigh_kernel, pair, levels),
            out_shape=(
                shape((16, 16, elements), f32),
                shape((16, 8, elements), f32),
                shape((lanes, 2 * elements), bf16),
            ),
            in_specs=[anywhere, vmem, vmem],
            compiler_params=params(),
            name="weigh_pair" if pair else "weigh_cross",
        )(after, packet, own)

    lifted = pl.pallas_call(
        lift_kernel,
        out_shape=shape((16, count, lanes), bf16),
        compiler_params=params(),
        name="lift",
    )(here, above, velocity)

    far_rows = 8 * (4 * count // elements)

    def contributions(pair, weights, after):
        return pl.pallas_call(
            functools.partial(remote_kernel, pair),
            out_shape=shape((12 * count + far_rows, elements), bf16),
            in_specs=[anywhere] + [vmem] * 4,
            scratch_shapes=[
                pltpu.VMEM((16, count, 2 * elements), f32),
                pltpu.VMEM((4 * count, elements), bf16),
            ],
            compiler_params=params(),
            name="remote_pair" if pair else "remote_cross",
        )(after, lifted, *weights)

    pair_out = contributions(True, weighed(True, pair_packet, pair_sent, lifted), lifted)
    pair_in = lax.ppermute(pair_out, "elem", pairing)
    cross_out = contributions(False, weighed(False, cross_packet, cross_sent, pair_out), pair_out)
    cross_in = lax.ppermute(cross_out, "elem", crossing)
    result = shape((elements, levels, columns), bf16)
    part, ends, sides = pl.pallas_call(
        local_kernel,
        out_shape=(result, shape((2, columns, elements), bf16), shape((2, levels, columns), bf16)),
        in_specs=[vmem] * 4 + [anywhere],
        out_specs=(anywhere, vmem, vmem),
        scratch_shapes=[
            pltpu.VMEM((2, 16, CHUNK, elements), f32),
            pltpu.VMEM((16, 16, elements), f32),
            pltpu.VMEM((2, 16, elements), f32),
            pltpu.VMEM((columns, lanes), bf16),
            pltpu.VMEM((elements - 2 * cap, levels, columns), bf16),
            pltpu.SemaphoreType.DMA((4,)),
        ],
        compiler_params=params(),
        cost_estimate=cost(10**9),
        name="local",
    )(velocity, node_mass, source, lifted, cross_out)
    for pair, received, sent in ((True, pair_in, pair_out), (False, cross_in, cross_out)):
        part = pl.pallas_call(
            functools.partial(combine_kernel, pair),
            out_shape=result,
            in_specs=[anywhere, vmem, vmem, vmem, vmem],
            out_specs=anywhere,
            scratch_shapes=[pltpu.VMEM((cap + 1, levels, columns), bf16), pltpu.SemaphoreType.DMA((4,))],
            input_output_aliases={0: 0},
            compiler_params=params(),
            name="combine_pair" if pair else "combine_cross",
        )(part, ends, sides, received, sent)
    return part


def solution(mesh):
    placed = (P("elem", "lev", None), P(None, None, "lev", "elem"), P(None, "elem"), P("elem"))
    return jax.shard_map(
        on_device, mesh=mesh, in_specs=placed, out_specs=P("elem", "lev", None), check_vma=False
    )
```

```python
import functools

import jax
import jax.numpy as jnp
from jax import lax
from jax.experimental import pallas as pl
from jax.experimental.pallas import tpu as pltpu
from jax.sharding import PartitionSpec as P

gll_points = (-1.0, -0.4472135954999579, 0.4472135954999579, 1.0)
courant = 0.15
f32 = jnp.float32
bf16 = jnp.bfloat16
VMEM_LIMIT = 40 << 20

MASS, NEAR, NEAR_MASS, SOURCE, PACKET = 32, 48, 56, 60, 64


def params():
    return pltpu.CompilerParams(vmem_limit_bytes=VMEM_LIMIT)


def cost(work):
    return pl.CostEstimate(flops=100 * work, bytes_accessed=work, transcendentals=0)


def interleave(groups, members):
    size = groups * members
    row = lax.broadcasted_iota(jnp.int32, (size, size), 0)
    column = lax.broadcasted_iota(jnp.int32, (size, size), 1)
    same = (row // groups == column % members) & (row % groups == column // members)
    return jnp.where(same, 1.0, 0.0).astype(bf16)


def basis(position):
    out = []
    for a in range(4):
        scale = 1.0
        factor = None
        for other in range(4):
            if other != a:
                scale /= gll_points[a] - gll_points[other]
                term = position - gll_points[other]
                factor = term if factor is None else factor * term
        out.append(factor * scale)
    return out


def node_rows(rows, lanes, of_i):
    row = lax.broadcasted_iota(jnp.int32, (rows, lanes), 0)
    index = row // 4 if of_i else row % 4
    out = jnp.full((rows, lanes), gll_points[0], f32)
    for a in range(1, 4):
        out = jnp.where(index == a, gll_points[a], out)
    return out


def table(winds, coefficient):
    rows, lanes = winds[0].shape
    along = basis(node_rows(rows, lanes, True) - courant * winds[0])
    across_position = node_rows(rows, lanes, False) - courant * winds[1]
    across = [factor * coefficient for factor in basis(across_position)]
    return along, across


def is_even():
    return lax.axis_index("elem") % 2 == 0


def prepare_kernel(
    tracers_hbm, velocity_hbm, mass_hbm, source_hbm,
    here_ref, lowest_ref, cross_ref, pair_ref, velocity_ref, mass_ref, source_ref,
    tracers_ref, sems,
):
    elements, levels, columns = tracers_hbm.shape
    step = 256
    copies = [
        pltpu.make_async_copy(here, there, sems.at[n])
        for n, (here, there) in enumerate(
            ((velocity_hbm, velocity_ref), (mass_hbm, mass_ref), (source_hbm, source_ref))
        )
    ]
    copies.append(pltpu.make_async_copy(tracers_hbm, tracers_ref, sems.at[3]))
    for copy in copies:
        copy.start()
    for copy in copies[:3]:
        copy.wait()
    even = is_even()
    refs = (velocity_ref, mass_ref, source_ref)

    def both(head_ref, tail_ref):
        pack(True, *refs, head_ref)
        pack(False, *refs, tail_ref)

    pl.when(even)(lambda: both(cross_ref, pair_ref))
    pl.when(jnp.logical_not(even))(lambda: both(pair_ref, cross_ref))
    order = interleave(levels, elements)
    copies[3].wait()
    x = tracers_ref[...].reshape(elements * levels, columns)
    for n in range(0, columns, step):
        y = lax.dot_general(
            x[:, n : n + step], order, (((0,), (0,)), ((), ())), preferred_element_type=f32
        ).astype(bf16)
        here_ref[n : n + step, :] = y
        lowest_ref[n : n + step, :] = y[:, (levels - 1) * elements :]


def pack(head, velocity_ref, mass_ref, source_ref, out_ref):
    _, _, levels, elements = velocity_ref.shape
    cap = elements // levels
    runs = lax.axis_size("elem")
    start = lax.axis_index("elem") * elements
    total = runs * elements
    low, nodes, step = (0, 0, 1) if head else (elements - cap, 3, -1)

    def lanes(pieces, shift=0):
        return jnp.concatenate([x[:, low + shift : low + shift + cap] for x in pieces], axis=1)

    for c in range(2):
        pieces = [velocity_ref[c, :, k, :] for k in range(levels)]
        out_ref[16 * c : 16 * c + 16, :] = lanes(pieces)
        near = lanes(pieces, step)
        for j in range(4):
            out_ref[NEAR + 4 * c + j : NEAR + 4 * c + j + 1, :] = near[4 * j + nodes : 4 * j + nodes + 1]
    mass = mass_ref[...]
    out_ref[MASS : MASS + 16, :] = lanes([mass] * levels)
    near = lanes([mass] * levels, step)
    for j in range(4):
        out_ref[NEAR_MASS + j : NEAR_MASS + j + 1, :] = near[4 * j + nodes : 4 * j + nodes + 1]
    relative = source_ref[...] - start + step * elements
    relative = jnp.where(relative < 0, relative + total, relative)
    relative = jnp.where(relative < 0, relative + total, relative)
    relative = jnp.where(relative >= total, relative - total, relative)
    out_ref[SOURCE : SOURCE + 1, :] = lanes([relative.astype(f32)] * levels)
    out_ref[SOURCE + 1 :, :] = jnp.zeros((PACKET - SOURCE - 1, elements), f32)


def lift(here, upper, descent):
    return ((1.0 - descent) * here.astype(f32) + descent * upper.astype(f32)).astype(bf16)


def descents(velocity_ref, k):
    return 1.0 / (1.0 + jnp.exp(-velocity_ref[2, :, k, :]))


def lift_rest_kernel(here_ref, velocity_ref, out_ref):
    _, nodes, levels, elements = velocity_ref.shape
    tracers = here_ref.shape[0] // nodes
    for k in range(1, levels):
        descent = descents(velocity_ref, k)
        for m in range(nodes):
            rows = slice(m * tracers, (m + 1) * tracers)
            here = here_ref[rows, k * elements : (k + 1) * elements]
            upper = here_ref[rows, (k - 1) * elements : k * elements]
            out_ref[m, :, (k - 1) * elements : k * elements] = lift(here, upper, descent[m : m + 1])


def lift_first_kernel(after_ref, here_ref, above_ref, velocity_ref, out_ref):
    del after_ref
    _, nodes, _, elements = velocity_ref.shape
    tracers = above_ref.shape[0] // nodes
    descent = descents(velocity_ref, 0)
    below_top = lax.axis_index("lev") > 0
    for m in range(nodes):
        rows = slice(m * tracers, (m + 1) * tracers)
        upper = jnp.where(below_top, above_ref[rows, :].astype(f32), 0.0)
        out_ref[m] = lift(here_ref[rows, 0:elements], upper, descent[m : m + 1])


def by_i(ref, first, nodes=16):
    return [ref[pl.ds(first + i, 4, stride=4), :] for i in range(4)]


def shared(mass_left, left, mass_right, right):
    return (mass_left * left + mass_right * right) / (mass_left + mass_right)


def interpolate(weights_ref, blocks, nodes):
    totals = [None] * len(nodes)
    for m in range(16):
        block = blocks(m)
        for n, node in enumerate(nodes):
            term = weights_ref[m, node : node + 1, :] * block
            totals[n] = term if totals[n] is None else totals[n] + term
    return totals


def by_side(pair, body, *args):
    even = is_even()
    ahead = even if pair else jnp.logical_not(even)
    pl.when(ahead)(lambda: body(True, *args))
    pl.when(jnp.logical_not(ahead))(lambda: body(False, *args))


def weigh_kernel(pair, levels, after_ref, packet_ref, own_ref, weights_ref, extra_ref, chosen_ref):
    del after_ref
    by_side(pair, weigh, levels, packet_ref, own_ref, weights_ref, extra_ref, chosen_ref)


def remote_kernel(pair, after_ref, *refs):
    del after_ref
    by_side(pair, remote, *refs)


def weigh(ahead, levels, packet_ref, own_ref, weights_ref, extra_ref, chosen_ref):
    lanes_all = packet_ref.shape[1]
    elements = lanes_all
    cap = elements // levels
    total = lax.axis_size("elem") * elements
    lane = lax.broadcasted_iota(jnp.int32, (1, lanes_all), 1)
    level, place = lane // cap, lane % cap
    edge = place == (0 if ahead else cap - 1)

    def beside(values, own):
        if ahead:
            return jnp.where(edge, pltpu.roll(own, lanes_all - (cap - 1), 1), pltpu.roll(values, 1, 1))
        return jnp.where(edge, pltpu.roll(own, cap - 1, 1), pltpu.roll(values, lanes_all - 1, 1))

    mass = by_i(packet_ref, MASS)
    own_mass = by_i(own_ref, MASS)
    near_mass = packet_ref[NEAR_MASS : NEAR_MASS + 4, :]
    if ahead:
        mass_before, mass_after = beside(mass[3], own_mass[3]), near_mass
    else:
        mass_before, mass_after = near_mass, beside(mass[0], own_mass[0])
    share_west = mass[0] / (mass_before + mass[0])
    share_east = mass[3] / (mass[3] + mass_after)
    winds = []
    edge_winds = []
    for c in range(2):
        wind = by_i(packet_ref, 16 * c)
        own = by_i(own_ref, 16 * c)
        near = packet_ref[NEAR + 4 * c : NEAR + 4 * c + 4, :]
        if ahead:
            before, after = beside(wind[3], own[3]), near
        else:
            before, after = near, beside(wind[0], own[0])
        west = shared(mass_before, before, mass[0], wind[0])
        east = shared(mass[3], wind[3], mass_after, after)
        winds.append(jnp.concatenate([west, wind[1], wind[2], east], axis=0))
        edge_winds.append(west if ahead else east)
    ones = jnp.ones((8, lanes_all), f32)
    along, across = table(winds, jnp.concatenate([share_west, ones, share_east], axis=0))
    for b in range(4):
        for a in range(4):
            weights_ref[4 * b + a] = along[a] * across[b]
    at = 0 if ahead else cap - 1

    def spread(rows):
        out = jnp.zeros((1, lanes_all), f32)
        for j in range(4):
            out = jnp.where(place == j, pltpu.roll(rows[j : j + 1], (j - at) % lanes_all, 1), out)
        return out

    edge_share = spread(1.0 - (share_west if ahead else share_east))
    node = jnp.where(place < 2, jnp.where(place == 0, *gll_points[:2]), jnp.where(place == 2, *gll_points[2:]))
    extra_along = basis(gll_points[3 if ahead else 0] - courant * spread(edge_winds[0]))
    extra_across = [factor * edge_share for factor in basis(node - courant * spread(edge_winds[1]))]
    for b in range(4):
        for a in range(4):
            extra_ref[4 * b + a, 0:1] = extra_along[a] * extra_across[b]

    source = packet_ref[SOURCE : SOURCE + 1, :].astype(jnp.int32)
    own_source = jnp.where(lane == (cap - 1 if ahead else 0), own_ref[SOURCE : SOURCE + 1, :], 0.0)
    own_source = jnp.sum(own_source, axis=1, keepdims=True).astype(jnp.int32) + (elements if ahead else -elements)
    own_source = jnp.where(own_source >= total, own_source - total, own_source)
    own_source = jnp.where(own_source < 0, own_source + total, own_source)
    row = lax.broadcasted_iota(jnp.int32, (levels * elements, lanes_all), 0)
    same = row // elements == level
    first = jnp.where(same & (row % elements == source), 1.0, 0.0).astype(bf16)
    second = jnp.where(same & (place < 4) & (row % elements == own_source), 1.0, 0.0).astype(bf16)
    chosen_ref[...] = jnp.concatenate([first, second], axis=1)


def remote(ahead, first_ref, rest_ref, weights_ref, extra_ref, chosen_ref, out_ref, blocks_ref, edge_ref):
    lanes_all = out_ref.shape[1]
    levels = 1 + rest_ref.shape[2] // lanes_all
    cap = lanes_all // levels
    tracers = first_ref.shape[1]
    lane = lax.broadcasted_iota(jnp.int32, (1, lanes_all), 1)
    place = lane % cap
    edge = place == (0 if ahead else cap - 1)
    chosen = chosen_ref[...]
    for m in range(0, 16, 4):
        x = first_ref[m : m + 4].reshape(4 * tracers, lanes_all)
        y = jnp.dot(x, chosen[:lanes_all], preferred_element_type=f32)
        x = rest_ref[m : m + 4].reshape(4 * tracers, (levels - 1) * lanes_all)
        y += jnp.dot(x, chosen[lanes_all:], preferred_element_type=f32)
        blocks_ref[m : m + 4] = y.reshape(4, tracers, 2 * lanes_all)

    first = slice(0, lanes_all)
    (own,) = interpolate(extra_ref, lambda m: blocks_ref[m, :, lanes_all:], (0,))
    for j in range(4):
        ends = interpolate(weights_ref, lambda m: blocks_ref[m, :, first], (j, 12 + j))
        middle = interpolate(weights_ref, lambda m: blocks_ref[m, :, first], (4 + j, 8 + j))
        own_here = pltpu.roll(own, ((0 if ahead else cap - 1) - j) % lanes_all, 1)
        if ahead:
            west = ends[0] + jnp.where(edge, own_here, pltpu.roll(ends[1], 1, 1))
            values, far = (west, *middle), ends[1]
        else:
            east = ends[1] + jnp.where(edge, own_here, pltpu.roll(ends[0], lanes_all - 1, 1))
            values, far = (*middle, east), ends[0]
        for i, value in enumerate(values):
            out_ref[(3 * j + i) * tracers : (3 * j + i + 1) * tracers, :] = value.astype(bf16)
        edge_ref[j * tracers : (j + 1) * tracers, :] = far.astype(bf16)
    row = lax.broadcasted_iota(jnp.int32, (8, lanes_all), 0)
    far_place = cap - 1 if ahead else 0
    pick = jnp.where(lane == row * cap + far_place, 1.0, 0.0).astype(bf16)
    far = lax.dot_general(pick, edge_ref[...], (((1,), (1,)), ((), ())), preferred_element_type=f32)
    far = [far[:, n : n + lanes_all] for n in range(0, 4 * tracers, lanes_all)]
    out_ref[12 * tracers :, :] = jnp.concatenate(far, axis=0).astype(bf16)


def local_kernel(
    velocity_ref, mass_ref, source_ref, first_ref, rest_ref, after_ref,
    out_ref, ends_ref, sides_ref,
    blocks_ref, weights_ref, wind_ref, moved_ref, inner_ref, sems,
):
    del after_ref
    _, _, levels, elements = velocity_ref.shape
    cap = elements // levels
    columns = out_ref.shape[2]
    tracers = columns // 16
    start = lax.axis_index("elem") * elements
    lane = lax.broadcasted_iota(jnp.int32, (1, elements), 1)
    mass = by_i(mass_ref, 0)
    mass_before = pltpu.roll(mass[3], 1, 1)
    mass_after = pltpu.roll(mass[0], elements - 1, 1)
    share_west = mass[0] / (mass_before + mass[0])
    share_east = mass[3] / (mass[3] + mass_after)
    coefficient = jnp.concatenate([share_west, jnp.ones((8, elements), f32), share_east], axis=0)
    row = lax.broadcasted_iota(jnp.int32, (elements, elements), 0)
    chosen = jnp.where(row == source_ref[...] - start, 1.0, 0.0).astype(bf16)

    def fetch(k):
        x = rest_ref[:, :, (k - 1) * elements : k * elements] if k else first_ref[...]
        y = jnp.dot(x.reshape(columns, elements), chosen, preferred_element_type=f32)
        blocks_ref[k % 2] = y.reshape(16, tracers, elements)

    fetch(0)
    for k in range(levels):
        winds = []
        for c in range(2):
            wind_ref[c] = velocity_ref[c, :, k, :]
            wind = [wind_ref[c, pl.ds(i, 4, stride=4), :] for i in range(4)]
            west = shared(mass_before, pltpu.roll(wind[3], 1, 1), mass[0], wind[0])
            east = shared(mass[3], wind[3], mass_after, pltpu.roll(wind[0], elements - 1, 1))
            winds.append(jnp.concatenate([west, wind[1], wind[2], east], axis=0))
        along, across = table(winds, coefficient)
        for b in range(4):
            for a in range(4):
                weights_ref[k % 2, 4 * b + a] = along[a] * across[b]
        if k + 1 < levels:
            fetch(k + 1)
        lanes = slice(k * elements, (k + 1) * elements)
        table_ref = weights_ref.at[k % 2]
        for j in range(4):
            ends = interpolate(table_ref, lambda m: blocks_ref[k % 2, m], (j, 12 + j))
            middle = interpolate(table_ref, lambda m: blocks_ref[k % 2, m], (4 + j, 8 + j))
            west = jnp.where(lane == 0, 0.0, ends[0] + pltpu.roll(ends[1], 1, 1))
            east = pltpu.roll(west, elements - 1, 1)
            for i, value in enumerate((west, *middle, east)):
                node = 4 * j + i
                moved_ref[node * tracers : (node + 1) * tracers, lanes] = value.astype(bf16)
    inner = elements - 2 * cap
    row = lax.broadcasted_iota(jnp.int32, (inner * levels, elements * levels), 0)
    column = lax.broadcasted_iota(jnp.int32, (inner * levels, elements * levels), 1)
    same = (row // levels + cap == column % elements) & (row % levels == column // elements)
    order = jnp.where(same, 1.0, 0.0).astype(bf16)
    step = columns // 4
    stores = []
    for n in range(4):
        part = pl.ds(n * step, step)
        y = lax.dot_general(
            order, moved_ref[part, :], (((1,), (1,)), ((), ())), preferred_element_type=f32
        )
        inner_ref[:, :, part] = y.reshape(inner, levels, step).astype(bf16)
        stores.append(pltpu.make_async_copy(
            inner_ref.at[pl.ds(1, inner - 2), :, part], out_ref.at[pl.ds(cap + 1, inner - 2), :, part], sems.at[n]
        ))
        stores[n].start()
    sides_ref[0] = inner_ref[0]
    sides_ref[1] = inner_ref[inner - 1]
    for n, low in enumerate((0, elements - cap)):
        ends_ref[n] = jnp.concatenate(
            [moved_ref[:, k * elements + low : k * elements + low + cap] for k in range(levels)], axis=1
        )
    for store in stores:
        store.wait()


def combine_kernel(pair, part_ref, ends_ref, sides_ref, received_ref, sent_ref, out_ref, rows_ref, sems):
    del part_ref
    refs = (ends_ref, sides_ref, received_ref, sent_ref, out_ref, rows_ref, sems)
    even = is_even()
    head = jnp.logical_not(even) if pair else even
    pl.when(head)(lambda: combine(True, *refs))
    pl.when(jnp.logical_not(head))(lambda: combine(False, *refs))


def combine(head, ends_ref, sides_ref, received_ref, sent_ref, out_ref, rows_ref, sems):
    elements, levels, columns = out_ref.shape
    lanes_all = received_ref.shape[1]
    cap = elements // levels
    tracers = columns // 16
    end = 0 if head else 1
    place = lax.broadcasted_iota(jnp.int32, (1, lanes_all), 1) % cap
    order = interleave(levels, cap)
    span = 4 * tracers
    spot = pl.ds(0, cap + 1) if head else pl.ds(elements - cap - 1, cap + 1)

    def rows(ref, block):
        return ref[block * tracers : (block + 1) * tracers, :].astype(f32)

    stores = []
    for j in range(4):
        got = [rows(received_ref, 3 * j + i) for i in range(3)]
        if head:
            own = pltpu.roll(rows(sent_ref, 3 * j + 2), lanes_all - (cap - 1), 1)
            west = got[0] + jnp.where(place == 0, own, 0.0)
            east = jnp.where(place == cap - 1, 0.0, pltpu.roll(got[0], lanes_all - 1, 1))
            got = [west, got[1], got[2], east]
        else:
            own = pltpu.roll(rows(sent_ref, 3 * j), cap - 1, 1)
            east = got[2] + jnp.where(place == cap - 1, own, 0.0)
            west = jnp.where(place == 0, 0.0, pltpu.roll(got[2], 1, 1))
            got = [west, got[0], got[1], east]
        pieces = []
        for i, value in enumerate(got):
            node = 4 * j + i
            here = ends_ref[end, node * tracers : (node + 1) * tracers, :].astype(f32)
            pieces.append((here + value).astype(bf16))
        y = lax.dot_general(
            order, jnp.concatenate(pieces, axis=0), (((1,), (1,)), ((), ())), preferred_element_type=f32
        ).reshape(cap, levels, span)
        first = 12 * tracers + 8 * (j * tracers // lanes_all)
        low = j * tracers % lanes_all
        far = received_ref[first : first + 8, low : low + tracers].astype(f32)[:levels]
        zeros = jnp.zeros((levels, span - tracers), f32)
        west = jnp.concatenate([far, zeros], axis=1)
        east = jnp.concatenate([zeros, far], axis=1)
        part = slice(j * span, (j + 1) * span)
        if head:
            rows_ref[0 : cap - 1, :, part] = y[: cap - 1].astype(bf16)
            rows_ref[cap - 1, :, part] = (y[cap - 1] + east).astype(bf16)
            rows_ref[cap, :, part] = (sides_ref[0, :, part].astype(f32) + west).astype(bf16)
        else:
            rows_ref[2:, :, part] = y[1:].astype(bf16)
            rows_ref[1, :, part] = (y[0] + west).astype(bf16)
            rows_ref[0, :, part] = (sides_ref[1, :, part].astype(f32) + east).astype(bf16)
        part = pl.ds(j * span, span)
        stores.append(pltpu.make_async_copy(rows_ref.at[:, :, part], out_ref.at[spot, :, part], sems.at[j]))
        stores[j].start()
    for store in stores:
        store.wait()


def on_device(tracers, velocity, node_mass, source):
    elements, levels, columns = tracers.shape
    cap = elements // 4
    assert cap * levels == elements
    count = columns // 16
    lanes = levels * elements
    runs = lax.axis_size("elem")
    pairing = [(i, i ^ 1) for i in range(runs)]
    crossing = [(i, (i - 1 if i % 2 == 0 else i + 1) % runs) for i in range(runs)]
    shape = jax.ShapeDtypeStruct
    vmem = pl.BlockSpec(memory_space=pltpu.VMEM)
    anywhere = pl.BlockSpec(memory_space=pl.ANY)
    source = source.reshape(1, elements)

    packet = shape((PACKET, elements), f32)
    inputs = (tracers, velocity, node_mass, source)
    here, lowest, cross_sent, pair_sent, velocity, node_mass, source = pl.pallas_call(
        prepare_kernel,
        out_shape=(shape((columns, lanes), bf16), shape((columns, elements), bf16), packet, packet)
        + tuple(shape(x.shape, x.dtype) for x in inputs[1:]),
        in_specs=[anywhere] * 4,
        scratch_shapes=[pltpu.VMEM(tracers.shape, bf16), pltpu.SemaphoreType.DMA((4,))],
        compiler_params=params(),
        name="prepare",
    )(*[pltpu.with_memory_space_constraint(x, pltpu.HBM) for x in inputs])
    blocks = lax.axis_size("lev")
    above = lax.ppermute(lowest, "lev", [(i, (i + 1) % blocks) for i in range(blocks)])
    pair_packet = lax.ppermute(pair_sent, "elem", pairing)
    cross_packet = lax.ppermute(cross_sent, "elem", crossing)
    def weighed(pair, packet, own, after):
        return pl.pallas_call(
            functools.partial(weigh_kernel, pair, levels),
            out_shape=(
                shape((16, 16, elements), f32),
                shape((16, 8, elements), f32),
                shape((lanes, 2 * elements), bf16),
            ),
            in_specs=[anywhere, vmem, vmem],
            compiler_params=params(),
            name="weigh_pair" if pair else "weigh_cross",
        )(after, packet, own)

    pair_weights = weighed(True, pair_packet, pair_sent, lowest)
    rest = pl.pallas_call(
        lift_rest_kernel,
        out_shape=shape((16, count, lanes - elements), bf16),
        compiler_params=params(),
        name="lift_rest",
    )(here, velocity)
    first = pl.pallas_call(
        lift_first_kernel,
        out_shape=shape((16, count, elements), bf16),
        in_specs=[anywhere] + [vmem] * 3,
        compiler_params=params(),
        name="lift_first",
    )(pair_weights[1], here, above, velocity)

    far_rows = 8 * (4 * count // elements)

    def contributions(pair, weights, after):
        return pl.pallas_call(
            functools.partial(remote_kernel, pair),
            out_shape=shape((12 * count + far_rows, elements), bf16),
            in_specs=[anywhere] + [vmem] * 5,
            scratch_shapes=[
                pltpu.VMEM((16, count, 2 * elements), f32),
                pltpu.VMEM((4 * count, elements), bf16),
            ],
            compiler_params=params(),
            name="remote_pair" if pair else "remote_cross",
        )(after, first, rest, *weights)

    pair_out = contributions(True, pair_weights, first)
    pair_in = lax.ppermute(pair_out, "elem", pairing)
    cross_out = contributions(False, weighed(False, cross_packet, cross_sent, pair_out), pair_out)
    cross_in = lax.ppermute(cross_out, "elem", crossing)
    result = shape((elements, levels, columns), bf16)
    part, ends, sides = pl.pallas_call(
        local_kernel,
        out_shape=(result, shape((2, columns, elements), bf16), shape((2, levels, columns), bf16)),
        in_specs=[vmem] * 5 + [anywhere],
        out_specs=(anywhere, vmem, vmem),
        scratch_shapes=[
            pltpu.VMEM((2, 16, count, elements), f32),
            pltpu.VMEM((2, 16, 16, elements), f32),
            pltpu.VMEM((2, 16, elements), f32),
            pltpu.VMEM((columns, lanes), bf16),
            pltpu.VMEM((elements - 2 * cap, levels, columns), bf16),
            pltpu.SemaphoreType.DMA((4,)),
        ],
        compiler_params=params(),
        cost_estimate=cost(10**9),
        name="local",
    )(velocity, node_mass, source, first, rest, cross_out)
    for pair, received, sent in ((True, pair_in, pair_out), (False, cross_in, cross_out)):
        part = pl.pallas_call(
            functools.partial(combine_kernel, pair),
            out_shape=result,
            in_specs=[anywhere, vmem, vmem, vmem, vmem],
            out_specs=anywhere,
            scratch_shapes=[pltpu.VMEM((cap + 1, levels, columns), bf16), pltpu.SemaphoreType.DMA((4,))],
            input_output_aliases={0: 0},
            compiler_params=params(),
            name="combine_pair" if pair else "combine_cross",
        )(part, ends, sides, received, sent)
    return part


def solution(mesh):
    placed = (P("elem", "lev", None), P(None, None, "lev", "elem"), P(None, "elem"), P("elem"))
    return jax.shard_map(
        on_device, mesh=mesh, in_specs=placed, out_specs=P("elem", "lev", None), check_vma=False
    )
```

```python
import functools

import jax
import jax.numpy as jnp
from jax import lax
from jax.experimental import pallas as pl
from jax.experimental.pallas import tpu as pltpu
from jax.sharding import PartitionSpec as P

gll_points = (-1.0, -0.4472135954999579, 0.4472135954999579, 1.0)
courant = 0.15
f32 = jnp.float32
bf16 = jnp.bfloat16
VMEM_LIMIT = 40 << 20

MASS, NEAR, NEAR_MASS, SOURCE, PACKET = 32, 48, 56, 60, 64


def params():
    return pltpu.CompilerParams(vmem_limit_bytes=VMEM_LIMIT)


def cost(work):
    return pl.CostEstimate(flops=100 * work, bytes_accessed=work, transcendentals=0)


def interleave(groups, members):
    size = groups * members
    row = lax.broadcasted_iota(jnp.int32, (size, size), 0)
    column = lax.broadcasted_iota(jnp.int32, (size, size), 1)
    same = (row // groups == column % members) & (row % groups == column // members)
    return jnp.where(same, 1.0, 0.0).astype(bf16)


def basis(position):
    out = []
    for a in range(4):
        scale = 1.0
        factor = None
        for other in range(4):
            if other != a:
                scale /= gll_points[a] - gll_points[other]
                term = position - gll_points[other]
                factor = term if factor is None else factor * term
        out.append(factor * scale)
    return out


def node_rows(rows, lanes, of_i):
    row = lax.broadcasted_iota(jnp.int32, (rows, lanes), 0)
    index = row // 4 if of_i else row % 4
    out = jnp.full((rows, lanes), gll_points[0], f32)
    for a in range(1, 4):
        out = jnp.where(index == a, gll_points[a], out)
    return out


def table(winds, coefficient):
    rows, lanes = winds[0].shape
    along = basis(node_rows(rows, lanes, True) - courant * winds[0])
    across_position = node_rows(rows, lanes, False) - courant * winds[1]
    across = [factor * coefficient for factor in basis(across_position)]
    return along, across


def is_even():
    return lax.axis_index("elem") % 2 == 0


def prepare_kernel(
    tracers_hbm, velocity_hbm, mass_hbm, source_hbm,
    lowest_ref, cross_ref, pair_ref, tracers_ref, velocity_ref, mass_ref, source_ref, sems,
):
    elements, levels, columns = tracers_hbm.shape
    step = 256
    copies = [
        pltpu.make_async_copy(here, there, sems.at[n])
        for n, (here, there) in enumerate(
            ((velocity_hbm, velocity_ref), (mass_hbm, mass_ref), (source_hbm, source_ref))
        )
    ]
    half = elements // 2
    for n in range(2):
        part = pl.ds(n * half, half)
        copies.append(pltpu.make_async_copy(tracers_hbm.at[part], tracers_ref.at[part], sems.at[3 + n]))
    for copy in copies:
        copy.start()
    for copy in copies[:3]:
        copy.wait()
    even = is_even()
    refs = (velocity_ref, mass_ref, source_ref)

    def both(head_ref, tail_ref):
        pack(True, *refs, head_ref)
        pack(False, *refs, tail_ref)

    pl.when(even)(lambda: both(cross_ref, pair_ref))
    pl.when(jnp.logical_not(even))(lambda: both(pair_ref, cross_ref))
    row = lax.broadcasted_iota(jnp.int32, (half * levels, elements), 0)
    column = lax.broadcasted_iota(jnp.int32, (half * levels, elements), 1)
    for n in range(2):
        copies[3 + n].wait()
        x = tracers_ref[n * half : (n + 1) * half].reshape(half * levels, columns)
        pick = jnp.where(row + n * half * levels == column * levels + levels - 1, 1.0, 0.0).astype(bf16)
        for c in range(0, columns, step):
            y = lax.dot_general(
                x[:, c : c + step], pick, (((0,), (0,)), ((), ())), preferred_element_type=f32
            ).astype(bf16)
            lowest_ref[c : c + step, n * half : (n + 1) * half] = y[:, n * half : (n + 1) * half]


def pack(head, velocity_ref, mass_ref, source_ref, out_ref):
    _, _, levels, elements = velocity_ref.shape
    cap = elements // levels
    runs = lax.axis_size("elem")
    start = lax.axis_index("elem") * elements
    total = runs * elements
    low, nodes, step = (0, 0, 1) if head else (elements - cap, 3, -1)

    def lanes(pieces, shift=0):
        return jnp.concatenate([x[:, low + shift : low + shift + cap] for x in pieces], axis=1)

    for c in range(2):
        pieces = [velocity_ref[c, :, k, :] for k in range(levels)]
        out_ref[16 * c : 16 * c + 16, :] = lanes(pieces)
        near = lanes(pieces, step)
        for j in range(4):
            out_ref[NEAR + 4 * c + j : NEAR + 4 * c + j + 1, :] = near[4 * j + nodes : 4 * j + nodes + 1]
    mass = mass_ref[...]
    out_ref[MASS : MASS + 16, :] = lanes([mass] * levels)
    near = lanes([mass] * levels, step)
    for j in range(4):
        out_ref[NEAR_MASS + j : NEAR_MASS + j + 1, :] = near[4 * j + nodes : 4 * j + nodes + 1]
    relative = source_ref[...] - start + step * elements
    relative = jnp.where(relative < 0, relative + total, relative)
    relative = jnp.where(relative < 0, relative + total, relative)
    relative = jnp.where(relative >= total, relative - total, relative)
    out_ref[SOURCE : SOURCE + 1, :] = lanes([relative.astype(f32)] * levels)
    out_ref[SOURCE + 1 :, :] = jnp.zeros((PACKET - SOURCE - 1, elements), f32)


def lift(here, upper, descent):
    return ((1.0 - descent) * here.astype(f32) + descent * upper.astype(f32)).astype(bf16)


def descents(velocity_ref, k):
    return 1.0 / (1.0 + jnp.exp(-velocity_ref[2, :, k, :]))


def spread(tracers_ref, velocity_ref, top_ref, rest_ref, here_ref):
    elements, levels, columns = tracers_ref.shape
    nodes = velocity_ref.shape[1]
    tracers = columns // nodes
    order = interleave(levels, elements)
    x = tracers_ref[...].reshape(elements * levels, columns)
    step = 256
    for n in range(0, columns, step):
        here_ref[n : n + step, :] = lax.dot_general(
            x[:, n : n + step], order, (((0,), (0,)), ((), ())), preferred_element_type=f32
        ).astype(bf16)
    top_ref[...] = here_ref[:, :elements]
    for k in range(1, levels):
        descent = descents(velocity_ref, k)
        for m in range(nodes):
            rows = slice(m * tracers, (m + 1) * tracers)
            here = here_ref[rows, k * elements : (k + 1) * elements]
            upper = here_ref[rows, (k - 1) * elements : k * elements]
            rest_ref[m, :, (k - 1) * elements : k * elements] = lift(here, upper, descent[m : m + 1])


def spread_early_kernel(tracers_ref, velocity_ref, packet_ref, top_ref, rest_ref, sent_ref, here_ref):
    sent_ref[...] = packet_ref[...]
    pl.when(lax.axis_index("elem") == 0)(lambda: spread(tracers_ref, velocity_ref, top_ref, rest_ref, here_ref))


def spread_kernel(tracers_ref, velocity_ref, early_top_ref, early_rest_ref, top_ref, rest_ref, here_ref):
    early = lax.axis_index("elem") == 0

    @pl.when(early)
    def _():
        top_ref[...] = early_top_ref[...]
        rest_ref[...] = early_rest_ref[...]

    pl.when(jnp.logical_not(early))(lambda: spread(tracers_ref, velocity_ref, top_ref, rest_ref, here_ref))


def lift_first_kernel(after_ref, top_ref, above_ref, velocity_ref, out_ref):
    del after_ref
    _, nodes, _, elements = velocity_ref.shape
    tracers = above_ref.shape[0] // nodes
    descent = descents(velocity_ref, 0)
    below_top = lax.axis_index("lev") > 0
    for m in range(nodes):
        rows = slice(m * tracers, (m + 1) * tracers)
        upper = jnp.where(below_top, above_ref[rows, :].astype(f32), 0.0)
        out_ref[m] = lift(top_ref[rows, :], upper, descent[m : m + 1])


def by_i(ref, first, nodes=16):
    return [ref[pl.ds(first + i, 4, stride=4), :] for i in range(4)]


def shared(mass_left, left, mass_right, right):
    return (mass_left * left + mass_right * right) / (mass_left + mass_right)


def interpolate(weights_ref, blocks, nodes):
    totals = [None] * len(nodes)
    for m in range(16):
        block = blocks(m)
        for n, node in enumerate(nodes):
            term = weights_ref[m, node : node + 1, :] * block
            totals[n] = term if totals[n] is None else totals[n] + term
    return totals


def by_side(pair, body, *args):
    even = is_even()
    ahead = even if pair else jnp.logical_not(even)
    pl.when(ahead)(lambda: body(True, *args))
    pl.when(jnp.logical_not(ahead))(lambda: body(False, *args))


def weigh_kernel(pair, levels, after_ref, packet_ref, own_ref, weights_ref, extra_ref, chosen_ref):
    del after_ref
    by_side(pair, weigh, levels, packet_ref, own_ref, weights_ref, extra_ref, chosen_ref)


def remote_kernel(pair, after_ref, *refs):
    del after_ref
    by_side(pair, remote, *refs)


def weigh_remote_kernel(
    pair, levels, after_ref, packet_ref, own_ref, first_ref, rest_ref,
    out_ref, blocks_ref, edge_ref, weights_ref, extra_ref, chosen_ref,
):
    del after_ref
    tables = (weights_ref, extra_ref, chosen_ref)

    def both(ahead):
        weigh(ahead, levels, packet_ref, own_ref, *tables)
        remote(ahead, first_ref, rest_ref, *tables, out_ref, blocks_ref, edge_ref)

    by_side(pair, both)


def weigh(ahead, levels, packet_ref, own_ref, weights_ref, extra_ref, chosen_ref):
    lanes_all = packet_ref.shape[1]
    elements = lanes_all
    cap = elements // levels
    total = lax.axis_size("elem") * elements
    lane = lax.broadcasted_iota(jnp.int32, (1, lanes_all), 1)
    level, place = lane // cap, lane % cap
    edge = place == (0 if ahead else cap - 1)

    def beside(values, own):
        if ahead:
            return jnp.where(edge, pltpu.roll(own, lanes_all - (cap - 1), 1), pltpu.roll(values, 1, 1))
        return jnp.where(edge, pltpu.roll(own, cap - 1, 1), pltpu.roll(values, lanes_all - 1, 1))

    mass = by_i(packet_ref, MASS)
    own_mass = by_i(own_ref, MASS)
    near_mass = packet_ref[NEAR_MASS : NEAR_MASS + 4, :]
    if ahead:
        mass_before, mass_after = beside(mass[3], own_mass[3]), near_mass
    else:
        mass_before, mass_after = near_mass, beside(mass[0], own_mass[0])
    share_west = mass[0] / (mass_before + mass[0])
    share_east = mass[3] / (mass[3] + mass_after)
    winds = []
    edge_winds = []
    for c in range(2):
        wind = by_i(packet_ref, 16 * c)
        own = by_i(own_ref, 16 * c)
        near = packet_ref[NEAR + 4 * c : NEAR + 4 * c + 4, :]
        if ahead:
            before, after = beside(wind[3], own[3]), near
        else:
            before, after = near, beside(wind[0], own[0])
        west = shared(mass_before, before, mass[0], wind[0])
        east = shared(mass[3], wind[3], mass_after, after)
        winds.append(jnp.concatenate([west, wind[1], wind[2], east], axis=0))
        edge_winds.append(west if ahead else east)
    ones = jnp.ones((8, lanes_all), f32)
    along, across = table(winds, jnp.concatenate([share_west, ones, share_east], axis=0))
    for b in range(4):
        for a in range(4):
            weights_ref[4 * b + a] = along[a] * across[b]
    at = 0 if ahead else cap - 1

    def spread(rows):
        out = jnp.zeros((1, lanes_all), f32)
        for j in range(4):
            out = jnp.where(place == j, pltpu.roll(rows[j : j + 1], (j - at) % lanes_all, 1), out)
        return out

    edge_share = spread(1.0 - (share_west if ahead else share_east))
    node = jnp.where(place < 2, jnp.where(place == 0, *gll_points[:2]), jnp.where(place == 2, *gll_points[2:]))
    extra_along = basis(gll_points[3 if ahead else 0] - courant * spread(edge_winds[0]))
    extra_across = [factor * edge_share for factor in basis(node - courant * spread(edge_winds[1]))]
    for b in range(4):
        for a in range(4):
            extra_ref[4 * b + a, 0:1] = extra_along[a] * extra_across[b]

    source = packet_ref[SOURCE : SOURCE + 1, :].astype(jnp.int32)
    own_source = jnp.where(lane == (cap - 1 if ahead else 0), own_ref[SOURCE : SOURCE + 1, :], 0.0)
    own_source = jnp.sum(own_source, axis=1, keepdims=True).astype(jnp.int32) + (elements if ahead else -elements)
    own_source = jnp.where(own_source >= total, own_source - total, own_source)
    own_source = jnp.where(own_source < 0, own_source + total, own_source)
    row = lax.broadcasted_iota(jnp.int32, (levels * elements, lanes_all), 0)
    same = row // elements == level
    first = jnp.where(same & (row % elements == source), 1.0, 0.0).astype(bf16)
    second = jnp.where(same & (place < 4) & (row % elements == own_source), 1.0, 0.0).astype(bf16)
    chosen_ref[...] = jnp.concatenate([first, second], axis=1)


def remote(ahead, first_ref, rest_ref, weights_ref, extra_ref, chosen_ref, out_ref, blocks_ref, edge_ref):
    lanes_all = out_ref.shape[1]
    levels = 1 + rest_ref.shape[2] // lanes_all
    cap = lanes_all // levels
    tracers = first_ref.shape[1]
    lane = lax.broadcasted_iota(jnp.int32, (1, lanes_all), 1)
    place = lane % cap
    edge = place == (0 if ahead else cap - 1)
    chosen = chosen_ref[...]
    lanes = slice(0, lanes_all)
    half = tracers // 2

    def fetch(n):
        rows = slice(n * half, (n + 1) * half)
        for m in range(0, 16, 8):
            near = jnp.concatenate([first_ref[m : m + 8, rows, :], rest_ref[m : m + 8, rows, lanes]], axis=2)
            far = rest_ref[m : m + 8, rows, lanes_all:]
            y = jnp.dot(
                near.reshape(8 * half, 2 * lanes_all), chosen[: 2 * lanes_all], preferred_element_type=f32
            ) + jnp.dot(
                far.reshape(8 * half, (levels - 2) * lanes_all), chosen[2 * lanes_all :], preferred_element_type=f32
            )
            blocks_ref[n, m : m + 8] = y.reshape(8, half, 2 * lanes_all)

    fetch(0)
    for n in range(2):
        if n == 0:
            fetch(1)
        (own,) = interpolate(extra_ref, lambda m: blocks_ref[n, m, :, lanes_all:], (0,))
        for j in range(4):
            ends = interpolate(weights_ref, lambda m: blocks_ref[n, m, :, lanes], (j, 12 + j))
            middle = interpolate(weights_ref, lambda m: blocks_ref[n, m, :, lanes], (4 + j, 8 + j))
            own_here = pltpu.roll(own, ((0 if ahead else cap - 1) - j) % lanes_all, 1)
            if ahead:
                west = ends[0] + jnp.where(edge, own_here, pltpu.roll(ends[1], 1, 1))
                values, far = (west, *middle), ends[1]
            else:
                east = ends[1] + jnp.where(edge, own_here, pltpu.roll(ends[0], lanes_all - 1, 1))
                values, far = (*middle, east), ends[0]
            for i, value in enumerate(values):
                row = (3 * j + i) * tracers + n * half
                out_ref[row : row + half, :] = value.astype(bf16)
            row = j * tracers + n * half
            edge_ref[row : row + half, :] = far.astype(bf16)
    row = lax.broadcasted_iota(jnp.int32, (8, lanes_all), 0)
    far_place = cap - 1 if ahead else 0
    pick = jnp.where(lane == row * cap + far_place, 1.0, 0.0).astype(bf16)
    far = lax.dot_general(pick, edge_ref[...], (((1,), (1,)), ((), ())), preferred_element_type=f32)
    far = [far[:, n : n + lanes_all] for n in range(0, 4 * tracers, lanes_all)]
    out_ref[12 * tracers :, :] = jnp.concatenate(far, axis=0).astype(bf16)


def local_kernel(
    velocity_ref, mass_ref, source_ref, first_ref, rest_ref, after_ref,
    out_ref, ends_ref, sides_ref,
    blocks_ref, weights_ref, wind_ref, moved_ref, inner_ref, sems,
):
    del after_ref
    _, _, levels, elements = velocity_ref.shape
    cap = elements // levels
    columns = out_ref.shape[2]
    tracers = columns // 16
    start = lax.axis_index("elem") * elements
    lane = lax.broadcasted_iota(jnp.int32, (1, elements), 1)
    mass = by_i(mass_ref, 0)
    mass_before = pltpu.roll(mass[3], 1, 1)
    mass_after = pltpu.roll(mass[0], elements - 1, 1)
    share_west = mass[0] / (mass_before + mass[0])
    share_east = mass[3] / (mass[3] + mass_after)
    coefficient = jnp.concatenate([share_west, jnp.ones((8, elements), f32), share_east], axis=0)
    row = lax.broadcasted_iota(jnp.int32, (elements, elements), 0)
    chosen = jnp.where(row == source_ref[...] - start, 1.0, 0.0).astype(bf16)

    def fetch(k):
        x = rest_ref[:, :, (k - 1) * elements : k * elements] if k else first_ref[...]
        y = jnp.dot(x.reshape(columns, elements), chosen, preferred_element_type=f32)
        blocks_ref[k % 2] = y.reshape(16, tracers, elements)

    fetch(0)
    for k in range(levels):
        winds = []
        for c in range(2):
            wind_ref[c] = velocity_ref[c, :, k, :]
            wind = [wind_ref[c, pl.ds(i, 4, stride=4), :] for i in range(4)]
            west = shared(mass_before, pltpu.roll(wind[3], 1, 1), mass[0], wind[0])
            east = shared(mass[3], wind[3], mass_after, pltpu.roll(wind[0], elements - 1, 1))
            winds.append(jnp.concatenate([west, wind[1], wind[2], east], axis=0))
        along, across = table(winds, coefficient)
        for b in range(4):
            for a in range(4):
                weights_ref[k % 2, 4 * b + a] = along[a] * across[b]
        if k + 1 < levels:
            fetch(k + 1)
        lanes = slice(k * elements, (k + 1) * elements)
        table_ref = weights_ref.at[k % 2]
        for j in range(4):
            ends = interpolate(table_ref, lambda m: blocks_ref[k % 2, m], (j, 12 + j))
            middle = interpolate(table_ref, lambda m: blocks_ref[k % 2, m], (4 + j, 8 + j))
            west = jnp.where(lane == 0, 0.0, ends[0] + pltpu.roll(ends[1], 1, 1))
            east = pltpu.roll(west, elements - 1, 1)
            for i, value in enumerate((west, *middle, east)):
                node = 4 * j + i
                moved_ref[node * tracers : (node + 1) * tracers, lanes] = value.astype(bf16)
    inner = elements - 2 * cap
    row = lax.broadcasted_iota(jnp.int32, (inner * levels, elements * levels), 0)
    column = lax.broadcasted_iota(jnp.int32, (inner * levels, elements * levels), 1)
    same = (row // levels + cap == column % elements) & (row % levels == column // elements)
    order = jnp.where(same, 1.0, 0.0).astype(bf16)
    step = columns // 4
    stores = []
    for n in range(4):
        part = pl.ds(n * step, step)
        y = lax.dot_general(
            order, moved_ref[part, :], (((1,), (1,)), ((), ())), preferred_element_type=f32
        )
        inner_ref[:, :, part] = y.reshape(inner, levels, step).astype(bf16)
        stores.append(pltpu.make_async_copy(
            inner_ref.at[pl.ds(1, inner - 2), :, part], out_ref.at[pl.ds(cap + 1, inner - 2), :, part], sems.at[n]
        ))
        stores[n].start()
    sides_ref[0] = inner_ref[0]
    sides_ref[1] = inner_ref[inner - 1]
    for n, low in enumerate((0, elements - cap)):
        ends_ref[n] = jnp.concatenate(
            [moved_ref[:, k * elements + low : k * elements + low + cap] for k in range(levels)], axis=1
        )
    for store in stores:
        store.wait()


def combine_kernel(pair, part_ref, ends_ref, sides_ref, received_ref, sent_ref, out_ref, rows_ref, sems):
    del part_ref
    refs = (ends_ref, sides_ref, received_ref, sent_ref, out_ref, rows_ref, sems)
    even = is_even()
    head = jnp.logical_not(even) if pair else even
    pl.when(head)(lambda: combine(True, *refs))
    pl.when(jnp.logical_not(head))(lambda: combine(False, *refs))


def combine(head, ends_ref, sides_ref, received_ref, sent_ref, out_ref, rows_ref, sems):
    elements, levels, columns = out_ref.shape
    lanes_all = received_ref.shape[1]
    cap = elements // levels
    tracers = columns // 16
    end = 0 if head else 1
    place = lax.broadcasted_iota(jnp.int32, (1, lanes_all), 1) % cap
    order = interleave(levels, cap)
    span = 4 * tracers
    spot = pl.ds(0, cap + 1) if head else pl.ds(elements - cap - 1, cap + 1)

    def rows(ref, block):
        return ref[block * tracers : (block + 1) * tracers, :].astype(f32)

    stores = []
    for j in range(4):
        got = [rows(received_ref, 3 * j + i) for i in range(3)]
        if head:
            own = pltpu.roll(rows(sent_ref, 3 * j + 2), lanes_all - (cap - 1), 1)
            west = got[0] + jnp.where(place == 0, own, 0.0)
            east = jnp.where(place == cap - 1, 0.0, pltpu.roll(got[0], lanes_all - 1, 1))
            got = [west, got[1], got[2], east]
        else:
            own = pltpu.roll(rows(sent_ref, 3 * j), cap - 1, 1)
            east = got[2] + jnp.where(place == cap - 1, own, 0.0)
            west = jnp.where(place == 0, 0.0, pltpu.roll(got[2], 1, 1))
            got = [west, got[0], got[1], east]
        pieces = []
        for i, value in enumerate(got):
            node = 4 * j + i
            here = ends_ref[end, node * tracers : (node + 1) * tracers, :].astype(f32)
            pieces.append((here + value).astype(bf16))
        y = lax.dot_general(
            order, jnp.concatenate(pieces, axis=0), (((1,), (1,)), ((), ())), preferred_element_type=f32
        ).reshape(cap, levels, span)
        first = 12 * tracers + 8 * (j * tracers // lanes_all)
        low = j * tracers % lanes_all
        far = received_ref[first : first + 8, low : low + tracers].astype(f32)[:levels]
        zeros = jnp.zeros((levels, span - tracers), f32)
        west = jnp.concatenate([far, zeros], axis=1)
        east = jnp.concatenate([zeros, far], axis=1)
        part = slice(j * span, (j + 1) * span)
        if head:
            rows_ref[0 : cap - 1, :, part] = y[: cap - 1].astype(bf16)
            rows_ref[cap - 1, :, part] = (y[cap - 1] + east).astype(bf16)
            rows_ref[cap, :, part] = (sides_ref[0, :, part].astype(f32) + west).astype(bf16)
        else:
            rows_ref[2:, :, part] = y[1:].astype(bf16)
            rows_ref[1, :, part] = (y[0] + west).astype(bf16)
            rows_ref[0, :, part] = (sides_ref[1, :, part].astype(f32) + east).astype(bf16)
        part = pl.ds(j * span, span)
        stores.append(pltpu.make_async_copy(rows_ref.at[:, :, part], out_ref.at[spot, :, part], sems.at[j]))
        stores[j].start()
    for store in stores:
        store.wait()


def on_device(tracers, velocity, node_mass, source):
    elements, levels, columns = tracers.shape
    cap = elements // 4
    assert cap * levels == elements
    count = columns // 16
    lanes = levels * elements
    runs = lax.axis_size("elem")
    pairing = [(i, i ^ 1) for i in range(runs)]
    crossing = [(i, (i - 1 if i % 2 == 0 else i + 1) % runs) for i in range(runs)]
    shape = jax.ShapeDtypeStruct
    vmem = pl.BlockSpec(memory_space=pltpu.VMEM)
    anywhere = pl.BlockSpec(memory_space=pl.ANY)
    source = source.reshape(1, elements)

    packet = shape((PACKET, elements), f32)
    inputs = (tracers, velocity, node_mass, source)
    lowest, cross_sent, pair_sent, tracers, velocity, node_mass, source = pl.pallas_call(
        prepare_kernel,
        out_shape=(shape((columns, elements), bf16), packet, packet)
        + tuple(shape(x.shape, x.dtype) for x in inputs),
        in_specs=[anywhere] * 4,
        scratch_shapes=[pltpu.SemaphoreType.DMA((5,))],
        compiler_params=params(),
        name="prepare",
    )(*[pltpu.with_memory_space_constraint(x, pltpu.HBM) for x in inputs])
    blocks = lax.axis_size("lev")
    above = lax.ppermute(lowest, "lev", [(i, (i + 1) % blocks) for i in range(blocks)])
    spread_out = (shape((columns, elements), bf16), shape((16, count, lanes - elements), bf16))
    spread_scratch = [pltpu.VMEM((columns, lanes), bf16)]
    *early, pair_sent = pl.pallas_call(
        spread_early_kernel,
        out_shape=spread_out + (packet,),
        scratch_shapes=spread_scratch,
        compiler_params=params(),
        name="spread_early",
    )(tracers, velocity, pair_sent)
    pair_packet = lax.ppermute(pair_sent, "elem", pairing)
    cross_packet = lax.ppermute(cross_sent, "elem", crossing)
    def weighed(pair, packet, own, after):
        return pl.pallas_call(
            functools.partial(weigh_kernel, pair, levels),
            out_shape=(
                shape((16, 16, elements), f32),
                shape((16, 8, elements), f32),
                shape((lanes, 2 * elements), bf16),
            ),
            in_specs=[anywhere, vmem, vmem],
            compiler_params=params(),
            name="weigh_pair" if pair else "weigh_cross",
        )(after, packet, own)

    pair_weights = weighed(True, pair_packet, pair_sent, lowest)
    top, rest = pl.pallas_call(
        spread_kernel,
        out_shape=spread_out,
        scratch_shapes=spread_scratch,
        compiler_params=params(),
        name="spread",
    )(tracers, velocity, *early)
    first = pl.pallas_call(
        lift_first_kernel,
        out_shape=shape((16, count, elements), bf16),
        in_specs=[anywhere] + [vmem] * 3,
        compiler_params=params(),
        name="lift_first",
    )(pair_weights[1], top, above, velocity)

    far_rows = 8 * (4 * count // elements)

    message = shape((12 * count + far_rows, elements), bf16)
    message_scratch = [pltpu.VMEM((2, 16, count // 2, 2 * elements), f32), pltpu.VMEM((4 * count, elements), bf16)]
    pair_out = pl.pallas_call(
        functools.partial(remote_kernel, True),
        out_shape=message,
        in_specs=[anywhere] + [vmem] * 5,
        scratch_shapes=message_scratch,
        compiler_params=params(),
        name="remote_pair",
    )(first, first, rest, *pair_weights)
    pair_in = lax.ppermute(pair_out, "elem", pairing)
    cross_out = pl.pallas_call(
        functools.partial(weigh_remote_kernel, False, levels),
        out_shape=message,
        in_specs=[anywhere] + [vmem] * 4,
        scratch_shapes=message_scratch + [
            pltpu.VMEM((16, 16, elements), f32),
            pltpu.VMEM((16, 8, elements), f32),
            pltpu.VMEM((lanes, 2 * elements), bf16),
        ],
        compiler_params=params(),
        name="remote_cross",
    )(pair_out, cross_packet, cross_sent, first, rest)
    cross_in = lax.ppermute(cross_out, "elem", crossing)
    result = shape((elements, levels, columns), bf16)
    part, ends, sides = pl.pallas_call(
        local_kernel,
        out_shape=(result, shape((2, columns, elements), bf16), shape((2, levels, columns), bf16)),
        in_specs=[vmem] * 5 + [anywhere],
        out_specs=(anywhere, vmem, vmem),
        scratch_shapes=[
            pltpu.VMEM((2, 16, count, elements), f32),
            pltpu.VMEM((2, 16, 16, elements), f32),
            pltpu.VMEM((2, 16, elements), f32),
            pltpu.VMEM((columns, lanes), bf16),
            pltpu.VMEM((elements - 2 * cap, levels, columns), bf16),
            pltpu.SemaphoreType.DMA((4,)),
        ],
        compiler_params=params(),
        cost_estimate=cost(10**9),
        name="local",
    )(velocity, node_mass, source, first, rest, cross_out)
    for pair, received, sent in ((True, pair_in, pair_out), (False, cross_in, cross_out)):
        part = pl.pallas_call(
            functools.partial(combine_kernel, pair),
            out_shape=result,
            in_specs=[anywhere, vmem, vmem, vmem, vmem],
            out_specs=anywhere,
            scratch_shapes=[pltpu.VMEM((cap + 1, levels, columns), bf16), pltpu.SemaphoreType.DMA((4,))],
            input_output_aliases={0: 0},
            compiler_params=params(),
            name="combine_pair" if pair else "combine_cross",
        )(part, ends, sides, received, sent)
    return part


def solution(mesh):
    placed = (P("elem", "lev", None), P(None, None, "lev", "elem"), P(None, "elem"), P("elem"))
    return jax.shard_map(
        on_device, mesh=mesh, in_specs=placed, out_specs=P("elem", "lev", None), check_vma=False
    )
```

```python
import functools

import jax
import jax.numpy as jnp
from jax import lax
from jax.experimental import pallas as pl
from jax.experimental.pallas import tpu as pltpu
from jax.sharding import PartitionSpec as P

gll_points = (-1.0, -0.4472135954999579, 0.4472135954999579, 1.0)
courant = 0.15
f32 = jnp.float32
bf16 = jnp.bfloat16
VMEM_LIMIT = 40 << 20

MASS, NEAR, NEAR_MASS, SOURCE, PACKET = 32, 48, 56, 60, 64


def params():
    return pltpu.CompilerParams(vmem_limit_bytes=VMEM_LIMIT)


def cost(work):
    return pl.CostEstimate(flops=100 * work, bytes_accessed=work, transcendentals=0)


def interleave(groups, members):
    size = groups * members
    row = lax.broadcasted_iota(jnp.int32, (size, size), 0)
    column = lax.broadcasted_iota(jnp.int32, (size, size), 1)
    same = (row // groups == column % members) & (row % groups == column // members)
    return jnp.where(same, 1.0, 0.0).astype(bf16)


def basis(position):
    out = []
    for a in range(4):
        scale = 1.0
        factor = None
        for other in range(4):
            if other != a:
                scale /= gll_points[a] - gll_points[other]
                term = position - gll_points[other]
                factor = term if factor is None else factor * term
        out.append(factor * scale)
    return out


def node_rows(rows, lanes, of_i):
    row = lax.broadcasted_iota(jnp.int32, (rows, lanes), 0)
    index = row // 4 if of_i else row % 4
    out = jnp.full((rows, lanes), gll_points[0], f32)
    for a in range(1, 4):
        out = jnp.where(index == a, gll_points[a], out)
    return out


def table(winds, coefficient):
    rows, lanes = winds[0].shape
    along = basis(node_rows(rows, lanes, True) - courant * winds[0])
    across_position = node_rows(rows, lanes, False) - courant * winds[1]
    across = [factor * coefficient for factor in basis(across_position)]
    return along, across


def is_even():
    return lax.axis_index("elem") % 2 == 0


def prepare_kernel(
    tracers_hbm, velocity_hbm, mass_hbm, source_hbm,
    lowest_ref, cross_ref, pair_ref, tracers_ref, velocity_ref, mass_ref, source_ref, pair_of_levels_ref, sems,
):
    elements, levels, columns = tracers_hbm.shape
    step = 256
    copies = [
        pltpu.make_async_copy(here, there, sems.at[n])
        for n, (here, there) in enumerate(
            ((velocity_hbm, velocity_ref), (mass_hbm, mass_ref), (source_hbm, source_ref))
        )
    ]
    copies.append(pltpu.make_async_copy(tracers_hbm.at[:, pl.ds(levels - 2, 2), :], pair_of_levels_ref, sems.at[3]))
    copies.append(pltpu.make_async_copy(tracers_hbm, tracers_ref, sems.at[4]))
    for copy in copies:
        copy.start()
    for copy in copies[:3]:
        copy.wait()
    even = is_even()
    refs = (velocity_ref, mass_ref, source_ref)

    def both(head_ref, tail_ref):
        pack(True, *refs, head_ref)
        pack(False, *refs, tail_ref)

    pl.when(even)(lambda: both(cross_ref, pair_ref))
    pl.when(jnp.logical_not(even))(lambda: both(pair_ref, cross_ref))
    copies[3].wait()
    row = lax.broadcasted_iota(jnp.int32, (2 * elements, elements), 0)
    column = lax.broadcasted_iota(jnp.int32, (2 * elements, elements), 1)
    pick = jnp.where(row == column * 2 + 1, 1.0, 0.0).astype(bf16)
    x = pair_of_levels_ref[...].reshape(2 * elements, columns)
    for c in range(0, columns, step):
        lowest_ref[c : c + step, :] = lax.dot_general(
            x[:, c : c + step], pick, (((0,), (0,)), ((), ())), preferred_element_type=f32
        ).astype(bf16)
    copies[4].wait()


def pack(head, velocity_ref, mass_ref, source_ref, out_ref):
    _, _, levels, elements = velocity_ref.shape
    cap = elements // levels
    runs = lax.axis_size("elem")
    start = lax.axis_index("elem") * elements
    total = runs * elements
    low, nodes, step = (0, 0, 1) if head else (elements - cap, 3, -1)

    def lanes(pieces, shift=0):
        return jnp.concatenate([x[:, low + shift : low + shift + cap] for x in pieces], axis=1)

    for c in range(2):
        pieces = [velocity_ref[c, :, k, :] for k in range(levels)]
        out_ref[16 * c : 16 * c + 16, :] = lanes(pieces)
        near = lanes(pieces, step)
        for j in range(4):
            out_ref[NEAR + 4 * c + j : NEAR + 4 * c + j + 1, :] = near[4 * j + nodes : 4 * j + nodes + 1]
    mass = mass_ref[...]
    out_ref[MASS : MASS + 16, :] = lanes([mass] * levels)
    near = lanes([mass] * levels, step)
    for j in range(4):
        out_ref[NEAR_MASS + j : NEAR_MASS + j + 1, :] = near[4 * j + nodes : 4 * j + nodes + 1]
    relative = source_ref[...] - start + step * elements
    relative = jnp.where(relative < 0, relative + total, relative)
    relative = jnp.where(relative < 0, relative + total, relative)
    relative = jnp.where(relative >= total, relative - total, relative)
    out_ref[SOURCE : SOURCE + 1, :] = lanes([relative.astype(f32)] * levels)
    out_ref[SOURCE + 1 :, :] = jnp.zeros((PACKET - SOURCE - 1, elements), f32)


def lift(here, upper, descent):
    return ((1.0 - descent) * here.astype(f32) + descent * upper.astype(f32)).astype(bf16)


def descents(velocity_ref, k):
    return 1.0 / (1.0 + jnp.exp(-velocity_ref[2, :, k, :]))


def spread(tracers_ref, velocity_ref, top_ref, rest_ref, here_ref):
    elements, levels, columns = tracers_ref.shape
    nodes = velocity_ref.shape[1]
    tracers = columns // nodes
    order = interleave(levels, elements)
    x = tracers_ref[...].reshape(elements * levels, columns)
    step = 256
    for n in range(0, columns, step):
        here_ref[n : n + step, :] = lax.dot_general(
            x[:, n : n + step], order, (((0,), (0,)), ((), ())), preferred_element_type=f32
        ).astype(bf16)
    top_ref[...] = here_ref[:, :elements]
    for k in range(1, levels):
        descent = descents(velocity_ref, k)
        for m in range(nodes):
            rows = slice(m * tracers, (m + 1) * tracers)
            here = here_ref[rows, k * elements : (k + 1) * elements]
            upper = here_ref[rows, (k - 1) * elements : k * elements]
            rest_ref[m, :, (k - 1) * elements : k * elements] = lift(here, upper, descent[m : m + 1])


def spread_early_kernel(tracers_ref, velocity_ref, packet_ref, top_ref, rest_ref, sent_ref, here_ref):
    sent_ref[...] = packet_ref[...]
    pl.when(lax.axis_index("elem") == 0)(lambda: spread(tracers_ref, velocity_ref, top_ref, rest_ref, here_ref))


def spread_kernel(tracers_ref, velocity_ref, early_top_ref, early_rest_ref, top_ref, rest_ref, here_ref):
    early = lax.axis_index("elem") == 0

    @pl.when(early)
    def _():
        top_ref[...] = early_top_ref[...]
        rest_ref[...] = early_rest_ref[...]

    pl.when(jnp.logical_not(early))(lambda: spread(tracers_ref, velocity_ref, top_ref, rest_ref, here_ref))


def lift_first_kernel(after_ref, top_ref, above_ref, velocity_ref, out_ref):
    del after_ref
    _, nodes, _, elements = velocity_ref.shape
    tracers = above_ref.shape[0] // nodes
    descent = descents(velocity_ref, 0)
    below_top = lax.axis_index("lev") > 0
    for m in range(nodes):
        rows = slice(m * tracers, (m + 1) * tracers)
        upper = jnp.where(below_top, above_ref[rows, :].astype(f32), 0.0)
        out_ref[m] = lift(top_ref[rows, :], upper, descent[m : m + 1])


def by_i(ref, first, nodes=16):
    return [ref[pl.ds(first + i, 4, stride=4), :] for i in range(4)]


def shared(mass_left, left, mass_right, right):
    return (mass_left * left + mass_right * right) / (mass_left + mass_right)


def interpolate(weights_ref, blocks, nodes):
    totals = [None] * len(nodes)
    for m in range(16):
        block = blocks(m)
        for n, node in enumerate(nodes):
            term = weights_ref[m, node : node + 1, :] * block
            totals[n] = term if totals[n] is None else totals[n] + term
    return totals


def by_side(pair, body, *args):
    even = is_even()
    ahead = even if pair else jnp.logical_not(even)
    pl.when(ahead)(lambda: body(True, *args))
    pl.when(jnp.logical_not(ahead))(lambda: body(False, *args))


def weigh_kernel(pair, levels, after_ref, packet_ref, own_ref, weights_ref, extra_ref, chosen_ref):
    del after_ref
    by_side(pair, weigh, levels, packet_ref, own_ref, weights_ref, extra_ref, chosen_ref)


def remote_kernel(pair, after_ref, *refs):
    del after_ref
    by_side(pair, remote, *refs)


def weigh_remote_kernel(
    pair, levels, after_ref, packet_ref, own_ref, first_ref, rest_ref,
    out_ref, blocks_ref, edge_ref, weights_ref, extra_ref, chosen_ref,
):
    del after_ref
    tables = (weights_ref, extra_ref, chosen_ref)

    def both(ahead):
        weigh(ahead, levels, packet_ref, own_ref, *tables)
        remote(ahead, first_ref, rest_ref, *tables, out_ref, blocks_ref, edge_ref)

    by_side(pair, both)


def weigh(ahead, levels, packet_ref, own_ref, weights_ref, extra_ref, chosen_ref):
    lanes_all = packet_ref.shape[1]
    elements = lanes_all
    cap = elements // levels
    total = lax.axis_size("elem") * elements
    lane = lax.broadcasted_iota(jnp.int32, (1, lanes_all), 1)
    level, place = lane // cap, lane % cap
    edge = place == (0 if ahead else cap - 1)

    def beside(values, own):
        if ahead:
            return jnp.where(edge, pltpu.roll(own, lanes_all - (cap - 1), 1), pltpu.roll(values, 1, 1))
        return jnp.where(edge, pltpu.roll(own, cap - 1, 1), pltpu.roll(values, lanes_all - 1, 1))

    mass = by_i(packet_ref, MASS)
    own_mass = by_i(own_ref, MASS)
    near_mass = packet_ref[NEAR_MASS : NEAR_MASS + 4, :]
    if ahead:
        mass_before, mass_after = beside(mass[3], own_mass[3]), near_mass
    else:
        mass_before, mass_after = near_mass, beside(mass[0], own_mass[0])
    share_west = mass[0] / (mass_before + mass[0])
    share_east = mass[3] / (mass[3] + mass_after)
    winds = []
    edge_winds = []
    for c in range(2):
        wind = by_i(packet_ref, 16 * c)
        own = by_i(own_ref, 16 * c)
        near = packet_ref[NEAR + 4 * c : NEAR + 4 * c + 4, :]
        if ahead:
            before, after = beside(wind[3], own[3]), near
        else:
            before, after = near, beside(wind[0], own[0])
        west = shared(mass_before, before, mass[0], wind[0])
        east = shared(mass[3], wind[3], mass_after, after)
        winds.append(jnp.concatenate([west, wind[1], wind[2], east], axis=0))
        edge_winds.append(west if ahead else east)
    ones = jnp.ones((8, lanes_all), f32)
    along, across = table(winds, jnp.concatenate([share_west, ones, share_east], axis=0))
    for b in range(4):
        for a in range(4):
            weights_ref[4 * b + a] = along[a] * across[b]
    at = 0 if ahead else cap - 1

    def spread(rows):
        out = jnp.zeros((1, lanes_all), f32)
        for j in range(4):
            out = jnp.where(place == j, pltpu.roll(rows[j : j + 1], (j - at) % lanes_all, 1), out)
        return out

    edge_share = spread(1.0 - (share_west if ahead else share_east))
    node = jnp.where(place < 2, jnp.where(place == 0, *gll_points[:2]), jnp.where(place == 2, *gll_points[2:]))
    extra_along = basis(gll_points[3 if ahead else 0] - courant * spread(edge_winds[0]))
    extra_across = [factor * edge_share for factor in basis(node - courant * spread(edge_winds[1]))]
    for b in range(4):
        for a in range(4):
            extra_ref[4 * b + a, 0:1] = extra_along[a] * extra_across[b]

    source = packet_ref[SOURCE : SOURCE + 1, :].astype(jnp.int32)
    own_source = jnp.where(lane == (cap - 1 if ahead else 0), own_ref[SOURCE : SOURCE + 1, :], 0.0)
    own_source = jnp.sum(own_source, axis=1, keepdims=True).astype(jnp.int32) + (elements if ahead else -elements)
    own_source = jnp.where(own_source >= total, own_source - total, own_source)
    own_source = jnp.where(own_source < 0, own_source + total, own_source)
    row = lax.broadcasted_iota(jnp.int32, (levels * elements, lanes_all), 0)
    same = row // elements == level
    first = jnp.where(same & (row % elements == source), 1.0, 0.0).astype(bf16)
    second = jnp.where(same & (place < 4) & (row % elements == own_source), 1.0, 0.0).astype(bf16)
    chosen_ref[...] = jnp.concatenate([first, second], axis=1)


def remote(ahead, first_ref, rest_ref, weights_ref, extra_ref, chosen_ref, out_ref, blocks_ref, edge_ref):
    lanes_all = out_ref.shape[1]
    levels = 1 + rest_ref.shape[2] // lanes_all
    cap = lanes_all // levels
    tracers = first_ref.shape[1]
    lane = lax.broadcasted_iota(jnp.int32, (1, lanes_all), 1)
    place = lane % cap
    edge = place == (0 if ahead else cap - 1)
    chosen = chosen_ref[...]
    lanes = slice(0, lanes_all)
    half = tracers // 2

    def fetch(n):
        rows = slice(n * half, (n + 1) * half)
        for m in range(0, 16, 8):
            near = jnp.concatenate([first_ref[m : m + 8, rows, :], rest_ref[m : m + 8, rows, lanes]], axis=2)
            far = rest_ref[m : m + 8, rows, lanes_all:]
            y = jnp.dot(
                near.reshape(8 * half, 2 * lanes_all), chosen[: 2 * lanes_all], preferred_element_type=f32
            ) + jnp.dot(
                far.reshape(8 * half, (levels - 2) * lanes_all), chosen[2 * lanes_all :], preferred_element_type=f32
            )
            blocks_ref[n, m : m + 8] = y.reshape(8, half, 2 * lanes_all)

    fetch(0)
    for n in range(2):
        if n == 0:
            fetch(1)
        (own,) = interpolate(extra_ref, lambda m: blocks_ref[n, m, :, lanes_all:], (0,))
        for j in range(4):
            ends = interpolate(weights_ref, lambda m: blocks_ref[n, m, :, lanes], (j, 12 + j))
            middle = interpolate(weights_ref, lambda m: blocks_ref[n, m, :, lanes], (4 + j, 8 + j))
            own_here = pltpu.roll(own, ((0 if ahead else cap - 1) - j) % lanes_all, 1)
            if ahead:
                west = ends[0] + jnp.where(edge, own_here, pltpu.roll(ends[1], 1, 1))
                values, far = (west, *middle), ends[1]
            else:
                east = ends[1] + jnp.where(edge, own_here, pltpu.roll(ends[0], lanes_all - 1, 1))
                values, far = (*middle, east), ends[0]
            for i, value in enumerate(values):
                row = (3 * j + i) * tracers + n * half
                out_ref[row : row + half, :] = value.astype(bf16)
            row = j * tracers + n * half
            edge_ref[row : row + half, :] = far.astype(bf16)
    row = lax.broadcasted_iota(jnp.int32, (8, lanes_all), 0)
    far_place = cap - 1 if ahead else 0
    pick = jnp.where(lane == row * cap + far_place, 1.0, 0.0).astype(bf16)
    far = lax.dot_general(pick, edge_ref[...], (((1,), (1,)), ((), ())), preferred_element_type=f32)
    far = [far[:, n : n + lanes_all] for n in range(0, 4 * tracers, lanes_all)]
    out_ref[12 * tracers :, :] = jnp.concatenate(far, axis=0).astype(bf16)


def local_kernel(
    velocity_ref, mass_ref, source_ref, first_ref, rest_ref, after_ref,
    out_ref, ends_ref, sides_ref,
    blocks_ref, weights_ref, wind_ref, moved_ref, inner_ref, sems,
):
    del after_ref
    _, _, levels, elements = velocity_ref.shape
    cap = elements // levels
    columns = out_ref.shape[2]
    tracers = columns // 16
    start = lax.axis_index("elem") * elements
    lane = lax.broadcasted_iota(jnp.int32, (1, elements), 1)
    mass = by_i(mass_ref, 0)
    mass_before = pltpu.roll(mass[3], 1, 1)
    mass_after = pltpu.roll(mass[0], elements - 1, 1)
    share_west = mass[0] / (mass_before + mass[0])
    share_east = mass[3] / (mass[3] + mass_after)
    coefficient = jnp.concatenate([share_west, jnp.ones((8, elements), f32), share_east], axis=0)
    row = lax.broadcasted_iota(jnp.int32, (elements, elements), 0)
    chosen = jnp.where(row == source_ref[...] - start, 1.0, 0.0).astype(bf16)

    def fetch(k):
        x = rest_ref[:, :, (k - 1) * elements : k * elements] if k else first_ref[...]
        y = jnp.dot(x.reshape(columns, elements), chosen, preferred_element_type=f32)
        blocks_ref[k % 2] = y.reshape(16, tracers, elements)

    fetch(0)
    for k in range(levels):
        winds = []
        for c in range(2):
            wind_ref[c] = velocity_ref[c, :, k, :]
            wind = [wind_ref[c, pl.ds(i, 4, stride=4), :] for i in range(4)]
            west = shared(mass_before, pltpu.roll(wind[3], 1, 1), mass[0], wind[0])
            east = shared(mass[3], wind[3], mass_after, pltpu.roll(wind[0], elements - 1, 1))
            winds.append(jnp.concatenate([west, wind[1], wind[2], east], axis=0))
        along, across = table(winds, coefficient)
        for b in range(4):
            for a in range(4):
                weights_ref[k % 2, 4 * b + a] = along[a] * across[b]
        if k + 1 < levels:
            fetch(k + 1)
        lanes = slice(k * elements, (k + 1) * elements)
        table_ref = weights_ref.at[k % 2]
        for j in range(4):
            ends = interpolate(table_ref, lambda m: blocks_ref[k % 2, m], (j, 12 + j))
            middle = interpolate(table_ref, lambda m: blocks_ref[k % 2, m], (4 + j, 8 + j))
            west = jnp.where(lane == 0, 0.0, ends[0] + pltpu.roll(ends[1], 1, 1))
            east = pltpu.roll(west, elements - 1, 1)
            for i, value in enumerate((west, *middle, east)):
                node = 4 * j + i
                moved_ref[node * tracers : (node + 1) * tracers, lanes] = value.astype(bf16)
    inner = elements - 2 * cap
    row = lax.broadcasted_iota(jnp.int32, (inner * levels, elements * levels), 0)
    column = lax.broadcasted_iota(jnp.int32, (inner * levels, elements * levels), 1)
    same = (row // levels + cap == column % elements) & (row % levels == column // elements)
    order = jnp.where(same, 1.0, 0.0).astype(bf16)
    step = columns // 4
    stores = []
    for n in range(4):
        part = pl.ds(n * step, step)
        y = lax.dot_general(
            order, moved_ref[part, :], (((1,), (1,)), ((), ())), preferred_element_type=f32
        )
        inner_ref[:, :, part] = y.reshape(inner, levels, step).astype(bf16)
        stores.append(pltpu.make_async_copy(
            inner_ref.at[pl.ds(1, inner - 2), :, part], out_ref.at[pl.ds(cap + 1, inner - 2), :, part], sems.at[n]
        ))
        stores[n].start()
    sides_ref[0] = inner_ref[0]
    sides_ref[1] = inner_ref[inner - 1]
    for n, low in enumerate((0, elements - cap)):
        ends_ref[n] = jnp.concatenate(
            [moved_ref[:, k * elements + low : k * elements + low + cap] for k in range(levels)], axis=1
        )
    for store in stores:
        store.wait()


def combine_kernel(pair, part_ref, ends_ref, sides_ref, received_ref, sent_ref, out_ref, rows_ref, sems):
    del part_ref
    refs = (ends_ref, sides_ref, received_ref, sent_ref, out_ref, rows_ref, sems)
    even = is_even()
    head = jnp.logical_not(even) if pair else even
    pl.when(head)(lambda: combine(True, *refs))
    pl.when(jnp.logical_not(head))(lambda: combine(False, *refs))


def combine(head, ends_ref, sides_ref, received_ref, sent_ref, out_ref, rows_ref, sems):
    elements, levels, columns = out_ref.shape
    lanes_all = received_ref.shape[1]
    cap = elements // levels
    tracers = columns // 16
    end = 0 if head else 1
    place = lax.broadcasted_iota(jnp.int32, (1, lanes_all), 1) % cap
    order = interleave(levels, cap)
    span = 4 * tracers
    spot = pl.ds(0, cap + 1) if head else pl.ds(elements - cap - 1, cap + 1)

    def rows(ref, block):
        return ref[block * tracers : (block + 1) * tracers, :].astype(f32)

    stores = []
    for j in range(4):
        got = [rows(received_ref, 3 * j + i) for i in range(3)]
        if head:
            own = pltpu.roll(rows(sent_ref, 3 * j + 2), lanes_all - (cap - 1), 1)
            west = got[0] + jnp.where(place == 0, own, 0.0)
            east = jnp.where(place == cap - 1, 0.0, pltpu.roll(got[0], lanes_all - 1, 1))
            got = [west, got[1], got[2], east]
        else:
            own = pltpu.roll(rows(sent_ref, 3 * j), cap - 1, 1)
            east = got[2] + jnp.where(place == cap - 1, own, 0.0)
            west = jnp.where(place == 0, 0.0, pltpu.roll(got[2], 1, 1))
            got = [west, got[0], got[1], east]
        pieces = []
        for i, value in enumerate(got):
            node = 4 * j + i
            here = ends_ref[end, node * tracers : (node + 1) * tracers, :].astype(f32)
            pieces.append((here + value).astype(bf16))
        y = lax.dot_general(
            order, jnp.concatenate(pieces, axis=0), (((1,), (1,)), ((), ())), preferred_element_type=f32
        ).reshape(cap, levels, span)
        first = 12 * tracers + 8 * (j * tracers // lanes_all)
        low = j * tracers % lanes_all
        far = received_ref[first : first + 8, low : low + tracers].astype(f32)[:levels]
        zeros = jnp.zeros((levels, span - tracers), f32)
        west = jnp.concatenate([far, zeros], axis=1)
        east = jnp.concatenate([zeros, far], axis=1)
        part = slice(j * span, (j + 1) * span)
        if head:
            rows_ref[0 : cap - 1, :, part] = y[: cap - 1].astype(bf16)
            rows_ref[cap - 1, :, part] = (y[cap - 1] + east).astype(bf16)
            rows_ref[cap, :, part] = (sides_ref[0, :, part].astype(f32) + west).astype(bf16)
        else:
            rows_ref[2:, :, part] = y[1:].astype(bf16)
            rows_ref[1, :, part] = (y[0] + west).astype(bf16)
            rows_ref[0, :, part] = (sides_ref[1, :, part].astype(f32) + east).astype(bf16)
        part = pl.ds(j * span, span)
        stores.append(pltpu.make_async_copy(rows_ref.at[:, :, part], out_ref.at[spot, :, part], sems.at[j]))
        stores[j].start()
    for store in stores:
        store.wait()


def on_device(tracers, velocity, node_mass, source):
    elements, levels, columns = tracers.shape
    cap = elements // 4
    assert cap * levels == elements
    count = columns // 16
    lanes = levels * elements
    runs = lax.axis_size("elem")
    pairing = [(i, i ^ 1) for i in range(runs)]
    crossing = [(i, (i - 1 if i % 2 == 0 else i + 1) % runs) for i in range(runs)]
    shape = jax.ShapeDtypeStruct
    vmem = pl.BlockSpec(memory_space=pltpu.VMEM)
    anywhere = pl.BlockSpec(memory_space=pl.ANY)
    source = source.reshape(1, elements)

    packet = shape((PACKET, elements), f32)
    inputs = (tracers, velocity, node_mass, source)
    lowest, cross_sent, pair_sent, tracers, velocity, node_mass, source = pl.pallas_call(
        prepare_kernel,
        out_shape=(shape((columns, elements), bf16), packet, packet)
        + tuple(shape(x.shape, x.dtype) for x in inputs),
        in_specs=[anywhere] * 4,
        scratch_shapes=[pltpu.VMEM((elements, 2, columns), bf16), pltpu.SemaphoreType.DMA((5,))],
        compiler_params=params(),
        name="prepare",
    )(*[pltpu.with_memory_space_constraint(x, pltpu.HBM) for x in inputs])
    blocks = lax.axis_size("lev")
    above = lax.ppermute(lowest, "lev", [(i, (i + 1) % blocks) for i in range(blocks)])
    spread_out = (shape((columns, elements), bf16), shape((16, count, lanes - elements), bf16))
    spread_scratch = [pltpu.VMEM((columns, lanes), bf16)]
    *early, pair_sent = pl.pallas_call(
        spread_early_kernel,
        out_shape=spread_out + (packet,),
        scratch_shapes=spread_scratch,
        compiler_params=params(),
        name="spread_early",
    )(tracers, velocity, pair_sent)
    pair_packet = lax.ppermute(pair_sent, "elem", pairing)
    cross_packet = lax.ppermute(cross_sent, "elem", crossing)
    def weighed(pair, packet, own, after):
        return pl.pallas_call(
            functools.partial(weigh_kernel, pair, levels),
            out_shape=(
                shape((16, 16, elements), f32),
                shape((16, 8, elements), f32),
                shape((lanes, 2 * elements), bf16),
            ),
            in_specs=[anywhere, vmem, vmem],
            compiler_params=params(),
            name="weigh_pair" if pair else "weigh_cross",
        )(after, packet, own)

    pair_weights = weighed(True, pair_packet, pair_sent, lowest)
    top, rest = pl.pallas_call(
        spread_kernel,
        out_shape=spread_out,
        scratch_shapes=spread_scratch,
        compiler_params=params(),
        name="spread",
    )(tracers, velocity, *early)
    first = pl.pallas_call(
        lift_first_kernel,
        out_shape=shape((16, count, elements), bf16),
        in_specs=[anywhere] + [vmem] * 3,
        compiler_params=params(),
        name="lift_first",
    )(pair_weights[1], top, above, velocity)

    far_rows = 8 * (4 * count // elements)

    message = shape((12 * count + far_rows, elements), bf16)
    message_scratch = [pltpu.VMEM((2, 16, count // 2, 2 * elements), f32), pltpu.VMEM((4 * count, elements), bf16)]
    pair_out = pl.pallas_call(
        functools.partial(remote_kernel, True),
        out_shape=message,
        in_specs=[anywhere] + [vmem] * 5,
        scratch_shapes=message_scratch,
        compiler_params=params(),
        name="remote_pair",
    )(first, first, rest, *pair_weights)
    pair_in = lax.ppermute(pair_out, "elem", pairing)
    cross_out = pl.pallas_call(
        functools.partial(weigh_remote_kernel, False, levels),
        out_shape=message,
        in_specs=[anywhere] + [vmem] * 4,
        scratch_shapes=message_scratch + [
            pltpu.VMEM((16, 16, elements), f32),
            pltpu.VMEM((16, 8, elements), f32),
            pltpu.VMEM((lanes, 2 * elements), bf16),
        ],
        compiler_params=params(),
        name="remote_cross",
    )(pair_out, cross_packet, cross_sent, first, rest)
    cross_in = lax.ppermute(cross_out, "elem", crossing)
    result = shape((elements, levels, columns), bf16)
    part, ends, sides = pl.pallas_call(
        local_kernel,
        out_shape=(result, shape((2, columns, elements), bf16), shape((2, levels, columns), bf16)),
        in_specs=[vmem] * 5 + [anywhere],
        out_specs=(anywhere, vmem, vmem),
        scratch_shapes=[
            pltpu.VMEM((2, 16, count, elements), f32),
            pltpu.VMEM((2, 16, 16, elements), f32),
            pltpu.VMEM((2, 16, elements), f32),
            pltpu.VMEM((columns, lanes), bf16),
            pltpu.VMEM((elements - 2 * cap, levels, columns), bf16),
            pltpu.SemaphoreType.DMA((4,)),
        ],
        compiler_params=params(),
        cost_estimate=cost(10**9),
        name="local",
    )(velocity, node_mass, source, first, rest, cross_out)
    for pair, received, sent in ((True, pair_in, pair_out), (False, cross_in, cross_out)):
        part = pl.pallas_call(
            functools.partial(combine_kernel, pair),
            out_shape=result,
            in_specs=[anywhere, vmem, vmem, vmem, vmem],
            out_specs=anywhere,
            scratch_shapes=[pltpu.VMEM((cap + 1, levels, columns), bf16), pltpu.SemaphoreType.DMA((4,))],
            input_output_aliases={0: 0},
            compiler_params=params(),
            name="combine_pair" if pair else "combine_cross",
        )(part, ends, sides, received, sent)
    return part


def solution(mesh):
    placed = (P("elem", "lev", None), P(None, None, "lev", "elem"), P(None, "elem"), P("elem"))
    return jax.shard_map(
        on_device, mesh=mesh, in_specs=placed, out_specs=P("elem", "lev", None), check_vma=False
    )
```

```python
import functools

import jax
import jax.numpy as jnp
from jax import lax
from jax.experimental import pallas as pl
from jax.experimental.pallas import tpu as pltpu
from jax.sharding import PartitionSpec as P

gll_points = (-1.0, -0.4472135954999579, 0.4472135954999579, 1.0)
courant = 0.15
f32 = jnp.float32
bf16 = jnp.bfloat16
VMEM_LIMIT = 40 << 20

MASS, NEAR, NEAR_MASS, SOURCE, PACKET = 32, 48, 56, 60, 64


def params():
    return pltpu.CompilerParams(vmem_limit_bytes=VMEM_LIMIT)


def cost(work):
    return pl.CostEstimate(flops=100 * work, bytes_accessed=work, transcendentals=0)


def interleave(groups, members):
    size = groups * members
    row = lax.broadcasted_iota(jnp.int32, (size, size), 0)
    column = lax.broadcasted_iota(jnp.int32, (size, size), 1)
    same = (row // groups == column % members) & (row % groups == column // members)
    return jnp.where(same, 1.0, 0.0).astype(bf16)


def basis(position):
    out = []
    for a in range(4):
        scale = 1.0
        factor = None
        for other in range(4):
            if other != a:
                scale /= gll_points[a] - gll_points[other]
                term = position - gll_points[other]
                factor = term if factor is None else factor * term
        out.append(factor * scale)
    return out


def node_rows(rows, lanes, of_i):
    row = lax.broadcasted_iota(jnp.int32, (rows, lanes), 0)
    index = row // 4 if of_i else row % 4
    out = jnp.full((rows, lanes), gll_points[0], f32)
    for a in range(1, 4):
        out = jnp.where(index == a, gll_points[a], out)
    return out


def table(winds):
    rows, lanes = winds[0].shape
    along = basis(node_rows(rows, lanes, True) - courant * winds[0])
    across = basis(node_rows(rows, lanes, False) - courant * winds[1])
    return along, across


def weight(along, across, share):
    return (along * across).astype(bf16).astype(f32) * share


def is_even():
    return lax.axis_index("elem") % 2 == 0


def prepare_kernel(
    tracers_hbm, velocity_hbm, mass_hbm, source_hbm,
    lowest_ref, cross_ref, pair_ref, tracers_ref, velocity_ref, mass_ref, source_ref, pair_of_levels_ref, sems,
):
    elements, levels, columns = tracers_hbm.shape
    step = 256
    copies = [
        pltpu.make_async_copy(here, there, sems.at[n])
        for n, (here, there) in enumerate(
            ((velocity_hbm, velocity_ref), (mass_hbm, mass_ref), (source_hbm, source_ref))
        )
    ]
    copies.append(pltpu.make_async_copy(tracers_hbm.at[:, pl.ds(levels - 2, 2), :], pair_of_levels_ref, sems.at[3]))
    copies.append(pltpu.make_async_copy(tracers_hbm, tracers_ref, sems.at[4]))
    for copy in copies:
        copy.start()
    for copy in copies[:3]:
        copy.wait()
    even = is_even()
    refs = (velocity_ref, mass_ref, source_ref)

    def both(head_ref, tail_ref):
        pack(True, *refs, head_ref)
        pack(False, *refs, tail_ref)

    pl.when(even)(lambda: both(cross_ref, pair_ref))
    pl.when(jnp.logical_not(even))(lambda: both(pair_ref, cross_ref))
    copies[3].wait()
    row = lax.broadcasted_iota(jnp.int32, (2 * elements, elements), 0)
    column = lax.broadcasted_iota(jnp.int32, (2 * elements, elements), 1)
    pick = jnp.where(row == column * 2 + 1, 1.0, 0.0).astype(bf16)
    x = pair_of_levels_ref[...].reshape(2 * elements, columns)
    for c in range(0, columns, step):
        lowest_ref[c : c + step, :] = lax.dot_general(
            x[:, c : c + step], pick, (((0,), (0,)), ((), ())), preferred_element_type=f32
        ).astype(bf16)
    copies[4].wait()


def pack(head, velocity_ref, mass_ref, source_ref, out_ref):
    _, _, levels, elements = velocity_ref.shape
    cap = elements // levels
    runs = lax.axis_size("elem")
    start = lax.axis_index("elem") * elements
    total = runs * elements
    low, nodes, step = (0, 0, 1) if head else (elements - cap, 3, -1)

    def lanes(pieces, shift=0):
        return jnp.concatenate([x[:, low + shift : low + shift + cap] for x in pieces], axis=1)

    for c in range(2):
        pieces = [velocity_ref[c, :, k, :] for k in range(levels)]
        out_ref[16 * c : 16 * c + 16, :] = lanes(pieces)
        near = lanes(pieces, step)
        for j in range(4):
            out_ref[NEAR + 4 * c + j : NEAR + 4 * c + j + 1, :] = near[4 * j + nodes : 4 * j + nodes + 1]
    mass = mass_ref[...]
    out_ref[MASS : MASS + 16, :] = lanes([mass] * levels)
    near = lanes([mass] * levels, step)
    for j in range(4):
        out_ref[NEAR_MASS + j : NEAR_MASS + j + 1, :] = near[4 * j + nodes : 4 * j + nodes + 1]
    relative = source_ref[...] - start + step * elements
    relative = jnp.where(relative < 0, relative + total, relative)
    relative = jnp.where(relative < 0, relative + total, relative)
    relative = jnp.where(relative >= total, relative - total, relative)
    out_ref[SOURCE : SOURCE + 1, :] = lanes([relative.astype(f32)] * levels)
    out_ref[SOURCE + 1 :, :] = jnp.zeros((PACKET - SOURCE - 1, elements), f32)


def lift(here, upper, descent):
    return ((1.0 - descent) * here.astype(f32) + descent * upper.astype(f32)).astype(bf16)


def descents(velocity_ref, k):
    return 1.0 / (1.0 + jnp.exp(-velocity_ref[2, :, k, :]))


def spread(tracers_ref, velocity_ref, top_ref, rest_ref, here_ref):
    elements, levels, columns = tracers_ref.shape
    nodes = velocity_ref.shape[1]
    tracers = columns // nodes
    order = interleave(levels, elements)
    x = tracers_ref[...].reshape(elements * levels, columns)
    step = 256
    for n in range(0, columns, step):
        here_ref[n : n + step, :] = lax.dot_general(
            x[:, n : n + step], order, (((0,), (0,)), ((), ())), preferred_element_type=f32
        ).astype(bf16)
    top_ref[...] = here_ref[:, :elements]
    for k in range(1, levels):
        descent = descents(velocity_ref, k)
        for m in range(nodes):
            rows = slice(m * tracers, (m + 1) * tracers)
            here = here_ref[rows, k * elements : (k + 1) * elements]
            upper = here_ref[rows, (k - 1) * elements : k * elements]
            rest_ref[m, :, (k - 1) * elements : k * elements] = lift(here, upper, descent[m : m + 1])


def spread_early_kernel(tracers_ref, velocity_ref, packet_ref, top_ref, rest_ref, sent_ref, here_ref):
    sent_ref[...] = packet_ref[...]
    pl.when(lax.axis_index("elem") == 0)(lambda: spread(tracers_ref, velocity_ref, top_ref, rest_ref, here_ref))


def spread_kernel(tracers_ref, velocity_ref, early_top_ref, early_rest_ref, top_ref, rest_ref, here_ref):
    early = lax.axis_index("elem") == 0

    @pl.when(early)
    def _():
        top_ref[...] = early_top_ref[...]
        rest_ref[...] = early_rest_ref[...]

    pl.when(jnp.logical_not(early))(lambda: spread(tracers_ref, velocity_ref, top_ref, rest_ref, here_ref))


def lift_first_kernel(after_ref, top_ref, above_ref, velocity_ref, out_ref):
    del after_ref
    _, nodes, _, elements = velocity_ref.shape
    tracers = above_ref.shape[0] // nodes
    descent = descents(velocity_ref, 0)
    below_top = lax.axis_index("lev") > 0
    for m in range(nodes):
        rows = slice(m * tracers, (m + 1) * tracers)
        upper = jnp.where(below_top, above_ref[rows, :].astype(f32), 0.0)
        out_ref[m] = lift(top_ref[rows, :], upper, descent[m : m + 1])


def by_i(ref, first, nodes=16):
    return [ref[pl.ds(first + i, 4, stride=4), :] for i in range(4)]


def shared(mass_left, left, mass_right, right):
    return (mass_left * left + mass_right * right) / (mass_left + mass_right)


def interpolate(weights_ref, blocks, nodes):
    totals = [None] * len(nodes)
    for m in range(16):
        block = blocks(m)
        for n, node in enumerate(nodes):
            term = weights_ref[m, node : node + 1, :] * block
            totals[n] = term if totals[n] is None else totals[n] + term
    return totals


def by_side(pair, body, *args):
    even = is_even()
    ahead = even if pair else jnp.logical_not(even)
    pl.when(ahead)(lambda: body(True, *args))
    pl.when(jnp.logical_not(ahead))(lambda: body(False, *args))


def weigh_kernel(pair, levels, after_ref, packet_ref, own_ref, weights_ref, extra_ref, chosen_ref):
    del after_ref
    by_side(pair, weigh, levels, packet_ref, own_ref, weights_ref, extra_ref, chosen_ref)


def remote_kernel(pair, after_ref, *refs):
    del after_ref
    by_side(pair, remote, *refs)


def weigh_remote_kernel(
    pair, levels, after_ref, packet_ref, own_ref, first_ref, rest_ref,
    out_ref, blocks_ref, edge_ref, weights_ref, extra_ref, chosen_ref,
):
    del after_ref
    tables = (weights_ref, extra_ref, chosen_ref)

    def both(ahead):
        weigh(ahead, levels, packet_ref, own_ref, *tables)
        remote(ahead, first_ref, rest_ref, *tables, out_ref, blocks_ref, edge_ref)

    by_side(pair, both)


def weigh(ahead, levels, packet_ref, own_ref, weights_ref, extra_ref, chosen_ref):
    lanes_all = packet_ref.shape[1]
    elements = lanes_all
    cap = elements // levels
    total = lax.axis_size("elem") * elements
    lane = lax.broadcasted_iota(jnp.int32, (1, lanes_all), 1)
    level, place = lane // cap, lane % cap
    edge = place == (0 if ahead else cap - 1)

    def beside(values, own):
        if ahead:
            return jnp.where(edge, pltpu.roll(own, lanes_all - (cap - 1), 1), pltpu.roll(values, 1, 1))
        return jnp.where(edge, pltpu.roll(own, cap - 1, 1), pltpu.roll(values, lanes_all - 1, 1))

    mass = by_i(packet_ref, MASS)
    own_mass = by_i(own_ref, MASS)
    near_mass = packet_ref[NEAR_MASS : NEAR_MASS + 4, :]
    if ahead:
        mass_before, mass_after = beside(mass[3], own_mass[3]), near_mass
    else:
        mass_before, mass_after = near_mass, beside(mass[0], own_mass[0])
    share_west = mass[0] / (mass_before + mass[0])
    share_east = mass[3] / (mass[3] + mass_after)
    winds = []
    edge_winds = []
    for c in range(2):
        wind = by_i(packet_ref, 16 * c)
        own = by_i(own_ref, 16 * c)
        near = packet_ref[NEAR + 4 * c : NEAR + 4 * c + 4, :]
        if ahead:
            before, after = beside(wind[3], own[3]), near
        else:
            before, after = near, beside(wind[0], own[0])
        west = shared(mass_before, before, mass[0], wind[0])
        east = shared(mass[3], wind[3], mass_after, after)
        winds.append(jnp.concatenate([west, wind[1], wind[2], east], axis=0))
        edge_winds.append(west if ahead else east)
    ones = jnp.ones((8, lanes_all), f32)
    along, across = table(winds)
    share = jnp.concatenate([share_west, ones, share_east], axis=0)
    for b in range(4):
        for a in range(4):
            weights_ref[4 * b + a] = weight(along[a], across[b], share)
    at = 0 if ahead else cap - 1

    def spread(rows):
        out = jnp.zeros((1, lanes_all), f32)
        for j in range(4):
            out = jnp.where(place == j, pltpu.roll(rows[j : j + 1], (j - at) % lanes_all, 1), out)
        return out

    edge_share = spread(1.0 - (share_west if ahead else share_east))
    node = jnp.where(place < 2, jnp.where(place == 0, *gll_points[:2]), jnp.where(place == 2, *gll_points[2:]))
    extra_along = basis(gll_points[3 if ahead else 0] - courant * spread(edge_winds[0]))
    extra_across = basis(node - courant * spread(edge_winds[1]))
    for b in range(4):
        for a in range(4):
            extra_ref[4 * b + a, 0:1] = weight(extra_along[a], extra_across[b], edge_share)

    source = packet_ref[SOURCE : SOURCE + 1, :].astype(jnp.int32)
    own_source = jnp.where(lane == (cap - 1 if ahead else 0), own_ref[SOURCE : SOURCE + 1, :], 0.0)
    own_source = jnp.sum(own_source, axis=1, keepdims=True).astype(jnp.int32) + (elements if ahead else -elements)
    own_source = jnp.where(own_source >= total, own_source - total, own_source)
    own_source = jnp.where(own_source < 0, own_source + total, own_source)
    row = lax.broadcasted_iota(jnp.int32, (levels * elements, lanes_all), 0)
    same = row // elements == level
    first = jnp.where(same & (row % elements == source), 1.0, 0.0).astype(bf16)
    second = jnp.where(same & (place < 4) & (row % elements == own_source), 1.0, 0.0).astype(bf16)
    chosen_ref[...] = jnp.concatenate([first, second], axis=1)


def remote(ahead, first_ref, rest_ref, weights_ref, extra_ref, chosen_ref, out_ref, blocks_ref, edge_ref):
    lanes_all = out_ref.shape[1]
    levels = 1 + rest_ref.shape[2] // lanes_all
    cap = lanes_all // levels
    tracers = first_ref.shape[1]
    lane = lax.broadcasted_iota(jnp.int32, (1, lanes_all), 1)
    place = lane % cap
    edge = place == (0 if ahead else cap - 1)
    chosen = chosen_ref[...]
    lanes = slice(0, lanes_all)
    half = tracers // 2

    def fetch(n):
        rows = slice(n * half, (n + 1) * half)
        for m in range(0, 16, 8):
            near = jnp.concatenate([first_ref[m : m + 8, rows, :], rest_ref[m : m + 8, rows, lanes]], axis=2)
            far = rest_ref[m : m + 8, rows, lanes_all:]
            y = jnp.dot(
                near.reshape(8 * half, 2 * lanes_all), chosen[: 2 * lanes_all], preferred_element_type=f32
            ) + jnp.dot(
                far.reshape(8 * half, (levels - 2) * lanes_all), chosen[2 * lanes_all :], preferred_element_type=f32
            )
            blocks_ref[n, m : m + 8] = y.reshape(8, half, 2 * lanes_all)

    fetch(0)
    for n in range(2):
        if n == 0:
            fetch(1)
        (own,) = interpolate(extra_ref, lambda m: blocks_ref[n, m, :, lanes_all:], (0,))
        for j in range(4):
            ends = interpolate(weights_ref, lambda m: blocks_ref[n, m, :, lanes], (j, 12 + j))
            middle = interpolate(weights_ref, lambda m: blocks_ref[n, m, :, lanes], (4 + j, 8 + j))
            own_here = pltpu.roll(own, ((0 if ahead else cap - 1) - j) % lanes_all, 1)
            if ahead:
                west = ends[0] + jnp.where(edge, own_here, pltpu.roll(ends[1], 1, 1))
                values, far = (west, *middle), ends[1]
            else:
                east = ends[1] + jnp.where(edge, own_here, pltpu.roll(ends[0], lanes_all - 1, 1))
                values, far = (*middle, east), ends[0]
            for i, value in enumerate(values):
                row = (3 * j + i) * tracers + n * half
                out_ref[row : row + half, :] = value.astype(bf16)
            row = j * tracers + n * half
            edge_ref[row : row + half, :] = far.astype(bf16)
    row = lax.broadcasted_iota(jnp.int32, (8, lanes_all), 0)
    far_place = cap - 1 if ahead else 0
    pick = jnp.where(lane == row * cap + far_place, 1.0, 0.0).astype(bf16)
    far = lax.dot_general(pick, edge_ref[...], (((1,), (1,)), ((), ())), preferred_element_type=f32)
    far = [far[:, n : n + lanes_all] for n in range(0, 4 * tracers, lanes_all)]
    out_ref[12 * tracers :, :] = jnp.concatenate(far, axis=0).astype(bf16)


def local_kernel(
    velocity_ref, mass_ref, source_ref, first_ref, rest_ref, after_ref,
    out_ref, ends_ref, sides_ref,
    blocks_ref, weights_ref, wind_ref, moved_ref, inner_ref, sems,
):
    del after_ref
    _, _, levels, elements = velocity_ref.shape
    cap = elements // levels
    columns = out_ref.shape[2]
    tracers = columns // 16
    start = lax.axis_index("elem") * elements
    lane = lax.broadcasted_iota(jnp.int32, (1, elements), 1)
    mass = by_i(mass_ref, 0)
    mass_before = pltpu.roll(mass[3], 1, 1)
    mass_after = pltpu.roll(mass[0], elements - 1, 1)
    share_west = mass[0] / (mass_before + mass[0])
    share_east = mass[3] / (mass[3] + mass_after)
    coefficient = jnp.concatenate([share_west, jnp.ones((8, elements), f32), share_east], axis=0)
    row = lax.broadcasted_iota(jnp.int32, (elements, elements), 0)
    chosen = jnp.where(row == source_ref[...] - start, 1.0, 0.0).astype(bf16)

    def fetch(k):
        x = rest_ref[:, :, (k - 1) * elements : k * elements] if k else first_ref[...]
        y = jnp.dot(x.reshape(columns, elements), chosen, preferred_element_type=f32)
        blocks_ref[k % 2] = y.reshape(16, tracers, elements)

    fetch(0)
    for k in range(levels):
        winds = []
        for c in range(2):
            wind_ref[c] = velocity_ref[c, :, k, :]
            wind = [wind_ref[c, pl.ds(i, 4, stride=4), :] for i in range(4)]
            west = shared(mass_before, pltpu.roll(wind[3], 1, 1), mass[0], wind[0])
            east = shared(mass[3], wind[3], mass_after, pltpu.roll(wind[0], elements - 1, 1))
            winds.append(jnp.concatenate([west, wind[1], wind[2], east], axis=0))
        along, across = table(winds)
        for b in range(4):
            for a in range(4):
                weights_ref[k % 2, 4 * b + a] = weight(along[a], across[b], coefficient)
        if k + 1 < levels:
            fetch(k + 1)
        lanes = slice(k * elements, (k + 1) * elements)
        table_ref = weights_ref.at[k % 2]
        for j in range(4):
            ends = interpolate(table_ref, lambda m: blocks_ref[k % 2, m], (j, 12 + j))
            middle = interpolate(table_ref, lambda m: blocks_ref[k % 2, m], (4 + j, 8 + j))
            west = jnp.where(lane == 0, 0.0, ends[0] + pltpu.roll(ends[1], 1, 1))
            east = pltpu.roll(west, elements - 1, 1)
            for i, value in enumerate((west, *middle, east)):
                node = 4 * j + i
                moved_ref[node * tracers : (node + 1) * tracers, lanes] = value.astype(bf16)
    inner = elements - 2 * cap
    row = lax.broadcasted_iota(jnp.int32, (inner * levels, elements * levels), 0)
    column = lax.broadcasted_iota(jnp.int32, (inner * levels, elements * levels), 1)
    same = (row // levels + cap == column % elements) & (row % levels == column // elements)
    order = jnp.where(same, 1.0, 0.0).astype(bf16)
    step = columns // 4
    stores = []
    for n in range(4):
        part = pl.ds(n * step, step)
        y = lax.dot_general(
            order, moved_ref[part, :], (((1,), (1,)), ((), ())), preferred_element_type=f32
        )
        inner_ref[:, :, part] = y.reshape(inner, levels, step).astype(bf16)
        stores.append(pltpu.make_async_copy(
            inner_ref.at[pl.ds(1, inner - 2), :, part], out_ref.at[pl.ds(cap + 1, inner - 2), :, part], sems.at[n]
        ))
        stores[n].start()
    sides_ref[0] = inner_ref[0]
    sides_ref[1] = inner_ref[inner - 1]
    for n, low in enumerate((0, elements - cap)):
        ends_ref[n] = jnp.concatenate(
            [moved_ref[:, k * elements + low : k * elements + low + cap] for k in range(levels)], axis=1
        )
    for store in stores:
        store.wait()


def combine_kernel(pair, part_ref, ends_ref, sides_ref, received_ref, sent_ref, out_ref, rows_ref, sems):
    del part_ref
    refs = (ends_ref, sides_ref, received_ref, sent_ref, out_ref, rows_ref, sems)
    even = is_even()
    head = jnp.logical_not(even) if pair else even
    pl.when(head)(lambda: combine(True, *refs))
    pl.when(jnp.logical_not(head))(lambda: combine(False, *refs))


def combine(head, ends_ref, sides_ref, received_ref, sent_ref, out_ref, rows_ref, sems):
    elements, levels, columns = out_ref.shape
    lanes_all = received_ref.shape[1]
    cap = elements // levels
    tracers = columns // 16
    end = 0 if head else 1
    place = lax.broadcasted_iota(jnp.int32, (1, lanes_all), 1) % cap
    order = interleave(levels, cap)
    span = 4 * tracers
    spot = pl.ds(0, cap + 1) if head else pl.ds(elements - cap - 1, cap + 1)

    def rows(ref, block):
        return ref[block * tracers : (block + 1) * tracers, :].astype(f32)

    stores = []
    for j in range(4):
        got = [rows(received_ref, 3 * j + i) for i in range(3)]
        if head:
            own = pltpu.roll(rows(sent_ref, 3 * j + 2), lanes_all - (cap - 1), 1)
            west = got[0] + jnp.where(place == 0, own, 0.0)
            east = jnp.where(place == cap - 1, 0.0, pltpu.roll(got[0], lanes_all - 1, 1))
            got = [west, got[1], got[2], east]
        else:
            own = pltpu.roll(rows(sent_ref, 3 * j), cap - 1, 1)
            east = got[2] + jnp.where(place == cap - 1, own, 0.0)
            west = jnp.where(place == 0, 0.0, pltpu.roll(got[2], 1, 1))
            got = [west, got[0], got[1], east]
        pieces = []
        for i, value in enumerate(got):
            node = 4 * j + i
            here = ends_ref[end, node * tracers : (node + 1) * tracers, :].astype(f32)
            pieces.append((here + value).astype(bf16))
        y = lax.dot_general(
            order, jnp.concatenate(pieces, axis=0), (((1,), (1,)), ((), ())), preferred_element_type=f32
        ).reshape(cap, levels, span)
        first = 12 * tracers + 8 * (j * tracers // lanes_all)
        low = j * tracers % lanes_all
        far = received_ref[first : first + 8, low : low + tracers].astype(f32)[:levels]
        zeros = jnp.zeros((levels, span - tracers), f32)
        west = jnp.concatenate([far, zeros], axis=1)
        east = jnp.concatenate([zeros, far], axis=1)
        part = slice(j * span, (j + 1) * span)
        if head:
            rows_ref[0 : cap - 1, :, part] = y[: cap - 1].astype(bf16)
            rows_ref[cap - 1, :, part] = (y[cap - 1] + east).astype(bf16)
            rows_ref[cap, :, part] = (sides_ref[0, :, part].astype(f32) + west).astype(bf16)
        else:
            rows_ref[2:, :, part] = y[1:].astype(bf16)
            rows_ref[1, :, part] = (y[0] + west).astype(bf16)
            rows_ref[0, :, part] = (sides_ref[1, :, part].astype(f32) + east).astype(bf16)
        part = pl.ds(j * span, span)
        stores.append(pltpu.make_async_copy(rows_ref.at[:, :, part], out_ref.at[spot, :, part], sems.at[j]))
        stores[j].start()
    for store in stores:
        store.wait()


def on_device(tracers, velocity, node_mass, source):
    elements, levels, columns = tracers.shape
    cap = elements // 4
    assert cap * levels == elements
    count = columns // 16
    lanes = levels * elements
    runs = lax.axis_size("elem")
    pairing = [(i, i ^ 1) for i in range(runs)]
    crossing = [(i, (i - 1 if i % 2 == 0 else i + 1) % runs) for i in range(runs)]
    shape = jax.ShapeDtypeStruct
    vmem = pl.BlockSpec(memory_space=pltpu.VMEM)
    anywhere = pl.BlockSpec(memory_space=pl.ANY)
    source = source.reshape(1, elements)

    packet = shape((PACKET, elements), f32)
    inputs = (tracers, velocity, node_mass, source)
    lowest, cross_sent, pair_sent, tracers, velocity, node_mass, source = pl.pallas_call(
        prepare_kernel,
        out_shape=(shape((columns, elements), bf16), packet, packet)
        + tuple(shape(x.shape, x.dtype) for x in inputs),
        in_specs=[anywhere] * 4,
        scratch_shapes=[pltpu.VMEM((elements, 2, columns), bf16), pltpu.SemaphoreType.DMA((5,))],
        compiler_params=params(),
        name="prepare",
    )(*[pltpu.with_memory_space_constraint(x, pltpu.HBM) for x in inputs])
    blocks = lax.axis_size("lev")
    above = lax.ppermute(lowest, "lev", [(i, (i + 1) % blocks) for i in range(blocks)])
    spread_out = (shape((columns, elements), bf16), shape((16, count, lanes - elements), bf16))
    spread_scratch = [pltpu.VMEM((columns, lanes), bf16)]
    *early, pair_sent = pl.pallas_call(
        spread_early_kernel,
        out_shape=spread_out + (packet,),
        scratch_shapes=spread_scratch,
        compiler_params=params(),
        name="spread_early",
    )(tracers, velocity, pair_sent)
    pair_packet = lax.ppermute(pair_sent, "elem", pairing)
    cross_packet = lax.ppermute(cross_sent, "elem", crossing)
    def weighed(pair, packet, own, after):
        return pl.pallas_call(
            functools.partial(weigh_kernel, pair, levels),
            out_shape=(
                shape((16, 16, elements), f32),
                shape((16, 8, elements), f32),
                shape((lanes, 2 * elements), bf16),
            ),
            in_specs=[anywhere, vmem, vmem],
            compiler_params=params(),
            name="weigh_pair" if pair else "weigh_cross",
        )(after, packet, own)

    pair_weights = weighed(True, pair_packet, pair_sent, lowest)
    top, rest = pl.pallas_call(
        spread_kernel,
        out_shape=spread_out,
        scratch_shapes=spread_scratch,
        compiler_params=params(),
        name="spread",
    )(tracers, velocity, *early)
    first = pl.pallas_call(
        lift_first_kernel,
        out_shape=shape((16, count, elements), bf16),
        in_specs=[anywhere] + [vmem] * 3,
        compiler_params=params(),
        name="lift_first",
    )(pair_weights[1], top, above, velocity)

    far_rows = 8 * (4 * count // elements)

    message = shape((12 * count + far_rows, elements), bf16)
    message_scratch = [pltpu.VMEM((2, 16, count // 2, 2 * elements), f32), pltpu.VMEM((4 * count, elements), bf16)]
    pair_out = pl.pallas_call(
        functools.partial(remote_kernel, True),
        out_shape=message,
        in_specs=[anywhere] + [vmem] * 5,
        scratch_shapes=message_scratch,
        compiler_params=params(),
        name="remote_pair",
    )(first, first, rest, *pair_weights)
    pair_in = lax.ppermute(pair_out, "elem", pairing)
    cross_out = pl.pallas_call(
        functools.partial(weigh_remote_kernel, False, levels),
        out_shape=message,
        in_specs=[anywhere] + [vmem] * 4,
        scratch_shapes=message_scratch + [
            pltpu.VMEM((16, 16, elements), f32),
            pltpu.VMEM((16, 8, elements), f32),
            pltpu.VMEM((lanes, 2 * elements), bf16),
        ],
        compiler_params=params(),
        name="remote_cross",
    )(pair_out, cross_packet, cross_sent, first, rest)
    cross_in = lax.ppermute(cross_out, "elem", crossing)
    result = shape((elements, levels, columns), bf16)
    part, ends, sides = pl.pallas_call(
        local_kernel,
        out_shape=(result, shape((2, columns, elements), bf16), shape((2, levels, columns), bf16)),
        in_specs=[vmem] * 5 + [anywhere],
        out_specs=(anywhere, vmem, vmem),
        scratch_shapes=[
            pltpu.VMEM((2, 16, count, elements), f32),
            pltpu.VMEM((2, 16, 16, elements), f32),
            pltpu.VMEM((2, 16, elements), f32),
            pltpu.VMEM((columns, lanes), bf16),
            pltpu.VMEM((elements - 2 * cap, levels, columns), bf16),
            pltpu.SemaphoreType.DMA((4,)),
        ],
        compiler_params=params(),
        cost_estimate=cost(10**9),
        name="local",
    )(velocity, node_mass, source, first, rest, cross_out)
    for pair, received, sent in ((True, pair_in, pair_out), (False, cross_in, cross_out)):
        part = pl.pallas_call(
            functools.partial(combine_kernel, pair),
            out_shape=result,
            in_specs=[anywhere, vmem, vmem, vmem, vmem],
            out_specs=anywhere,
            scratch_shapes=[pltpu.VMEM((cap + 1, levels, columns), bf16), pltpu.SemaphoreType.DMA((4,))],
            input_output_aliases={0: 0},
            compiler_params=params(),
            name="combine_pair" if pair else "combine_cross",
        )(part, ends, sides, received, sent)
    return part


def solution(mesh):
    placed = (P("elem", "lev", None), P(None, None, "lev", "elem"), P(None, "elem"), P("elem"))
    return jax.shard_map(
        on_device, mesh=mesh, in_specs=placed, out_specs=P("elem", "lev", None), check_vma=False
    )
```

```python
import functools

import jax
import jax.numpy as jnp
from jax import lax
from jax.experimental import pallas as pl
from jax.experimental.pallas import tpu as pltpu
from jax.sharding import PartitionSpec as P

gll_points = (-1.0, -0.4472135954999579, 0.4472135954999579, 1.0)
courant = 0.15
f32 = jnp.float32
bf16 = jnp.bfloat16
VMEM_LIMIT = 40 << 20

MASS, NEAR, NEAR_MASS, SOURCE, PACKET = 32, 48, 56, 60, 64


def params():
    return pltpu.CompilerParams(vmem_limit_bytes=VMEM_LIMIT)


def cost(work):
    return pl.CostEstimate(flops=100 * work, bytes_accessed=work, transcendentals=0)


def interleave(groups, members):
    size = groups * members
    row = lax.broadcasted_iota(jnp.int32, (size, size), 0)
    column = lax.broadcasted_iota(jnp.int32, (size, size), 1)
    same = (row // groups == column % members) & (row % groups == column // members)
    return jnp.where(same, 1.0, 0.0).astype(bf16)


def basis(position):
    out = []
    for a in range(4):
        scale = 1.0
        factor = None
        for other in range(4):
            if other != a:
                scale /= gll_points[a] - gll_points[other]
                term = position - gll_points[other]
                factor = term if factor is None else factor * term
        out.append(factor * scale)
    return out


def node_rows(rows, lanes, of_i):
    row = lax.broadcasted_iota(jnp.int32, (rows, lanes), 0)
    index = row // 4 if of_i else row % 4
    out = jnp.full((rows, lanes), gll_points[0], f32)
    for a in range(1, 4):
        out = jnp.where(index == a, gll_points[a], out)
    return out


def table(winds):
    rows, lanes = winds[0].shape
    along = basis(node_rows(rows, lanes, True) - courant * winds[0])
    across = basis(node_rows(rows, lanes, False) - courant * winds[1])
    return along, across


def weight(along, across, share):
    return (along * across).astype(bf16).astype(f32) * share


def is_even():
    return lax.axis_index("elem") % 2 == 0


def prepare_kernel(
    tracers_hbm, velocity_hbm, mass_hbm, source_hbm,
    lowest_ref, cross_ref, pair_ref, tracers_ref, velocity_ref, mass_ref, source_ref, pair_of_levels_ref, sems,
):
    elements, levels, columns = tracers_hbm.shape
    step = 256
    copies = [
        pltpu.make_async_copy(here, there, sems.at[n])
        for n, (here, there) in enumerate(
            ((velocity_hbm, velocity_ref), (mass_hbm, mass_ref), (source_hbm, source_ref))
        )
    ]
    copies.append(pltpu.make_async_copy(tracers_hbm.at[:, pl.ds(levels - 2, 2), :], pair_of_levels_ref, sems.at[3]))
    copies.append(pltpu.make_async_copy(tracers_hbm, tracers_ref, sems.at[4]))
    for copy in copies:
        copy.start()
    for copy in copies[:3]:
        copy.wait()
    even = is_even()
    refs = (velocity_ref, mass_ref, source_ref)

    def both(head_ref, tail_ref):
        pack(True, *refs, head_ref)
        pack(False, *refs, tail_ref)

    pl.when(even)(lambda: both(cross_ref, pair_ref))
    pl.when(jnp.logical_not(even))(lambda: both(pair_ref, cross_ref))
    copies[3].wait()
    row = lax.broadcasted_iota(jnp.int32, (2 * elements, elements), 0)
    column = lax.broadcasted_iota(jnp.int32, (2 * elements, elements), 1)
    pick = jnp.where(row == column * 2 + 1, 1.0, 0.0).astype(bf16)
    x = pair_of_levels_ref[...].reshape(2 * elements, columns)
    for c in range(0, columns, step):
        lowest_ref[c : c + step, :] = lax.dot_general(
            x[:, c : c + step], pick, (((0,), (0,)), ((), ())), preferred_element_type=f32
        ).astype(bf16)
    copies[4].wait()


def pack(head, velocity_ref, mass_ref, source_ref, out_ref):
    _, _, levels, elements = velocity_ref.shape
    cap = elements // levels
    runs = lax.axis_size("elem")
    start = lax.axis_index("elem") * elements
    total = runs * elements
    low, nodes, step = (0, 0, 1) if head else (elements - cap, 3, -1)

    def lanes(pieces, shift=0):
        return jnp.concatenate([x[:, low + shift : low + shift + cap] for x in pieces], axis=1)

    for c in range(2):
        pieces = [velocity_ref[c, :, k, :] for k in range(levels)]
        out_ref[16 * c : 16 * c + 16, :] = lanes(pieces)
        near = lanes(pieces, step)
        for j in range(4):
            out_ref[NEAR + 4 * c + j : NEAR + 4 * c + j + 1, :] = near[4 * j + nodes : 4 * j + nodes + 1]
    mass = mass_ref[...]
    out_ref[MASS : MASS + 16, :] = lanes([mass] * levels)
    near = lanes([mass] * levels, step)
    for j in range(4):
        out_ref[NEAR_MASS + j : NEAR_MASS + j + 1, :] = near[4 * j + nodes : 4 * j + nodes + 1]
    relative = source_ref[...] - start + step * elements
    relative = jnp.where(relative < 0, relative + total, relative)
    relative = jnp.where(relative < 0, relative + total, relative)
    relative = jnp.where(relative >= total, relative - total, relative)
    out_ref[SOURCE : SOURCE + 1, :] = lanes([relative.astype(f32)] * levels)
    out_ref[SOURCE + 1 :, :] = jnp.zeros((PACKET - SOURCE - 1, elements), f32)


def lift(here, upper, descent):
    return ((1.0 - descent) * here.astype(f32) + descent * upper.astype(f32)).astype(bf16)


def descents(velocity_ref, k):
    return 1.0 / (1.0 + jnp.exp(-velocity_ref[2, :, k, :]))


def spread(tracers_ref, velocity_ref, top_ref, rest_ref, here_ref):
    elements, levels, columns = tracers_ref.shape
    nodes = velocity_ref.shape[1]
    tracers = columns // nodes
    order = interleave(levels, elements)
    x = tracers_ref[...].reshape(elements * levels, columns)
    step = 256
    for n in range(0, columns, step):
        here_ref[n : n + step, :] = lax.dot_general(
            x[:, n : n + step], order, (((0,), (0,)), ((), ())), preferred_element_type=f32
        ).astype(bf16)
    top_ref[...] = here_ref[:, :elements]
    for k in range(1, levels):
        descent = descents(velocity_ref, k)
        for m in range(nodes):
            rows = slice(m * tracers, (m + 1) * tracers)
            here = here_ref[rows, k * elements : (k + 1) * elements]
            upper = here_ref[rows, (k - 1) * elements : k * elements]
            rest_ref[m, :, (k - 1) * elements : k * elements] = lift(here, upper, descent[m : m + 1])


def spread_early_kernel(tracers_ref, velocity_ref, packet_ref, top_ref, rest_ref, sent_ref, here_ref):
    sent_ref[...] = packet_ref[...]
    pl.when(lax.axis_index("elem") == 0)(lambda: spread(tracers_ref, velocity_ref, top_ref, rest_ref, here_ref))


def spread_kernel(tracers_ref, velocity_ref, early_top_ref, early_rest_ref, top_ref, rest_ref, here_ref):
    early = lax.axis_index("elem") == 0

    @pl.when(early)
    def _():
        top_ref[...] = early_top_ref[...]
        rest_ref[...] = early_rest_ref[...]

    pl.when(jnp.logical_not(early))(lambda: spread(tracers_ref, velocity_ref, top_ref, rest_ref, here_ref))


def lift_first(top_ref, above_ref, velocity_ref, out_ref):
    _, nodes, _, elements = velocity_ref.shape
    tracers = above_ref.shape[0] // nodes
    descent = descents(velocity_ref, 0)
    below_top = lax.axis_index("lev") > 0
    for m in range(nodes):
        rows = slice(m * tracers, (m + 1) * tracers)
        upper = jnp.where(below_top, above_ref[rows, :].astype(f32), 0.0)
        out_ref[m] = lift(top_ref[rows, :], upper, descent[m : m + 1])


def by_i(ref, first, nodes=16):
    return [ref[pl.ds(first + i, 4, stride=4), :] for i in range(4)]


def shared(mass_left, left, mass_right, right):
    return (mass_left * left + mass_right * right) / (mass_left + mass_right)


def interpolate(weights_ref, blocks, nodes):
    totals = [None] * len(nodes)
    for m in range(16):
        block = blocks(m)
        for n, node in enumerate(nodes):
            term = weights_ref[m, node : node + 1, :] * block
            totals[n] = term if totals[n] is None else totals[n] + term
    return totals


def by_side(pair, body, *args):
    even = is_even()
    ahead = even if pair else jnp.logical_not(even)
    pl.when(ahead)(lambda: body(True, *args))
    pl.when(jnp.logical_not(ahead))(lambda: body(False, *args))


def weigh_kernel(pair, levels, after_ref, packet_ref, own_ref, weights_ref, extra_ref, chosen_ref):
    del after_ref
    by_side(pair, weigh, levels, packet_ref, own_ref, weights_ref, extra_ref, chosen_ref)


def pair_kernel(
    top_ref, above_ref, velocity_ref, rest_ref, weights_ref, extra_ref, chosen_ref,
    out_ref, first_ref, blocks_ref, edge_ref,
):
    def both(ahead):
        lift_first(top_ref, above_ref, velocity_ref, first_ref)
        remote(ahead, first_ref, rest_ref, weights_ref, extra_ref, chosen_ref, out_ref, blocks_ref, edge_ref)

    by_side(True, both)


def weigh_remote_kernel(
    pair, levels, after_ref, packet_ref, own_ref, first_ref, rest_ref,
    out_ref, blocks_ref, edge_ref, weights_ref, extra_ref, chosen_ref,
):
    del after_ref
    tables = (weights_ref, extra_ref, chosen_ref)

    def both(ahead):
        weigh(ahead, levels, packet_ref, own_ref, *tables)
        remote(ahead, first_ref, rest_ref, *tables, out_ref, blocks_ref, edge_ref)

    by_side(pair, both)


def weigh(ahead, levels, packet_ref, own_ref, weights_ref, extra_ref, chosen_ref):
    lanes_all = packet_ref.shape[1]
    elements = lanes_all
    cap = elements // levels
    total = lax.axis_size("elem") * elements
    lane = lax.broadcasted_iota(jnp.int32, (1, lanes_all), 1)
    level, place = lane // cap, lane % cap
    edge = place == (0 if ahead else cap - 1)

    def beside(values, own):
        if ahead:
            return jnp.where(edge, pltpu.roll(own, lanes_all - (cap - 1), 1), pltpu.roll(values, 1, 1))
        return jnp.where(edge, pltpu.roll(own, cap - 1, 1), pltpu.roll(values, lanes_all - 1, 1))

    mass = by_i(packet_ref, MASS)
    own_mass = by_i(own_ref, MASS)
    near_mass = packet_ref[NEAR_MASS : NEAR_MASS + 4, :]
    if ahead:
        mass_before, mass_after = beside(mass[3], own_mass[3]), near_mass
    else:
        mass_before, mass_after = near_mass, beside(mass[0], own_mass[0])
    share_west = mass[0] / (mass_before + mass[0])
    share_east = mass[3] / (mass[3] + mass_after)
    winds = []
    edge_winds = []
    for c in range(2):
        wind = by_i(packet_ref, 16 * c)
        own = by_i(own_ref, 16 * c)
        near = packet_ref[NEAR + 4 * c : NEAR + 4 * c + 4, :]
        if ahead:
            before, after = beside(wind[3], own[3]), near
        else:
            before, after = near, beside(wind[0], own[0])
        west = shared(mass_before, before, mass[0], wind[0])
        east = shared(mass[3], wind[3], mass_after, after)
        winds.append(jnp.concatenate([west, wind[1], wind[2], east], axis=0))
        edge_winds.append(west if ahead else east)
    ones = jnp.ones((8, lanes_all), f32)
    along, across = table(winds)
    share = jnp.concatenate([share_west, ones, share_east], axis=0)
    for b in range(4):
        for a in range(4):
            weights_ref[4 * b + a] = weight(along[a], across[b], share)
    at = 0 if ahead else cap - 1

    def spread(rows):
        out = jnp.zeros((1, lanes_all), f32)
        for j in range(4):
            out = jnp.where(place == j, pltpu.roll(rows[j : j + 1], (j - at) % lanes_all, 1), out)
        return out

    edge_share = spread(1.0 - (share_west if ahead else share_east))
    node = jnp.where(place < 2, jnp.where(place == 0, *gll_points[:2]), jnp.where(place == 2, *gll_points[2:]))
    extra_along = basis(gll_points[3 if ahead else 0] - courant * spread(edge_winds[0]))
    extra_across = basis(node - courant * spread(edge_winds[1]))
    for b in range(4):
        for a in range(4):
            extra_ref[4 * b + a, 0:1] = weight(extra_along[a], extra_across[b], edge_share)

    source = packet_ref[SOURCE : SOURCE + 1, :].astype(jnp.int32)
    own_source = jnp.where(lane == (cap - 1 if ahead else 0), own_ref[SOURCE : SOURCE + 1, :], 0.0)
    own_source = jnp.sum(own_source, axis=1, keepdims=True).astype(jnp.int32) + (elements if ahead else -elements)
    own_source = jnp.where(own_source >= total, own_source - total, own_source)
    own_source = jnp.where(own_source < 0, own_source + total, own_source)
    row = lax.broadcasted_iota(jnp.int32, (levels * elements, lanes_all), 0)
    same = row // elements == level
    first = jnp.where(same & (row % elements == source), 1.0, 0.0).astype(bf16)
    second = jnp.where(same & (place < 4) & (row % elements == own_source), 1.0, 0.0).astype(bf16)
    chosen_ref[...] = jnp.concatenate([first, second], axis=1)


def remote(ahead, first_ref, rest_ref, weights_ref, extra_ref, chosen_ref, out_ref, blocks_ref, edge_ref):
    lanes_all = out_ref.shape[1]
    levels = 1 + rest_ref.shape[2] // lanes_all
    cap = lanes_all // levels
    tracers = first_ref.shape[1]
    lane = lax.broadcasted_iota(jnp.int32, (1, lanes_all), 1)
    place = lane % cap
    edge = place == (0 if ahead else cap - 1)
    chosen = chosen_ref[...]
    lanes = slice(0, lanes_all)
    half = tracers // 2

    def fetch(n):
        rows = slice(n * half, (n + 1) * half)
        for m in range(0, 16, 8):
            near = jnp.concatenate([first_ref[m : m + 8, rows, :], rest_ref[m : m + 8, rows, lanes]], axis=2)
            far = rest_ref[m : m + 8, rows, lanes_all:]
            y = jnp.dot(
                near.reshape(8 * half, 2 * lanes_all), chosen[: 2 * lanes_all], preferred_element_type=f32
            ) + jnp.dot(
                far.reshape(8 * half, (levels - 2) * lanes_all), chosen[2 * lanes_all :], preferred_element_type=f32
            )
            blocks_ref[n, m : m + 8] = y.reshape(8, half, 2 * lanes_all)

    fetch(0)
    for n in range(2):
        if n == 0:
            fetch(1)
        (own,) = interpolate(extra_ref, lambda m: blocks_ref[n, m, :, lanes_all:], (0,))
        for j in range(4):
            ends = interpolate(weights_ref, lambda m: blocks_ref[n, m, :, lanes], (j, 12 + j))
            middle = interpolate(weights_ref, lambda m: blocks_ref[n, m, :, lanes], (4 + j, 8 + j))
            own_here = pltpu.roll(own, ((0 if ahead else cap - 1) - j) % lanes_all, 1)
            if ahead:
                west = ends[0] + jnp.where(edge, own_here, pltpu.roll(ends[1], 1, 1))
                values, far = (west, *middle), ends[1]
            else:
                east = ends[1] + jnp.where(edge, own_here, pltpu.roll(ends[0], lanes_all - 1, 1))
                values, far = (*middle, east), ends[0]
            for i, value in enumerate(values):
                row = (3 * j + i) * tracers + n * half
                out_ref[row : row + half, :] = value.astype(bf16)
            row = j * tracers + n * half
            edge_ref[row : row + half, :] = far.astype(bf16)
    row = lax.broadcasted_iota(jnp.int32, (8, lanes_all), 0)
    far_place = cap - 1 if ahead else 0
    pick = jnp.where(lane == row * cap + far_place, 1.0, 0.0).astype(bf16)
    far = lax.dot_general(pick, edge_ref[...], (((1,), (1,)), ((), ())), preferred_element_type=f32)
    far = [far[:, n : n + lanes_all] for n in range(0, 4 * tracers, lanes_all)]
    out_ref[12 * tracers :, :] = jnp.concatenate(far, axis=0).astype(bf16)


def local_kernel(
    velocity_ref, mass_ref, source_ref, first_ref, rest_ref, after_ref,
    out_ref, ends_ref, sides_ref,
    blocks_ref, weights_ref, wind_ref, moved_ref, inner_ref, sems,
):
    del after_ref
    _, _, levels, elements = velocity_ref.shape
    cap = elements // levels
    columns = out_ref.shape[2]
    tracers = columns // 16
    start = lax.axis_index("elem") * elements
    lane = lax.broadcasted_iota(jnp.int32, (1, elements), 1)
    mass = by_i(mass_ref, 0)
    mass_before = pltpu.roll(mass[3], 1, 1)
    mass_after = pltpu.roll(mass[0], elements - 1, 1)
    share_west = mass[0] / (mass_before + mass[0])
    share_east = mass[3] / (mass[3] + mass_after)
    coefficient = jnp.concatenate([share_west, jnp.ones((8, elements), f32), share_east], axis=0)
    row = lax.broadcasted_iota(jnp.int32, (elements, elements), 0)
    chosen = jnp.where(row == source_ref[...] - start, 1.0, 0.0).astype(bf16)

    def fetch(k):
        x = rest_ref[:, :, (k - 1) * elements : k * elements] if k else first_ref[...]
        y = jnp.dot(x.reshape(columns, elements), chosen, preferred_element_type=f32)
        blocks_ref[k % 2] = y.reshape(16, tracers, elements)

    fetch(0)
    for k in range(levels):
        winds = []
        for c in range(2):
            wind_ref[c] = velocity_ref[c, :, k, :]
            wind = [wind_ref[c, pl.ds(i, 4, stride=4), :] for i in range(4)]
            west = shared(mass_before, pltpu.roll(wind[3], 1, 1), mass[0], wind[0])
            east = shared(mass[3], wind[3], mass_after, pltpu.roll(wind[0], elements - 1, 1))
            winds.append(jnp.concatenate([west, wind[1], wind[2], east], axis=0))
        along, across = table(winds)
        for b in range(4):
            for a in range(4):
                weights_ref[k % 2, 4 * b + a] = weight(along[a], across[b], coefficient)
        if k + 1 < levels:
            fetch(k + 1)
        lanes = slice(k * elements, (k + 1) * elements)
        table_ref = weights_ref.at[k % 2]
        for j in range(4):
            ends = interpolate(table_ref, lambda m: blocks_ref[k % 2, m], (j, 12 + j))
            middle = interpolate(table_ref, lambda m: blocks_ref[k % 2, m], (4 + j, 8 + j))
            west = jnp.where(lane == 0, 0.0, ends[0] + pltpu.roll(ends[1], 1, 1))
            east = pltpu.roll(west, elements - 1, 1)
            for i, value in enumerate((west, *middle, east)):
                node = 4 * j + i
                moved_ref[node * tracers : (node + 1) * tracers, lanes] = value.astype(bf16)
    inner = elements - 2 * cap
    row = lax.broadcasted_iota(jnp.int32, (inner * levels, elements * levels), 0)
    column = lax.broadcasted_iota(jnp.int32, (inner * levels, elements * levels), 1)
    same = (row // levels + cap == column % elements) & (row % levels == column // elements)
    order = jnp.where(same, 1.0, 0.0).astype(bf16)
    step = columns // 4
    stores = []
    for n in range(4):
        part = pl.ds(n * step, step)
        y = lax.dot_general(
            order, moved_ref[part, :], (((1,), (1,)), ((), ())), preferred_element_type=f32
        )
        inner_ref[:, :, part] = y.reshape(inner, levels, step).astype(bf16)
        stores.append(pltpu.make_async_copy(
            inner_ref.at[pl.ds(1, inner - 2), :, part], out_ref.at[pl.ds(cap + 1, inner - 2), :, part], sems.at[n]
        ))
        stores[n].start()
    sides_ref[0] = inner_ref[0]
    sides_ref[1] = inner_ref[inner - 1]
    for n, low in enumerate((0, elements - cap)):
        ends_ref[n] = jnp.concatenate(
            [moved_ref[:, k * elements + low : k * elements + low + cap] for k in range(levels)], axis=1
        )
    for store in stores:
        store.wait()


def combine_kernel(pair, part_ref, ends_ref, sides_ref, received_ref, sent_ref, out_ref, rows_ref, sems):
    del part_ref
    refs = (ends_ref, sides_ref, received_ref, sent_ref, out_ref, rows_ref, sems)
    even = is_even()
    head = jnp.logical_not(even) if pair else even
    pl.when(head)(lambda: combine(True, *refs))
    pl.when(jnp.logical_not(head))(lambda: combine(False, *refs))


def combine(head, ends_ref, sides_ref, received_ref, sent_ref, out_ref, rows_ref, sems):
    elements, levels, columns = out_ref.shape
    lanes_all = received_ref.shape[1]
    cap = elements // levels
    tracers = columns // 16
    end = 0 if head else 1
    place = lax.broadcasted_iota(jnp.int32, (1, lanes_all), 1) % cap
    order = interleave(levels, cap)
    span = 4 * tracers
    spot = pl.ds(0, cap + 1) if head else pl.ds(elements - cap - 1, cap + 1)

    def rows(ref, block):
        return ref[block * tracers : (block + 1) * tracers, :].astype(f32)

    stores = []
    for j in range(4):
        got = [rows(received_ref, 3 * j + i) for i in range(3)]
        if head:
            own = pltpu.roll(rows(sent_ref, 3 * j + 2), lanes_all - (cap - 1), 1)
            west = got[0] + jnp.where(place == 0, own, 0.0)
            east = jnp.where(place == cap - 1, 0.0, pltpu.roll(got[0], lanes_all - 1, 1))
            got = [west, got[1], got[2], east]
        else:
            own = pltpu.roll(rows(sent_ref, 3 * j), cap - 1, 1)
            east = got[2] + jnp.where(place == cap - 1, own, 0.0)
            west = jnp.where(place == 0, 0.0, pltpu.roll(got[2], 1, 1))
            got = [west, got[0], got[1], east]
        pieces = []
        for i, value in enumerate(got):
            node = 4 * j + i
            here = ends_ref[end, node * tracers : (node + 1) * tracers, :].astype(f32)
            pieces.append((here + value).astype(bf16))
        y = lax.dot_general(
            order, jnp.concatenate(pieces, axis=0), (((1,), (1,)), ((), ())), preferred_element_type=f32
        ).reshape(cap, levels, span)
        first = 12 * tracers + 8 * (j * tracers // lanes_all)
        low = j * tracers % lanes_all
        far = received_ref[first : first + 8, low : low + tracers].astype(f32)[:levels]
        zeros = jnp.zeros((levels, span - tracers), f32)
        west = jnp.concatenate([far, zeros], axis=1)
        east = jnp.concatenate([zeros, far], axis=1)
        part = slice(j * span, (j + 1) * span)
        if head:
            rows_ref[0 : cap - 1, :, part] = y[: cap - 1].astype(bf16)
            rows_ref[cap - 1, :, part] = (y[cap - 1] + east).astype(bf16)
            rows_ref[cap, :, part] = (sides_ref[0, :, part].astype(f32) + west).astype(bf16)
        else:
            rows_ref[2:, :, part] = y[1:].astype(bf16)
            rows_ref[1, :, part] = (y[0] + west).astype(bf16)
            rows_ref[0, :, part] = (sides_ref[1, :, part].astype(f32) + east).astype(bf16)
        part = pl.ds(j * span, span)
        stores.append(pltpu.make_async_copy(rows_ref.at[:, :, part], out_ref.at[spot, :, part], sems.at[j]))
        stores[j].start()
    for store in stores:
        store.wait()


def on_device(tracers, velocity, node_mass, source):
    elements, levels, columns = tracers.shape
    cap = elements // 4
    assert cap * levels == elements
    count = columns // 16
    lanes = levels * elements
    runs = lax.axis_size("elem")
    pairing = [(i, i ^ 1) for i in range(runs)]
    crossing = [(i, (i - 1 if i % 2 == 0 else i + 1) % runs) for i in range(runs)]
    shape = jax.ShapeDtypeStruct
    vmem = pl.BlockSpec(memory_space=pltpu.VMEM)
    anywhere = pl.BlockSpec(memory_space=pl.ANY)
    source = source.reshape(1, elements)

    packet = shape((PACKET, elements), f32)
    inputs = (tracers, velocity, node_mass, source)
    lowest, cross_sent, pair_sent, tracers, velocity, node_mass, source = pl.pallas_call(
        prepare_kernel,
        out_shape=(shape((columns, elements), bf16), packet, packet)
        + tuple(shape(x.shape, x.dtype) for x in inputs),
        in_specs=[anywhere] * 4,
        scratch_shapes=[pltpu.VMEM((elements, 2, columns), bf16), pltpu.SemaphoreType.DMA((5,))],
        compiler_params=params(),
        name="prepare",
    )(*[pltpu.with_memory_space_constraint(x, pltpu.HBM) for x in inputs])
    blocks = lax.axis_size("lev")
    above = lax.ppermute(lowest, "lev", [(i, (i + 1) % blocks) for i in range(blocks)])
    spread_out = (shape((columns, elements), bf16), shape((16, count, lanes - elements), bf16))
    spread_scratch = [pltpu.VMEM((columns, lanes), bf16)]
    *early, pair_sent = pl.pallas_call(
        spread_early_kernel,
        out_shape=spread_out + (packet,),
        scratch_shapes=spread_scratch,
        compiler_params=params(),
        name="spread_early",
    )(tracers, velocity, pair_sent)
    pair_packet = lax.ppermute(pair_sent, "elem", pairing)
    cross_packet = lax.ppermute(cross_sent, "elem", crossing)
    def weighed(pair, packet, own, after):
        return pl.pallas_call(
            functools.partial(weigh_kernel, pair, levels),
            out_shape=(
                shape((16, 16, elements), f32),
                shape((16, 8, elements), f32),
                shape((lanes, 2 * elements), bf16),
            ),
            in_specs=[anywhere, vmem, vmem],
            compiler_params=params(),
            name="weigh_pair" if pair else "weigh_cross",
        )(after, packet, own)

    pair_weights = weighed(True, pair_packet, pair_sent, lowest)
    top, rest = pl.pallas_call(
        spread_kernel,
        out_shape=spread_out,
        scratch_shapes=spread_scratch,
        compiler_params=params(),
        name="spread",
    )(tracers, velocity, *early)
    far_rows = 8 * (4 * count // elements)

    message = shape((12 * count + far_rows, elements), bf16)
    message_scratch = [pltpu.VMEM((2, 16, count // 2, 2 * elements), f32), pltpu.VMEM((4 * count, elements), bf16)]
    pair_out, first = pl.pallas_call(
        pair_kernel,
        out_shape=(message, shape((16, count, elements), bf16)),
        scratch_shapes=message_scratch,
        compiler_params=params(),
        name="remote_pair",
    )(top, above, velocity, rest, *pair_weights)
    pair_in = lax.ppermute(pair_out, "elem", pairing)
    cross_out = pl.pallas_call(
        functools.partial(weigh_remote_kernel, False, levels),
        out_shape=message,
        in_specs=[anywhere] + [vmem] * 4,
        scratch_shapes=message_scratch + [
            pltpu.VMEM((16, 16, elements), f32),
            pltpu.VMEM((16, 8, elements), f32),
            pltpu.VMEM((lanes, 2 * elements), bf16),
        ],
        compiler_params=params(),
        name="remote_cross",
    )(pair_out, cross_packet, cross_sent, first, rest)
    cross_in = lax.ppermute(cross_out, "elem", crossing)
    result = shape((elements, levels, columns), bf16)
    part, ends, sides = pl.pallas_call(
        local_kernel,
        out_shape=(result, shape((2, columns, elements), bf16), shape((2, levels, columns), bf16)),
        in_specs=[vmem] * 5 + [anywhere],
        out_specs=(anywhere, vmem, vmem),
        scratch_shapes=[
            pltpu.VMEM((2, 16, count, elements), f32),
            pltpu.VMEM((2, 16, 16, elements), f32),
            pltpu.VMEM((2, 16, elements), f32),
            pltpu.VMEM((columns, lanes), bf16),
            pltpu.VMEM((elements - 2 * cap, levels, columns), bf16),
            pltpu.SemaphoreType.DMA((4,)),
        ],
        compiler_params=params(),
        cost_estimate=cost(10**9),
        name="local",
    )(velocity, node_mass, source, first, rest, cross_out)
    for pair, received, sent in ((True, pair_in, pair_out), (False, cross_in, cross_out)):
        part = pl.pallas_call(
            functools.partial(combine_kernel, pair),
            out_shape=result,
            in_specs=[anywhere, vmem, vmem, vmem, vmem],
            out_specs=anywhere,
            scratch_shapes=[pltpu.VMEM((cap + 1, levels, columns), bf16), pltpu.SemaphoreType.DMA((4,))],
            input_output_aliases={0: 0},
            compiler_params=params(),
            name="combine_pair" if pair else "combine_cross",
        )(part, ends, sides, received, sent)
    return part


def solution(mesh):
    placed = (P("elem", "lev", None), P(None, None, "lev", "elem"), P(None, "elem"), P("elem"))
    return jax.shard_map(
        on_device, mesh=mesh, in_specs=placed, out_specs=P("elem", "lev", None), check_vma=False
    )
```

```python
import functools

import jax
import jax.numpy as jnp
from jax import lax
from jax.experimental import pallas as pl
from jax.experimental.pallas import tpu as pltpu
from jax.sharding import PartitionSpec as P

gll_points = (-1.0, -0.4472135954999579, 0.4472135954999579, 1.0)
courant = 0.15
f32 = jnp.float32
bf16 = jnp.bfloat16
VMEM_LIMIT = 40 << 20

MASS, NEAR, NEAR_MASS, SOURCE, PACKET = 32, 48, 56, 60, 64


def params():
    return pltpu.CompilerParams(vmem_limit_bytes=VMEM_LIMIT)


def cost(work):
    return pl.CostEstimate(flops=100 * work, bytes_accessed=work, transcendentals=0)


def interleave(groups, members):
    size = groups * members
    row = lax.broadcasted_iota(jnp.int32, (size, size), 0)
    column = lax.broadcasted_iota(jnp.int32, (size, size), 1)
    same = (row // groups == column % members) & (row % groups == column // members)
    return jnp.where(same, 1.0, 0.0).astype(bf16)


def basis(position):
    out = []
    for a in range(4):
        scale = 1.0
        factor = None
        for other in range(4):
            if other != a:
                scale /= gll_points[a] - gll_points[other]
                term = position - gll_points[other]
                factor = term if factor is None else factor * term
        out.append(factor * scale)
    return out


def node_rows(rows, lanes, of_i):
    row = lax.broadcasted_iota(jnp.int32, (rows, lanes), 0)
    index = row // 4 if of_i else row % 4
    out = jnp.full((rows, lanes), gll_points[0], f32)
    for a in range(1, 4):
        out = jnp.where(index == a, gll_points[a], out)
    return out


def table(winds):
    rows, lanes = winds[0].shape
    along = basis(node_rows(rows, lanes, True) - courant * winds[0])
    across = basis(node_rows(rows, lanes, False) - courant * winds[1])
    return along, across


def weight(along, across, share):
    return (along * across).astype(bf16).astype(f32) * share


def is_even():
    return lax.axis_index("elem") % 2 == 0


def prepare_kernel(
    tracers_hbm, velocity_hbm, mass_hbm, source_hbm,
    lowest_ref, cross_ref, pair_ref, tracers_ref, velocity_ref, mass_ref, source_ref, pair_of_levels_ref, sems,
):
    elements, levels, columns = tracers_hbm.shape
    step = 512
    copies = [
        pltpu.make_async_copy(here, there, sems.at[n])
        for n, (here, there) in enumerate(
            ((velocity_hbm, velocity_ref), (mass_hbm, mass_ref), (source_hbm, source_ref))
        )
    ]
    copies.append(pltpu.make_async_copy(tracers_hbm.at[:, pl.ds(levels - 2, 2), :], pair_of_levels_ref, sems.at[3]))
    copies.append(pltpu.make_async_copy(tracers_hbm, tracers_ref, sems.at[4]))
    for copy in copies:
        copy.start()
    for copy in copies[:3]:
        copy.wait()
    even = is_even()
    refs = (velocity_ref, mass_ref, source_ref)

    def both(head_ref, tail_ref):
        pack(True, *refs, head_ref)
        pack(False, *refs, tail_ref)

    pl.when(even)(lambda: both(cross_ref, pair_ref))
    pl.when(jnp.logical_not(even))(lambda: both(pair_ref, cross_ref))
    copies[3].wait()
    row = lax.broadcasted_iota(jnp.int32, (2 * elements, elements), 0)
    column = lax.broadcasted_iota(jnp.int32, (2 * elements, elements), 1)
    pick = jnp.where(row == column * 2 + 1, 1.0, 0.0).astype(bf16)
    x = pair_of_levels_ref[...].reshape(2 * elements, columns)
    for c in range(0, columns, step):
        lowest_ref[c : c + step, :] = lax.dot_general(
            x[:, c : c + step], pick, (((0,), (0,)), ((), ())), preferred_element_type=f32
        ).astype(bf16)
    copies[4].wait()


def pack(head, velocity_ref, mass_ref, source_ref, out_ref):
    _, _, levels, elements = velocity_ref.shape
    cap = elements // levels
    runs = lax.axis_size("elem")
    start = lax.axis_index("elem") * elements
    total = runs * elements
    low, nodes, step = (0, 0, 1) if head else (elements - cap, 3, -1)

    def lanes(pieces, shift=0):
        return jnp.concatenate([x[:, low + shift : low + shift + cap] for x in pieces], axis=1)

    for c in range(2):
        pieces = [velocity_ref[c, :, k, :] for k in range(levels)]
        out_ref[16 * c : 16 * c + 16, :] = lanes(pieces)
        near = lanes(pieces, step)
        for j in range(4):
            out_ref[NEAR + 4 * c + j : NEAR + 4 * c + j + 1, :] = near[4 * j + nodes : 4 * j + nodes + 1]
    mass = mass_ref[...]
    out_ref[MASS : MASS + 16, :] = lanes([mass] * levels)
    near = lanes([mass] * levels, step)
    for j in range(4):
        out_ref[NEAR_MASS + j : NEAR_MASS + j + 1, :] = near[4 * j + nodes : 4 * j + nodes + 1]
    relative = source_ref[...] - start + step * elements
    relative = jnp.where(relative < 0, relative + total, relative)
    relative = jnp.where(relative < 0, relative + total, relative)
    relative = jnp.where(relative >= total, relative - total, relative)
    out_ref[SOURCE : SOURCE + 1, :] = lanes([relative.astype(f32)] * levels)
    out_ref[SOURCE + 1 :, :] = jnp.zeros((PACKET - SOURCE - 1, elements), f32)


def lift(here, upper, descent):
    return ((1.0 - descent) * here.astype(f32) + descent * upper.astype(f32)).astype(bf16)


def descents(velocity_ref, k):
    return 1.0 / (1.0 + jnp.exp(-velocity_ref[2, :, k, :]))


def spread(tracers_ref, velocity_ref, top_ref, rest_ref, here_ref):
    elements, levels, columns = tracers_ref.shape
    nodes = velocity_ref.shape[1]
    tracers = columns // nodes
    order = interleave(levels, elements)
    x = tracers_ref[...].reshape(elements * levels, columns)
    step = 256
    for n in range(0, columns, step):
        here_ref[n : n + step, :] = lax.dot_general(
            x[:, n : n + step], order, (((0,), (0,)), ((), ())), preferred_element_type=f32
        ).astype(bf16)
    top_ref[...] = here_ref[:, :elements]
    for k in range(1, levels):
        descent = descents(velocity_ref, k)
        for m in range(nodes):
            rows = slice(m * tracers, (m + 1) * tracers)
            here = here_ref[rows, k * elements : (k + 1) * elements]
            upper = here_ref[rows, (k - 1) * elements : k * elements]
            rest_ref[m, :, (k - 1) * elements : k * elements] = lift(here, upper, descent[m : m + 1])


def spread_early_kernel(tracers_ref, velocity_ref, packet_ref, top_ref, rest_ref, sent_ref, here_ref):
    sent_ref[...] = packet_ref[...]
    pl.when(lax.axis_index("elem") == 0)(lambda: spread(tracers_ref, velocity_ref, top_ref, rest_ref, here_ref))


def spread_kernel(tracers_ref, velocity_ref, early_top_ref, early_rest_ref, top_ref, rest_ref, here_ref):
    early = lax.axis_index("elem") == 0

    @pl.when(early)
    def _():
        top_ref[...] = early_top_ref[...]
        rest_ref[...] = early_rest_ref[...]

    pl.when(jnp.logical_not(early))(lambda: spread(tracers_ref, velocity_ref, top_ref, rest_ref, here_ref))


def lift_first(top_ref, above_ref, velocity_ref, out_ref):
    _, nodes, _, elements = velocity_ref.shape
    tracers = above_ref.shape[0] // nodes
    descent = descents(velocity_ref, 0)
    below_top = lax.axis_index("lev") > 0
    for m in range(nodes):
        rows = slice(m * tracers, (m + 1) * tracers)
        upper = jnp.where(below_top, above_ref[rows, :].astype(f32), 0.0)
        out_ref[m] = lift(top_ref[rows, :], upper, descent[m : m + 1])


def by_i(ref, first, nodes=16):
    return [ref[pl.ds(first + i, 4, stride=4), :] for i in range(4)]


def shared(mass_left, left, mass_right, right):
    return (mass_left * left + mass_right * right) / (mass_left + mass_right)


def interpolate(weights_ref, blocks, nodes):
    totals = [None] * len(nodes)
    for m in range(16):
        block = blocks(m)
        for n, node in enumerate(nodes):
            term = weights_ref[m, node : node + 1, :] * block
            totals[n] = term if totals[n] is None else totals[n] + term
    return totals


def by_side(pair, body, *args):
    even = is_even()
    ahead = even if pair else jnp.logical_not(even)
    pl.when(ahead)(lambda: body(True, *args))
    pl.when(jnp.logical_not(ahead))(lambda: body(False, *args))


def weigh_kernel(pair, levels, after_ref, packet_ref, own_ref, weights_ref, extra_ref, chosen_ref):
    del after_ref
    by_side(pair, weigh, levels, packet_ref, own_ref, weights_ref, extra_ref, chosen_ref)


def pair_kernel(
    top_ref, above_ref, velocity_ref, rest_ref, weights_ref, extra_ref, chosen_ref,
    out_ref, first_ref, blocks_ref, edge_ref,
):
    def both(ahead):
        lift_first(top_ref, above_ref, velocity_ref, first_ref)
        remote(ahead, first_ref, rest_ref, weights_ref, extra_ref, chosen_ref, out_ref, blocks_ref, edge_ref)

    by_side(True, both)


def weigh_remote_kernel(
    pair, levels, after_ref, packet_ref, own_ref, first_ref, rest_ref,
    out_ref, blocks_ref, edge_ref, weights_ref, extra_ref, chosen_ref,
):
    del after_ref
    tables = (weights_ref, extra_ref, chosen_ref)

    def both(ahead):
        weigh(ahead, levels, packet_ref, own_ref, *tables)
        remote(ahead, first_ref, rest_ref, *tables, out_ref, blocks_ref, edge_ref)

    by_side(pair, both)


def weigh(ahead, levels, packet_ref, own_ref, weights_ref, extra_ref, chosen_ref):
    lanes_all = packet_ref.shape[1]
    elements = lanes_all
    cap = elements // levels
    total = lax.axis_size("elem") * elements
    lane = lax.broadcasted_iota(jnp.int32, (1, lanes_all), 1)
    level, place = lane // cap, lane % cap
    edge = place == (0 if ahead else cap - 1)

    def beside(values, own):
        if ahead:
            return jnp.where(edge, pltpu.roll(own, lanes_all - (cap - 1), 1), pltpu.roll(values, 1, 1))
        return jnp.where(edge, pltpu.roll(own, cap - 1, 1), pltpu.roll(values, lanes_all - 1, 1))

    mass = by_i(packet_ref, MASS)
    own_mass = by_i(own_ref, MASS)
    near_mass = packet_ref[NEAR_MASS : NEAR_MASS + 4, :]
    if ahead:
        mass_before, mass_after = beside(mass[3], own_mass[3]), near_mass
    else:
        mass_before, mass_after = near_mass, beside(mass[0], own_mass[0])
    share_west = mass[0] / (mass_before + mass[0])
    share_east = mass[3] / (mass[3] + mass_after)
    winds = []
    edge_winds = []
    for c in range(2):
        wind = by_i(packet_ref, 16 * c)
        own = by_i(own_ref, 16 * c)
        near = packet_ref[NEAR + 4 * c : NEAR + 4 * c + 4, :]
        if ahead:
            before, after = beside(wind[3], own[3]), near
        else:
            before, after = near, beside(wind[0], own[0])
        west = shared(mass_before, before, mass[0], wind[0])
        east = shared(mass[3], wind[3], mass_after, after)
        winds.append(jnp.concatenate([west, wind[1], wind[2], east], axis=0))
        edge_winds.append(west if ahead else east)
    ones = jnp.ones((8, lanes_all), f32)
    along, across = table(winds)
    share = jnp.concatenate([share_west, ones, share_east], axis=0)
    for b in range(4):
        for a in range(4):
            weights_ref[4 * b + a] = weight(along[a], across[b], share)
    at = 0 if ahead else cap - 1

    def spread(rows):
        out = jnp.zeros((1, lanes_all), f32)
        for j in range(4):
            out = jnp.where(place == j, pltpu.roll(rows[j : j + 1], (j - at) % lanes_all, 1), out)
        return out

    edge_share = spread(1.0 - (share_west if ahead else share_east))
    node = jnp.where(place < 2, jnp.where(place == 0, *gll_points[:2]), jnp.where(place == 2, *gll_points[2:]))
    extra_along = basis(gll_points[3 if ahead else 0] - courant * spread(edge_winds[0]))
    extra_across = basis(node - courant * spread(edge_winds[1]))
    for b in range(4):
        for a in range(4):
            extra_ref[4 * b + a, 0:1] = weight(extra_along[a], extra_across[b], edge_share)

    source = packet_ref[SOURCE : SOURCE + 1, :].astype(jnp.int32)
    own_source = jnp.where(lane == (cap - 1 if ahead else 0), own_ref[SOURCE : SOURCE + 1, :], 0.0)
    own_source = jnp.sum(own_source, axis=1, keepdims=True).astype(jnp.int32) + (elements if ahead else -elements)
    own_source = jnp.where(own_source >= total, own_source - total, own_source)
    own_source = jnp.where(own_source < 0, own_source + total, own_source)
    row = lax.broadcasted_iota(jnp.int32, (levels * elements, lanes_all), 0)
    same = row // elements == level
    first = jnp.where(same & (row % elements == source), 1.0, 0.0).astype(bf16)
    second = jnp.where(same & (place < 4) & (row % elements == own_source), 1.0, 0.0).astype(bf16)
    chosen_ref[...] = jnp.concatenate([first, second], axis=1)


def remote(ahead, first_ref, rest_ref, weights_ref, extra_ref, chosen_ref, out_ref, blocks_ref, edge_ref):
    lanes_all = out_ref.shape[1]
    levels = 1 + rest_ref.shape[2] // lanes_all
    cap = lanes_all // levels
    tracers = first_ref.shape[1]
    lane = lax.broadcasted_iota(jnp.int32, (1, lanes_all), 1)
    place = lane % cap
    edge = place == (0 if ahead else cap - 1)
    chosen = chosen_ref[...]
    lanes = slice(0, lanes_all)
    half = tracers // 2

    def fetch(n):
        rows = slice(n * half, (n + 1) * half)
        for m in range(0, 16, 8):
            near = jnp.concatenate([first_ref[m : m + 8, rows, :], rest_ref[m : m + 8, rows, lanes]], axis=2)
            far = rest_ref[m : m + 8, rows, lanes_all:]
            y = jnp.dot(
                near.reshape(8 * half, 2 * lanes_all), chosen[: 2 * lanes_all], preferred_element_type=f32
            ) + jnp.dot(
                far.reshape(8 * half, (levels - 2) * lanes_all), chosen[2 * lanes_all :], preferred_element_type=f32
            )
            blocks_ref[n, m : m + 8] = y.reshape(8, half, 2 * lanes_all)

    fetch(0)
    for n in range(2):
        if n == 0:
            fetch(1)
        (own,) = interpolate(extra_ref, lambda m: blocks_ref[n, m, :, lanes_all:], (0,))
        for j in range(4):
            ends = interpolate(weights_ref, lambda m: blocks_ref[n, m, :, lanes], (j, 12 + j))
            middle = interpolate(weights_ref, lambda m: blocks_ref[n, m, :, lanes], (4 + j, 8 + j))
            own_here = pltpu.roll(own, ((0 if ahead else cap - 1) - j) % lanes_all, 1)
            if ahead:
                west = ends[0] + jnp.where(edge, own_here, pltpu.roll(ends[1], 1, 1))
                values, far = (west, *middle), ends[1]
            else:
                east = ends[1] + jnp.where(edge, own_here, pltpu.roll(ends[0], lanes_all - 1, 1))
                values, far = (*middle, east), ends[0]
            for i, value in enumerate(values):
                row = (3 * j + i) * tracers + n * half
                out_ref[row : row + half, :] = value.astype(bf16)
            row = j * tracers + n * half
            edge_ref[row : row + half, :] = far.astype(bf16)
    row = lax.broadcasted_iota(jnp.int32, (8, lanes_all), 0)
    far_place = cap - 1 if ahead else 0
    pick = jnp.where(lane == row * cap + far_place, 1.0, 0.0).astype(bf16)
    far = lax.dot_general(pick, edge_ref[...], (((1,), (1,)), ((), ())), preferred_element_type=f32)
    far = [far[:, n : n + lanes_all] for n in range(0, 4 * tracers, lanes_all)]
    out_ref[12 * tracers :, :] = jnp.concatenate(far, axis=0).astype(bf16)


def local_kernel(
    velocity_ref, mass_ref, source_ref, first_ref, rest_ref, after_ref,
    out_ref, ends_ref, sides_ref,
    blocks_ref, weights_ref, wind_ref, moved_ref, inner_ref, sems,
):
    del after_ref
    _, _, levels, elements = velocity_ref.shape
    cap = elements // levels
    columns = out_ref.shape[2]
    tracers = columns // 16
    start = lax.axis_index("elem") * elements
    lane = lax.broadcasted_iota(jnp.int32, (1, elements), 1)
    mass = by_i(mass_ref, 0)
    mass_before = pltpu.roll(mass[3], 1, 1)
    mass_after = pltpu.roll(mass[0], elements - 1, 1)
    share_west = mass[0] / (mass_before + mass[0])
    share_east = mass[3] / (mass[3] + mass_after)
    coefficient = jnp.concatenate([share_west, jnp.ones((8, elements), f32), share_east], axis=0)
    row = lax.broadcasted_iota(jnp.int32, (elements, elements), 0)
    chosen = jnp.where(row == source_ref[...] - start, 1.0, 0.0).astype(bf16)

    def fetch(k):
        x = rest_ref[:, :, (k - 1) * elements : k * elements] if k else first_ref[...]
        y = jnp.dot(x.reshape(columns, elements), chosen, preferred_element_type=f32)
        blocks_ref[k % 2] = y.reshape(16, tracers, elements)

    fetch(0)
    for k in range(levels):
        winds = []
        for c in range(2):
            wind_ref[c] = velocity_ref[c, :, k, :]
            wind = [wind_ref[c, pl.ds(i, 4, stride=4), :] for i in range(4)]
            west = shared(mass_before, pltpu.roll(wind[3], 1, 1), mass[0], wind[0])
            east = shared(mass[3], wind[3], mass_after, pltpu.roll(wind[0], elements - 1, 1))
            winds.append(jnp.concatenate([west, wind[1], wind[2], east], axis=0))
        along, across = table(winds)
        for b in range(4):
            for a in range(4):
                weights_ref[k % 2, 4 * b + a] = weight(along[a], across[b], coefficient)
        if k + 1 < levels:
            fetch(k + 1)
        lanes = slice(k * elements, (k + 1) * elements)
        table_ref = weights_ref.at[k % 2]
        for j in range(4):
            ends = interpolate(table_ref, lambda m: blocks_ref[k % 2, m], (j, 12 + j))
            middle = interpolate(table_ref, lambda m: blocks_ref[k % 2, m], (4 + j, 8 + j))
            west = jnp.where(lane == 0, 0.0, ends[0] + pltpu.roll(ends[1], 1, 1))
            east = pltpu.roll(west, elements - 1, 1)
            for i, value in enumerate((west, *middle, east)):
                node = 4 * j + i
                moved_ref[node * tracers : (node + 1) * tracers, lanes] = value.astype(bf16)
    inner = elements - 2 * cap
    row = lax.broadcasted_iota(jnp.int32, (inner * levels, elements * levels), 0)
    column = lax.broadcasted_iota(jnp.int32, (inner * levels, elements * levels), 1)
    same = (row // levels + cap == column % elements) & (row % levels == column // elements)
    order = jnp.where(same, 1.0, 0.0).astype(bf16)
    step = columns // 4
    stores = []
    for n in range(4):
        part = pl.ds(n * step, step)
        y = lax.dot_general(
            order, moved_ref[part, :], (((1,), (1,)), ((), ())), preferred_element_type=f32
        )
        inner_ref[:, :, part] = y.reshape(inner, levels, step).astype(bf16)
        stores.append(pltpu.make_async_copy(
            inner_ref.at[pl.ds(1, inner - 2), :, part], out_ref.at[pl.ds(cap + 1, inner - 2), :, part], sems.at[n]
        ))
        stores[n].start()
    sides_ref[0] = inner_ref[0]
    sides_ref[1] = inner_ref[inner - 1]
    for n, low in enumerate((0, elements - cap)):
        ends_ref[n] = jnp.concatenate(
            [moved_ref[:, k * elements + low : k * elements + low + cap] for k in range(levels)], axis=1
        )
    for store in stores:
        store.wait()


def combine_kernel(pair, part_ref, ends_ref, sides_ref, received_ref, sent_ref, out_ref, rows_ref, sems):
    del part_ref
    refs = (ends_ref, sides_ref, received_ref, sent_ref, out_ref, rows_ref, sems)
    even = is_even()
    head = jnp.logical_not(even) if pair else even
    pl.when(head)(lambda: combine(True, *refs))
    pl.when(jnp.logical_not(head))(lambda: combine(False, *refs))


def combine(head, ends_ref, sides_ref, received_ref, sent_ref, out_ref, rows_ref, sems):
    elements, levels, columns = out_ref.shape
    lanes_all = received_ref.shape[1]
    cap = elements // levels
    tracers = columns // 16
    end = 0 if head else 1
    place = lax.broadcasted_iota(jnp.int32, (1, lanes_all), 1) % cap
    order = interleave(levels, cap)
    span = 4 * tracers
    spot = pl.ds(0, cap + 1) if head else pl.ds(elements - cap - 1, cap + 1)

    def rows(ref, block):
        return ref[block * tracers : (block + 1) * tracers, :].astype(f32)

    stores = []
    for j in range(4):
        got = [rows(received_ref, 3 * j + i) for i in range(3)]
        if head:
            own = pltpu.roll(rows(sent_ref, 3 * j + 2), lanes_all - (cap - 1), 1)
            west = got[0] + jnp.where(place == 0, own, 0.0)
            east = jnp.where(place == cap - 1, 0.0, pltpu.roll(got[0], lanes_all - 1, 1))
            got = [west, got[1], got[2], east]
        else:
            own = pltpu.roll(rows(sent_ref, 3 * j), cap - 1, 1)
            east = got[2] + jnp.where(place == cap - 1, own, 0.0)
            west = jnp.where(place == 0, 0.0, pltpu.roll(got[2], 1, 1))
            got = [west, got[0], got[1], east]
        pieces = []
        for i, value in enumerate(got):
            node = 4 * j + i
            here = ends_ref[end, node * tracers : (node + 1) * tracers, :].astype(f32)
            pieces.append((here + value).astype(bf16))
        y = lax.dot_general(
            order, jnp.concatenate(pieces, axis=0), (((1,), (1,)), ((), ())), preferred_element_type=f32
        ).reshape(cap, levels, span)
        first = 12 * tracers + 8 * (j * tracers // lanes_all)
        low = j * tracers % lanes_all
        far = received_ref[first : first + 8, low : low + tracers].astype(f32)[:levels]
        zeros = jnp.zeros((levels, span - tracers), f32)
        west = jnp.concatenate([far, zeros], axis=1)
        east = jnp.concatenate([zeros, far], axis=1)
        part = slice(j * span, (j + 1) * span)
        if head:
            rows_ref[0 : cap - 1, :, part] = y[: cap - 1].astype(bf16)
            rows_ref[cap - 1, :, part] = (y[cap - 1] + east).astype(bf16)
            rows_ref[cap, :, part] = (sides_ref[0, :, part].astype(f32) + west).astype(bf16)
        else:
            rows_ref[2:, :, part] = y[1:].astype(bf16)
            rows_ref[1, :, part] = (y[0] + west).astype(bf16)
            rows_ref[0, :, part] = (sides_ref[1, :, part].astype(f32) + east).astype(bf16)
        part = pl.ds(j * span, span)
        stores.append(pltpu.make_async_copy(rows_ref.at[:, :, part], out_ref.at[spot, :, part], sems.at[j]))
        stores[j].start()
    for store in stores:
        store.wait()


def on_device(tracers, velocity, node_mass, source):
    elements, levels, columns = tracers.shape
    cap = elements // 4
    assert cap * levels == elements
    count = columns // 16
    lanes = levels * elements
    runs = lax.axis_size("elem")
    pairing = [(i, i ^ 1) for i in range(runs)]
    crossing = [(i, (i - 1 if i % 2 == 0 else i + 1) % runs) for i in range(runs)]
    shape = jax.ShapeDtypeStruct
    vmem = pl.BlockSpec(memory_space=pltpu.VMEM)
    anywhere = pl.BlockSpec(memory_space=pl.ANY)
    source = source.reshape(1, elements)

    packet = shape((PACKET, elements), f32)
    inputs = (tracers, velocity, node_mass, source)
    lowest, cross_sent, pair_sent, tracers, velocity, node_mass, source = pl.pallas_call(
        prepare_kernel,
        out_shape=(shape((columns, elements), bf16), packet, packet)
        + tuple(shape(x.shape, x.dtype) for x in inputs),
        in_specs=[anywhere] * 4,
        scratch_shapes=[pltpu.VMEM((elements, 2, columns), bf16), pltpu.SemaphoreType.DMA((5,))],
        compiler_params=params(),
        name="prepare",
    )(*[pltpu.with_memory_space_constraint(x, pltpu.HBM) for x in inputs])
    blocks = lax.axis_size("lev")
    above = lax.ppermute(lowest, "lev", [(i, (i + 1) % blocks) for i in range(blocks)])
    spread_out = (shape((columns, elements), bf16), shape((16, count, lanes - elements), bf16))
    spread_scratch = [pltpu.VMEM((columns, lanes), bf16)]
    *early, pair_sent = pl.pallas_call(
        spread_early_kernel,
        out_shape=spread_out + (packet,),
        scratch_shapes=spread_scratch,
        compiler_params=params(),
        name="spread_early",
    )(tracers, velocity, pair_sent)
    pair_packet = lax.ppermute(pair_sent, "elem", pairing)
    cross_packet = lax.ppermute(cross_sent, "elem", crossing)
    def weighed(pair, packet, own, after):
        return pl.pallas_call(
            functools.partial(weigh_kernel, pair, levels),
            out_shape=(
                shape((16, 16, elements), f32),
                shape((16, 8, elements), f32),
                shape((lanes, 2 * elements), bf16),
            ),
            in_specs=[anywhere, vmem, vmem],
            compiler_params=params(),
            name="weigh_pair" if pair else "weigh_cross",
        )(after, packet, own)

    pair_weights = weighed(True, pair_packet, pair_sent, lowest)
    top, rest = pl.pallas_call(
        spread_kernel,
        out_shape=spread_out,
        scratch_shapes=spread_scratch,
        compiler_params=params(),
        name="spread",
    )(tracers, velocity, *early)
    far_rows = 8 * (4 * count // elements)

    message = shape((12 * count + far_rows, elements), bf16)
    message_scratch = [pltpu.VMEM((2, 16, count // 2, 2 * elements), f32), pltpu.VMEM((4 * count, elements), bf16)]
    pair_out, first = pl.pallas_call(
        pair_kernel,
        out_shape=(message, shape((16, count, elements), bf16)),
        scratch_shapes=message_scratch,
        compiler_params=params(),
        name="remote_pair",
    )(top, above, velocity, rest, *pair_weights)
    pair_in = lax.ppermute(pair_out, "elem", pairing)
    cross_out = pl.pallas_call(
        functools.partial(weigh_remote_kernel, False, levels),
        out_shape=message,
        in_specs=[anywhere] + [vmem] * 4,
        scratch_shapes=message_scratch + [
            pltpu.VMEM((16, 16, elements), f32),
            pltpu.VMEM((16, 8, elements), f32),
            pltpu.VMEM((lanes, 2 * elements), bf16),
        ],
        compiler_params=params(),
        name="remote_cross",
    )(pair_out, cross_packet, cross_sent, first, rest)
    cross_in = lax.ppermute(cross_out, "elem", crossing)
    result = shape((elements, levels, columns), bf16)
    part, ends, sides = pl.pallas_call(
        local_kernel,
        out_shape=(result, shape((2, columns, elements), bf16), shape((2, levels, columns), bf16)),
        in_specs=[vmem] * 5 + [anywhere],
        out_specs=(anywhere, vmem, vmem),
        scratch_shapes=[
            pltpu.VMEM((2, 16, count, elements), f32),
            pltpu.VMEM((2, 16, 16, elements), f32),
            pltpu.VMEM((2, 16, elements), f32),
            pltpu.VMEM((columns, lanes), bf16),
            pltpu.VMEM((elements - 2 * cap, levels, columns), bf16),
            pltpu.SemaphoreType.DMA((4,)),
        ],
        compiler_params=params(),
        cost_estimate=cost(10**9),
        name="local",
    )(velocity, node_mass, source, first, rest, cross_out)
    for pair, received, sent in ((True, pair_in, pair_out), (False, cross_in, cross_out)):
        part = pl.pallas_call(
            functools.partial(combine_kernel, pair),
            out_shape=result,
            in_specs=[anywhere, vmem, vmem, vmem, vmem],
            out_specs=anywhere,
            scratch_shapes=[pltpu.VMEM((cap + 1, levels, columns), bf16), pltpu.SemaphoreType.DMA((4,))],
            input_output_aliases={0: 0},
            compiler_params=params(),
            name="combine_pair" if pair else "combine_cross",
        )(part, ends, sides, received, sent)
    return part


def solution(mesh):
    placed = (P("elem", "lev", None), P(None, None, "lev", "elem"), P(None, "elem"), P("elem"))
    return jax.shard_map(
        on_device, mesh=mesh, in_specs=placed, out_specs=P("elem", "lev", None), check_vma=False
    )
```
